32 devices in a mesh: dp: 4 (over x, core), sp: 8 (over z, y).
Axes of the slice: x: 2, y: 2, z: 4, core: 2. Of those that a mesh axis runs over, the one named last changes fastest.
Arguments:
- tokens: bfloat16 [4, 2048, 1536], P('dp', 'sp'), may hold values from -6 to 6
- cotangent: bfloat16 [4, 2048, 1536], P('dp', 'sp'), may hold values from -6 to 6
- captions: bfloat16 [4, 2, 128, 4096], P('dp', None, 'sp'), may hold values from -6 to 6
- conditioning: float32 [4, 2, 1024], P('dp'), may hold values from -6 to 6
- clip_lens: int32 [4, 2], P('dp'), may hold values from 1024 to 1024, as said below
- w_ada: bfloat16 [1024, 9216], P(None, 'sp'), may hold values from -0.1875 to 0.1875
- b_ada: float32 [9216], P('sp'), may hold values from -3 to 3
- w_query: bfloat16 [1536, 1536], P('sp'), may hold values from -0.15625 to 0.15625
- w_key: bfloat16 [1536, 1536], P('sp'), may hold values from -0.15625 to 0.15625
- w_value: bfloat16 [1536, 1536], P('sp'), may hold values from -0.15625 to 0.15625
- w_out: bfloat16 [1536, 1536], P('sp'), may hold values from -1.25 to 1.25
- gate_cross: float32 [24], replicated, may hold values from -1.5 to 1.5
- w_text_key: bfloat16 [4096, 1536], P('sp'), may hold values from -0.09375 to 0.09375
- w_text_value: bfloat16 [4096, 1536], P('sp'), may hold values from -0.09375 to 0.09375
- w_gate: bfloat16 [1536, 4096], P('sp'), may hold values from -0.15625 to 0.15625
- w_up: bfloat16 [1536, 4096], P('sp'), may hold values from -0.15625 to 0.15625
- w_down: bfloat16 [4096, 1536], P('sp'), may hold values from -0.09375 to 0.09375
Outputs:
- result: bfloat16 [4, 2048, 1536], P('dp', 'sp')
- d_tokens: float32 [4, 2048, 1536], P('dp', 'sp')
- d_captions: float32 [4, 2, 128, 4096], P('dp', None, 'sp')
- d_conditioning: float32 [4, 2, 1024], P('dp')
- d_w_ada: float32 [1024, 9216], P(None, 'sp')
- d_b_ada: float32 [9216], P('sp')
- d_w_query: float32 [1536, 1536], P('sp')
- d_w_key: float32 [1536, 1536], P('sp')
- d_w_value: float32 [1536, 1536], P('sp')
- d_w_out: float32 [1536, 1536], P('sp')
- d_gate_cross: float32 [24], replicated
- d_w_text_key: float32 [4096, 1536], P('sp')
- d_w_text_value: float32 [4096, 1536], P('sp')
- d_w_gate: float32 [1536, 4096], P('sp')
- d_w_up: float32 [1536, 4096], P('sp')
- d_w_down: float32 [4096, 1536], P('sp')
The draws below stay inside these ranges and needn't reach their ends.
Inputs may be any that keep to these rules, and one draw needn't show every extreme that they name: `clip_lens`: the 2 lengths of a pack sum to 2048; each is 1024 or more, and one of them is half of 2048 or more.
All inputs are finite; a program needn't handle non-finite values.
Results may differ from the reference program's by a relative error of at most 0.04.
Values may be sent and summed in bfloat16 or wider, within the bound.
No kernel may reach another device: no remote copies, remote signals or barrier semaphores. Data moves between devices by JAX's collectives and lax.ppermute only.
A program may use at most 384 MiB of HBM per device.

```python
import jax
import jax.numpy as jnp
from jax import lax

D = 1536
HEADS = 24
HD = 64
FF = 4096
TEXT = 4096
COND = 1024
CAP = 128
CLIPS = 2
MIN_CLIP = 1024
TOK_DEV = 256
PACK = 2048
PACKS = 4
N_SP = 8


def draw_clip_lens(key, part):
    key = jax.random.fold_in(key, 7)
    first_key, order_key = jax.random.split(key)
    extra = jax.random.randint(first_key, (PACKS,), 0, PACK // 2 - MIN_CLIP + 1)
    extra = extra.at[0].set(PACK // 2 - MIN_CLIP)
    longer = PACK // 2 + extra
    shorter = PACK - longer
    flipped = jax.random.randint(order_key, (PACKS,), 0, 2)
    leading = jnp.where(flipped == 1, longer, shorter)
    return jnp.stack([leading, PACK - leading], axis=1).astype(jnp.int32)


def block_levels(stream_key, shape, cuts, low, high):
    def one(dim, blocks):
        heights = jax.random.uniform(jax.random.fold_in(jax.random.fold_in(stream_key, 6), dim), (blocks,), jnp.float32, low / len(cuts), high / len(cuts))
        return jnp.repeat(jnp.exp(heights), shape[dim] // blocks).reshape((-1,) + (1,) * (len(shape) - dim - 1))

    loudness = one(*cuts[0])
    for cut in cuts[1:]:
        loudness = loudness * one(*cut)
    return loudness


def noise(stream_key, dims, deviation, bound, cuts=(), kind=jnp.bfloat16):
    entries = deviation * jax.random.normal(stream_key, dims, jnp.float32)
    if cuts:
        entries = entries * block_levels(stream_key, dims, cuts, -0.22, 0.18)
    return jnp.clip(entries, -bound, bound).astype(kind)


def setup_inputs(seed: int = 0) -> dict:
    key_list = jax.random.split(jax.random.key(seed), 18)
    return {
        "tokens": noise(key_list[0], (PACKS, PACK, D), 1.0, 6.0, ((0, 4), (1, 8))),
        "cotangent": noise(key_list[1], (PACKS, PACK, D), 1.0, 6.0, ((0, 4), (1, 8))),
        "captions": noise(key_list[2], (PACKS, CLIPS, CAP, TEXT), 1.0, 6.0, ((0, 4), (2, 8))),
        "conditioning": noise(key_list[3], (PACKS, CLIPS, COND), 1.0, 6.0, ((0, 4),), jnp.float32),
        "clip_lens": draw_clip_lens(jax.random.fold_in(key_list[17], 71), 0),
        "w_ada": noise(key_list[5], (COND, 6 * D), COND ** -0.5, 0.1875, ((1, 8),)),
        "b_ada": noise(key_list[6], (6 * D,), 0.3, 3.0, ((0, 8),), jnp.float32),
        "w_query": noise(key_list[7], (D, D), D ** -0.5, 0.15625, ((0, 8),)),
        "w_key": noise(key_list[8], (D, D), D ** -0.5, 0.15625, ((0, 8),)),
        "w_value": noise(key_list[9], (D, D), D ** -0.5, 0.15625, ((0, 8),)),
        "w_out": noise(key_list[10], (D, D), (max(1, D // 64)) ** -0.5, 1.25, ((0, 8),)),
        "gate_cross": jnp.clip(jax.random.uniform(key_list[11], (HEADS,), jnp.float32, -1.5, 1.5), -1.5, 1.5),
        "w_text_key": noise(key_list[12], (TEXT, D), TEXT ** -0.5, 0.09375, ((0, 8),)),
        "w_text_value": noise(key_list[13], (TEXT, D), TEXT ** -0.5, 0.09375, ((0, 8),)),
        "w_gate": noise(key_list[14], (D, FF), D ** -0.5, 0.15625, ((0, 8),)),
        "w_up": noise(key_list[15], (D, FF), D ** -0.5, 0.15625, ((0, 8),)),
        "w_down": noise(key_list[16], (FF, D), FF ** -0.5, 0.09375, ((0, 8),)),
    }


EPSILON = 1e-06
MASKED = -1e+30
HIGHEST = lax.Precision.HIGHEST

@jax.custom_vjp
def low(v):
    return lax.optimization_barrier(v.astype(jnp.bfloat16)).astype(jnp.float32)

@jax.custom_vjp
def low_back(v):
    return v

def low_keep(v):
    return (low(v), None)

def low_pass(kept, grad):
    return (grad,)

def back_keep(v):
    return (v, None)

def back_low(kept, grad):
    return (low(grad),)
low.defvjp(low_keep, low_pass)
low_back.defvjp(back_keep, back_low)

def matmul(left, right):
    return jnp.dot(left, right, precision=HIGHEST)

def rms_norm(values):
    return values * lax.rsqrt(lax.optimization_barrier(jnp.mean(values * values, axis=-1, keepdims=True)) + EPSILON)

def layout(lengths):
    half_block = TOK_DEV // 2
    stored = jnp.arange(PACK, dtype=jnp.int32)
    unit_index = stored // half_block
    owner = unit_index // 2
    logical_block = jnp.where(unit_index % 2 == 0, owner, 2 * N_SP - 1 - owner)
    logical = (logical_block * half_block + stored % half_block).astype(jnp.int32)
    clip_ends = jnp.cumsum(lengths).astype(jnp.int32)
    clip_starts = (clip_ends - lengths).astype(jnp.int32)
    segment = jnp.zeros((PACK,), jnp.int32)
    for clip_index in range(CLIPS - 1):
        segment = segment + (logical >= clip_ends[clip_index]).astype(jnp.int32)
    offset = jnp.zeros((PACK,), jnp.int32)
    for clip_index in range(CLIPS):
        offset = offset + jnp.where(segment == clip_index, clip_starts[clip_index], 0).astype(jnp.int32)
    return (segment, (logical - offset).astype(jnp.int32))

def rope_tables(positions):
    half_width = HD // 2
    freq = 10000.0 ** (-(jnp.arange(half_width, dtype=jnp.float32) * 2.0 / HD))
    angle = positions.astype(jnp.float32)[:, None] * freq[None, :]
    return (jnp.cos(angle)[:, None, :], jnp.sin(angle)[:, None, :])

def rotate(values, cos_table, sin_table):
    half_width = values.shape[-1] // 2
    first_half = values[..., :half_width]
    second_half = values[..., half_width:]
    return jnp.concatenate([first_half * cos_table - second_half * sin_table, first_half * sin_table + second_half * cos_table], axis=-1)

def pack_forward(inputs, caption_feats, cond_rows, segment, positions, weights):
    w_ada, b_ada, w_query, w_key, w_value, w_out, gate_cross, w_text_key, w_text_value, w_gate, w_up, w_down = weights
    score_scale = HD ** (-0.5)
    cond_act = low(jax.nn.silu(cond_rows))
    modulation = low_back(matmul(cond_act, w_ada) + b_ada[None, :])
    per_token = modulation[segment]
    shift_one, scale_one, gate_one, shift_two, scale_two, gate_two = jnp.split(per_token, 6, axis=-1)
    block_in = low(rms_norm(inputs) * (1.0 + scale_one) + shift_one)
    cos_table, sin_table = rope_tables(positions)

    def as_heads(values):
        return values.reshape(PACK, HEADS, HD)
    query_rot = low(rotate(rms_norm(as_heads(low_back(matmul(block_in, w_query)))), cos_table, sin_table))
    key_rot = low(rotate(rms_norm(as_heads(low_back(matmul(block_in, w_key)))), cos_table, sin_table))
    value_low = low(as_heads(low_back(matmul(block_in, w_value))))
    flat_caption = caption_feats.reshape(CLIPS * CAP, TEXT)
    cap_keys = low(low_back(matmul(flat_caption, w_text_key))).reshape(CLIPS * CAP, HEADS, HD)
    cap_values = low(low_back(matmul(flat_caption, w_text_value))).reshape(CLIPS * CAP, HEADS, HD)
    caption_clip = jnp.arange(CLIPS * CAP, dtype=jnp.int32) // CAP
    block_rows = min(512, PACK)
    tanh_gate = jnp.tanh(gate_cross)

    def attend(block):
        block_query, block_segment = block
        scores = low_back(jnp.einsum('qhd,khd->hqk', block_query, key_rot, precision=HIGHEST) * score_scale)
        allowed = (block_segment[:, None] == segment[None, :])[None]
        probs = jax.nn.softmax(jnp.where(allowed, scores, MASKED), axis=-1)
        self_out = low_back(jnp.einsum('hqk,khd->qhd', low(probs), value_low, precision=HIGHEST))
        cross_scores = low_back(jnp.einsum('qhd,khd->hqk', block_query, cap_keys, precision=HIGHEST) * score_scale)
        own_clip = (block_segment[:, None] == caption_clip[None, :])[None]
        cross_probs = jax.nn.softmax(jnp.where(own_clip, cross_scores, MASKED), axis=-1)
        cross_out = low_back(jnp.einsum('hqk,khd->qhd', low(cross_probs), cap_values, precision=HIGHEST))
        mixed = self_out + tanh_gate[None, :, None] * cross_out
        return low(mixed).reshape(block_rows, D)
    blocks = (query_rot.reshape(PACK // block_rows, block_rows, HEADS, HD), segment.reshape(PACK // block_rows, block_rows))
    attended = lax.map(jax.checkpoint(attend), blocks).reshape(PACK, D)
    attn_out = low_back(matmul(attended, w_out))
    middle = inputs + gate_one * attn_out
    ffn_in = low(rms_norm(middle) * (1.0 + scale_two) + shift_two)
    gate_proj = low_back(matmul(ffn_in, w_gate))
    up_proj = low_back(matmul(ffn_in, w_up))
    hidden = low(jax.nn.silu(gate_proj) * up_proj)
    branch = low_back(matmul(hidden, w_down))
    return middle + gate_two * branch

def reference(tokens, cotangent, captions, conditioning, clip_lens, w_ada, b_ada, w_query, w_key, w_value, w_out, gate_cross, w_text_key, w_text_value, w_gate, w_up, w_down):
    segments, positions = jax.vmap(layout)(clip_lens)

    def forward(tokens_in, captions_in, cond_in, *weights):

        def one_pack(packed):
            return pack_forward(packed[0], packed[1], packed[2], packed[3], packed[4], weights)
        return lax.map(one_pack, (tokens_in, captions_in, cond_in, segments, positions))
    primals = (tokens.astype(jnp.float32), captions.astype(jnp.float32), conditioning, w_ada.astype(jnp.float32), b_ada, w_query.astype(jnp.float32), w_key.astype(jnp.float32), w_value.astype(jnp.float32), w_out.astype(jnp.float32), gate_cross, w_text_key.astype(jnp.float32), w_text_value.astype(jnp.float32), w_gate.astype(jnp.float32), w_up.astype(jnp.float32), w_down.astype(jnp.float32))
    outcome, pullback = jax.vjp(forward, *primals)
    grads = pullback(cotangent.astype(jnp.float32))
    return (outcome.astype(jnp.bfloat16), grads[0], grads[1], grads[2], grads[3], grads[4], grads[5], grads[6], grads[7], grads[8], grads[9], grads[10], grads[11], grads[12], grads[13], grads[14])
```

```python
import functools

import jax
import jax.numpy as jnp
from jax import lax
from jax.experimental import pallas as pl
from jax.experimental.pallas import tpu as pltpu
from jax.sharding import PartitionSpec as P

D = 1536
HEADS = 24
HD = 64
TEXT = 4096
CAP = 128
CLIPS = 2


EPSILON = 1e-06
MASKED = -1e30
HIGHEST = lax.Precision.HIGHEST


def rope_tables(positions):
    half_width = HD // 2
    freq = 10000.0 ** (-(jnp.arange(half_width, dtype=jnp.float32) * 2.0 / HD))
    angle = positions.astype(jnp.float32)[:, None] * freq[None, :]
    return (jnp.cos(angle)[:, None, :], jnp.sin(angle)[:, None, :])


def rotate(values, cos_table, sin_table):
    half_width = values.shape[-1] // 2
    first_half = values[..., :half_width]
    second_half = values[..., half_width:]
    return jnp.concatenate(
        [
            first_half * cos_table - second_half * sin_table,
            first_half * sin_table + second_half * cos_table,
        ],
        axis=-1,
    )


def rotate_back(grads, cos_table, sin_table):
    half_width = grads.shape[-1] // 2
    first_half = grads[..., :half_width]
    second_half = grads[..., half_width:]
    return jnp.concatenate(
        [
            first_half * cos_table + second_half * sin_table,
            second_half * cos_table - first_half * sin_table,
        ],
        axis=-1,
    )


def inverse_rms(values):
    return lax.rsqrt(jnp.mean(values * values, axis=-1, keepdims=True) + EPSILON)


def norm_back(grads, normed, inverse):
    return inverse * (grads - normed * jnp.mean(grads * normed, axis=-1, keepdims=True))


def per_clip(select, values):
    return jnp.einsum("tc,td->cd", select, values, precision=HIGHEST)


def local(
    tokens,
    cotangent,
    captions,
    conditioning,
    clip_lens,
    w_ada,
    b_ada,
    w_query,
    w_key,
    w_value,
    w_out,
    gate_cross,
    w_text_key,
    w_text_value,
    w_gate,
    w_up,
    w_down,
):
    shard = lax.axis_index("sp")
    cycle_size = lax.axis_size("sp")
    tok_rows = tokens.shape[1]
    half_rows = tok_rows // 2
    score_scale = HD ** (-0.5)
    row_index = jnp.arange(tok_rows, dtype=jnp.int32)
    logical_block = jnp.where(row_index < half_rows, shard, 2 * cycle_size - 1 - shard)
    logical = logical_block * half_rows + row_index % half_rows
    lengths = clip_lens[0]
    clip_ends = jnp.cumsum(lengths)
    clip_starts = clip_ends - lengths
    clip_index = 0
    segment = (logical >= clip_ends[clip_index]).astype(jnp.int32)
    offset = jnp.zeros((tok_rows,), jnp.int32)
    for clip_index in range(CLIPS):
        offset = offset + jnp.where(segment == clip_index, clip_starts[clip_index], 0)
    positions = logical - offset
    inputs = tokens[0].astype(jnp.float32)
    cond_row = conditioning[0]
    cond_act = jax.nn.silu(cond_row).astype(jnp.bfloat16)
    mod_part = jnp.dot(cond_act, w_ada, preferred_element_type=jnp.float32) + b_ada[None, :]
    modulation = lax.all_gather(mod_part, "sp", axis=1, tiled=True)
    select = (segment[:, None] == jnp.arange(CLIPS, dtype=jnp.int32)[None, :]).astype(jnp.float32)
    per_token = jnp.dot(select, modulation, precision=HIGHEST)
    shift_one, scale_one, gate_one, shift_two, scale_two, gate_two = jnp.split(per_token, 6, axis=1)
    weights_full = (
        lax.all_gather(w_query, "sp", axis=0, tiled=True),
        lax.all_gather(w_key, "sp", axis=0, tiled=True),
        lax.all_gather(w_value, "sp", axis=0, tiled=True),
        lax.all_gather(w_out, "sp", axis=0, tiled=True),
        lax.all_gather(w_gate, "sp", axis=0, tiled=True),
        lax.all_gather(w_up, "sp", axis=0, tiled=True),
        lax.all_gather(w_down, "sp", axis=0, tiled=True),
        lax.all_gather(w_text_key, "sp", axis=0, tiled=True),
        lax.all_gather(w_text_value, "sp", axis=0, tiled=True),
    )
    (
        query_full,
        key_full,
        value_full,
        out_full,
        gate_full,
        up_full,
        down_full,
        text_key_full,
        text_value_full,
    ) = weights_full
    inverse_one = inverse_rms(inputs)
    normed_one = inputs * inverse_one
    block_in = (normed_one * (1.0 + scale_one) + shift_one).astype(jnp.bfloat16)
    cos_table, sin_table = rope_tables(positions)

    def project(weight):
        return jnp.dot(block_in, weight, preferred_element_type=jnp.float32).reshape(
            tok_rows, HEADS, HD
        )

    query_raw = project(query_full)
    inverse_query = inverse_rms(query_raw)
    query_normed = query_raw * inverse_query
    query_rot = rotate(query_normed, cos_table, sin_table).astype(jnp.bfloat16)
    key_raw = project(key_full)
    inverse_key = inverse_rms(key_raw)
    key_normed = key_raw * inverse_key
    key_rot = rotate(key_normed, cos_table, sin_table).astype(jnp.bfloat16)
    value_rows = project(value_full).astype(jnp.bfloat16)
    caption_feats = captions[0]
    flat_caption = caption_feats.reshape(-1, TEXT)
    cap_key_part = (
        jnp.dot(flat_caption, text_key_full, preferred_element_type=jnp.float32)
        .astype(jnp.bfloat16)
        .reshape(CLIPS, -1, D)
    )
    cap_value_part = (
        jnp.dot(flat_caption, text_value_full, preferred_element_type=jnp.float32)
        .astype(jnp.bfloat16)
        .reshape(CLIPS, -1, D)
    )
    cap_key_all, cap_value_all = (
        lax.all_gather(cap_key_part, "sp", axis=1, tiled=True),
        lax.all_gather(cap_value_part, "sp", axis=1, tiled=True),
    )
    cap_key_heads = cap_key_all.reshape(CLIPS * CAP, HEADS, HD)
    cap_value_heads = cap_value_all.reshape(CLIPS * CAP, HEADS, HD)
    caption_clip = jnp.arange(CLIPS * CAP, dtype=jnp.int32) // CAP
    run_max = jnp.full((HEADS, tok_rows), MASKED, jnp.float32)
    key_piece = lax.all_gather(key_rot, "sp", axis=0, tiled=True)
    value_piece = lax.all_gather(value_rows, "sp", axis=0, tiled=True)
    segment_piece = lax.all_gather(segment, "sp", axis=0, tiled=True)
    scores = (
        jnp.einsum("qhd,khd->hqk", query_rot, key_piece, preferred_element_type=jnp.float32)
        * score_scale
    )
    allowed = (segment[:, None] == segment_piece[None, :])[None]
    scores = jnp.where(allowed, scores, MASKED)
    new_max = jnp.maximum(run_max, jnp.max(scores, axis=-1))
    weights_exp = jnp.where(allowed, jnp.exp(scores - new_max[:, :, None]), 0.0)
    new_total = jnp.sum(weights_exp, axis=-1)
    new_acc = jnp.einsum(
        "hqk,khd->qhd",
        weights_exp.astype(jnp.bfloat16),
        value_piece,
        preferred_element_type=jnp.float32,
    )
    self_out = new_acc / jnp.transpose(new_total)[:, :, None]
    log_total = jnp.transpose(new_max + jnp.log(new_total))
    cross_scores = (
        jnp.einsum("qhd,khd->hqk", query_rot, cap_key_heads, preferred_element_type=jnp.float32)
        * score_scale
    )
    own_clip = (segment[:, None] == caption_clip[None, :])[None]
    cross_probs = jax.nn.softmax(jnp.where(own_clip, cross_scores, MASKED), axis=-1)
    cross_low = cross_probs.astype(jnp.bfloat16)
    cross_out = jnp.einsum(
        "hqk,khd->qhd", cross_low, cap_value_heads, preferred_element_type=jnp.float32
    )
    tanh_gate = jnp.tanh(gate_cross)
    mixed = (
        (self_out + tanh_gate[None, :, None] * cross_out).astype(jnp.bfloat16).reshape(tok_rows, D)
    )
    attn_out = jnp.dot(mixed, out_full, preferred_element_type=jnp.float32)
    middle = inputs + gate_one * attn_out
    inverse_two = inverse_rms(middle)
    normed_two = middle * inverse_two
    ffn_in = (normed_two * (1.0 + scale_two) + shift_two).astype(jnp.bfloat16)
    gate_proj = jnp.dot(ffn_in, gate_full, preferred_element_type=jnp.float32)
    up_proj = jnp.dot(ffn_in, up_full, preferred_element_type=jnp.float32)
    sigmoid_gate = jax.nn.sigmoid(gate_proj)
    silu_gate = jax.nn.silu(gate_proj)
    hidden = (silu_gate * up_proj).astype(jnp.bfloat16)
    branch = jnp.dot(hidden, down_full, preferred_element_type=jnp.float32)
    result = (middle + gate_two * branch).astype(jnp.bfloat16)
    out_grad = cotangent[0].astype(jnp.float32)
    branch_grad = (gate_two * out_grad).astype(jnp.bfloat16)
    hidden_grad = jnp.einsum(
        "td,fd->tf", branch_grad, down_full, preferred_element_type=jnp.float32
    )
    grad_down = jnp.einsum("tf,td->fd", hidden, branch_grad, preferred_element_type=jnp.float32)
    gate_grad = (
        hidden_grad * up_proj * sigmoid_gate * (1.0 + gate_proj * (1.0 - sigmoid_gate))
    ).astype(jnp.bfloat16)
    up_grad = (hidden_grad * silu_gate).astype(jnp.bfloat16)
    ffn_in_grad = jnp.einsum(
        "tf,df->td", gate_grad, gate_full, preferred_element_type=jnp.float32
    ) + jnp.einsum("tf,df->td", up_grad, up_full, preferred_element_type=jnp.float32)
    grad_gate_w = jnp.einsum("td,tf->df", ffn_in, gate_grad, preferred_element_type=jnp.float32)
    grad_up_w = jnp.einsum("td,tf->df", ffn_in, up_grad, preferred_element_type=jnp.float32)
    gate_two_tok = out_grad * branch
    scale_two_tok = ffn_in_grad * normed_two
    middle_grad = out_grad + norm_back(ffn_in_grad * (1.0 + scale_two), normed_two, inverse_two)
    attn_grad = (gate_one * middle_grad).astype(jnp.bfloat16)
    gate_one_tok = middle_grad * attn_out
    grad_out_w = jnp.einsum("td,te->de", mixed, attn_grad, preferred_element_type=jnp.float32)
    mixed_grad = jnp.einsum(
        "te,de->td", attn_grad, out_full, preferred_element_type=jnp.float32
    ).reshape(tok_rows, HEADS, HD)
    gate_cross_part = jnp.sum(mixed_grad * cross_out, axis=(0, 2)) * (1.0 - tanh_gate * tanh_gate)
    self_grad = mixed_grad.astype(jnp.bfloat16)
    cross_grad = (tanh_gate[None, :, None] * mixed_grad).astype(jnp.bfloat16)
    cross_dp = jnp.einsum(
        "qhd,khd->hqk", cross_grad, cap_value_heads, preferred_element_type=jnp.float32
    )
    cap_value_grad = jnp.einsum(
        "hqk,qhd->khd", cross_low, cross_grad, preferred_element_type=jnp.float32
    )
    cross_ds = (
        cross_probs * (cross_dp - jnp.sum(cross_probs * cross_dp, axis=-1, keepdims=True))
    ).astype(jnp.bfloat16)
    query_grad_cross = jnp.einsum(
        "hqk,khd->qhd", cross_ds, cap_key_heads, preferred_element_type=jnp.float32
    )
    cap_key_grad = (
        jnp.einsum("hqk,qhd->khd", cross_ds, query_rot, preferred_element_type=jnp.float32)
        * score_scale
    )
    row_delta = jnp.sum(self_grad.astype(jnp.float32) * self_out, axis=-1)
    query_piece = lax.all_gather(query_rot, "sp", axis=0, tiled=True)
    grad_piece = lax.all_gather(self_grad, "sp", axis=0, tiled=True)
    log_piece = lax.all_gather(log_total.astype(jnp.bfloat16), "sp", axis=0, tiled=True).astype(
        jnp.float32
    )
    delta_piece = lax.all_gather(row_delta.astype(jnp.bfloat16), "sp", axis=0, tiled=True).astype(
        jnp.float32
    )
    segment_piece = lax.all_gather(segment, "sp", axis=0, tiled=True)
    scores = (
        jnp.einsum("qhd,khd->hqk", query_piece, key_rot, preferred_element_type=jnp.float32)
        * score_scale
    )
    allowed = (segment_piece[:, None] == segment[None, :])[None]
    probs = jnp.where(allowed, jnp.exp(scores - jnp.transpose(log_piece)[:, :, None]), 0.0)
    value_acc = jnp.einsum(
        "hqk,qhd->khd", probs.astype(jnp.bfloat16), grad_piece, preferred_element_type=jnp.float32
    )
    prob_grad = jnp.einsum(
        "qhd,khd->hqk", grad_piece, value_rows, preferred_element_type=jnp.float32
    )
    score_grad = (probs * (prob_grad - jnp.transpose(delta_piece)[:, :, None])).astype(jnp.bfloat16)
    key_acc = jnp.einsum(
        "hqk,qhd->khd", score_grad, query_piece, preferred_element_type=jnp.float32
    )
    key_acc, value_acc = (key_acc, value_acc)
    key_piece = lax.all_gather(key_rot, "sp", axis=0, tiled=True)
    value_piece = lax.all_gather(value_rows, "sp", axis=0, tiled=True)
    segment_piece = lax.all_gather(segment, "sp", axis=0, tiled=True)
    scores = (
        jnp.einsum("qhd,khd->hqk", query_rot, key_piece, preferred_element_type=jnp.float32)
        * score_scale
    )
    allowed = (segment[:, None] == segment_piece[None, :])[None]
    probs = jnp.where(allowed, jnp.exp(scores - jnp.transpose(log_total)[:, :, None]), 0.0)
    prob_grad = jnp.einsum(
        "qhd,khd->hqk", self_grad, value_piece, preferred_element_type=jnp.float32
    )
    score_grad = (probs * (prob_grad - jnp.transpose(row_delta)[:, :, None])).astype(jnp.bfloat16)
    query_acc = jnp.einsum(
        "hqk,khd->qhd", score_grad, key_piece, preferred_element_type=jnp.float32
    )
    query_rot_grad = (query_acc + query_grad_cross) * score_scale
    key_rot_grad = key_acc * score_scale
    query_raw_grad = (
        norm_back(rotate_back(query_rot_grad, cos_table, sin_table), query_normed, inverse_query)
        .astype(jnp.bfloat16)
        .reshape(tok_rows, D)
    )
    key_raw_grad = (
        norm_back(rotate_back(key_rot_grad, cos_table, sin_table), key_normed, inverse_key)
        .astype(jnp.bfloat16)
        .reshape(tok_rows, D)
    )
    value_raw_grad = value_acc.astype(jnp.bfloat16).reshape(tok_rows, D)
    block_in_grad = (
        jnp.einsum("te,de->td", query_raw_grad, query_full, preferred_element_type=jnp.float32)
        + jnp.einsum("te,de->td", key_raw_grad, key_full, preferred_element_type=jnp.float32)
        + jnp.einsum("te,de->td", value_raw_grad, value_full, preferred_element_type=jnp.float32)
    )
    grad_query_w = jnp.einsum(
        "td,te->de", block_in, query_raw_grad, preferred_element_type=jnp.float32
    )
    grad_key_w = jnp.einsum("td,te->de", block_in, key_raw_grad, preferred_element_type=jnp.float32)
    grad_value_w = jnp.einsum(
        "td,te->de", block_in, value_raw_grad, preferred_element_type=jnp.float32
    )
    scale_one_tok = block_in_grad * normed_one
    inputs_grad = middle_grad + norm_back(
        block_in_grad * (1.0 + scale_one), normed_one, inverse_one
    )
    mod_grad_part = jnp.concatenate(
        [
            per_clip(select, block_in_grad),
            per_clip(select, scale_one_tok),
            per_clip(select, gate_one_tok),
            per_clip(select, ffn_in_grad),
            per_clip(select, scale_two_tok),
            per_clip(select, gate_two_tok),
        ],
        axis=1,
    )
    cap_key_home, cap_value_home, mod_grad = (
        lax.psum_scatter(
            cap_key_grad.reshape(CLIPS, CAP, D).astype(jnp.bfloat16),
            "sp",
            scatter_dimension=1,
            tiled=True,
        ).astype(jnp.float32),
        lax.psum_scatter(
            cap_value_grad.reshape(CLIPS, CAP, D).astype(jnp.bfloat16),
            "sp",
            scatter_dimension=1,
            tiled=True,
        ).astype(jnp.float32),
        lax.psum_scatter(
            mod_grad_part.astype(jnp.bfloat16), "sp", scatter_dimension=1, tiled=True
        ).astype(jnp.float32),
    )
    cap_key_low = cap_key_home.astype(jnp.bfloat16)
    cap_value_low = cap_value_home.astype(jnp.bfloat16)
    mod_low = mod_grad.astype(jnp.bfloat16)
    caption_grad = jnp.einsum(
        "cpd,ed->cpe", cap_key_low, text_key_full, preferred_element_type=jnp.float32
    ) + jnp.einsum(
        "cpd,ed->cpe", cap_value_low, text_value_full, preferred_element_type=jnp.float32
    )
    grad_text_key = jnp.einsum(
        "cpe,cpd->ed", caption_feats, cap_key_low, preferred_element_type=jnp.float32
    )
    grad_text_value = jnp.einsum(
        "cpe,cpd->ed", caption_feats, cap_value_low, preferred_element_type=jnp.float32
    )
    grad_ada = jnp.einsum("cu,cv->uv", cond_act, mod_low, preferred_element_type=jnp.float32)
    grad_bias = jnp.sum(mod_low.astype(jnp.float32), axis=0)
    cond_part = jnp.einsum("cv,uv->cu", mod_low, w_ada, preferred_element_type=jnp.float32)
    cond_sum, gate_sum = lax.psum((cond_part, gate_cross_part), "sp")
    sigmoid_cond = jax.nn.sigmoid(cond_row)
    cond_grad = cond_sum * sigmoid_cond * (1.0 + cond_row * (1.0 - sigmoid_cond))
    home = (
        lax.psum_scatter(
            grad_query_w.astype(jnp.bfloat16), "sp", scatter_dimension=0, tiled=True
        ).astype(jnp.float32),
        lax.psum_scatter(
            grad_key_w.astype(jnp.bfloat16), "sp", scatter_dimension=0, tiled=True
        ).astype(jnp.float32),
        lax.psum_scatter(
            grad_value_w.astype(jnp.bfloat16), "sp", scatter_dimension=0, tiled=True
        ).astype(jnp.float32),
        lax.psum_scatter(
            grad_out_w.astype(jnp.bfloat16), "sp", scatter_dimension=0, tiled=True
        ).astype(jnp.float32),
        lax.psum_scatter(
            grad_gate_w.astype(jnp.bfloat16), "sp", scatter_dimension=0, tiled=True
        ).astype(jnp.float32),
        lax.psum_scatter(
            grad_up_w.astype(jnp.bfloat16), "sp", scatter_dimension=0, tiled=True
        ).astype(jnp.float32),
        lax.psum_scatter(
            grad_down.astype(jnp.bfloat16), "sp", scatter_dimension=0, tiled=True
        ).astype(jnp.float32),
        lax.psum_scatter(
            grad_text_key.astype(jnp.bfloat16), "sp", scatter_dimension=0, tiled=True
        ).astype(jnp.float32),
        lax.psum_scatter(
            grad_text_value.astype(jnp.bfloat16), "sp", scatter_dimension=0, tiled=True
        ).astype(jnp.float32),
    )
    totals = (
        lax.psum(home[0].astype(jnp.bfloat16), "dp").astype(jnp.float32),
        lax.psum(home[1].astype(jnp.bfloat16), "dp").astype(jnp.float32),
        lax.psum(home[2].astype(jnp.bfloat16), "dp").astype(jnp.float32),
        lax.psum(home[3].astype(jnp.bfloat16), "dp").astype(jnp.float32),
        lax.psum(home[4].astype(jnp.bfloat16), "dp").astype(jnp.float32),
        lax.psum(home[5].astype(jnp.bfloat16), "dp").astype(jnp.float32),
        lax.psum(home[6].astype(jnp.bfloat16), "dp").astype(jnp.float32),
        lax.psum(home[7].astype(jnp.bfloat16), "dp").astype(jnp.float32),
        lax.psum(home[8].astype(jnp.bfloat16), "dp").astype(jnp.float32),
        lax.psum(grad_ada.astype(jnp.bfloat16), "dp").astype(jnp.float32),
        lax.psum(grad_bias.astype(jnp.bfloat16), "dp").astype(jnp.float32),
        lax.psum(gate_sum.astype(jnp.bfloat16), "dp").astype(jnp.float32),
    )
    (
        d_query,
        d_key,
        d_value,
        d_out,
        d_gate_w,
        d_up_w,
        d_down_w,
        d_text_key,
        d_text_value,
        d_ada,
        d_bias,
        d_gate_cross,
    ) = totals
    return (
        result[None],
        inputs_grad[None],
        caption_grad[None],
        cond_grad[None],
        d_ada,
        d_bias,
        d_query,
        d_key,
        d_value,
        d_out,
        d_gate_cross,
        d_text_key,
        d_text_value,
        d_gate_w,
        d_up_w,
        d_down_w,
    )


MIN_CLIP = 1024
N_DP = 4
VMEM_BYTES = 48 * 1024 * 1024
NT = (((1,), (1,)), ((), ()))
TN = (((0,), (0,)), ((), ()))
F32 = jnp.float32
BF16 = jnp.bfloat16


def dot(left, right, dims=(((1,), (0,)), ((), ()))):
    return lax.dot_general(left, right, dims, preferred_element_type=F32)


class Ring:
    def __init__(self, size):
        self.size = size
        self.order = list(range(0, size, 2)) + list(range(size - 1, 0, -2))
        self.up = [(self.order[i], self.order[(i + 1) % size]) for i in range(size)]
        self.down = [(b, a) for a, b in self.up]
        place = [0] * size
        for spot, device in enumerate(self.order):
            place[device] = spot
        self.spot = jnp.array(place, jnp.int32)[lax.axis_index("sp")]

    def device(self, shift):
        return jnp.array(self.order, jnp.int32)[(self.spot + shift + self.size) % self.size]

    def send_up(self, value):
        return lax.ppermute(value, "sp", self.up)

    def send_down(self, value):
        return lax.ppermute(value, "sp", self.down)

    def gather(self, own):
        half = own.shape[0] // 2
        blocks = [(self.device(0), 0, own)]
        above = below = own
        for step in range(1, self.size // 2):
            above, below = self.send_up(above), self.send_down(below)
            blocks += [(self.device(-step), 0, above), (self.device(step), 0, below)]
        step = self.size // 2
        blocks += [
            (self.device(step), 0, self.send_up(above[:half])),
            (self.device(step), half, self.send_down(below[half:])),
        ]
        return blocks

    def gather_whole(self, own):
        whole = jnp.zeros((self.size,) + own.shape, own.dtype)
        for device, start, block in self.gather(own):
            whole = lax.dynamic_update_slice(
                whole, block[None], (device, start) + (0,) * (own.ndim - 1)
            )
        return whole

    def scatter(self, part):
        far = self.size // 2
        first = part(self.device(far))
        half = first.shape[0] // 2
        above = self.send_up(first[:half].astype(BF16))
        below = self.send_down(first[half:].astype(BF16))
        for step in range(far - 1, 0, -1):
            upper, lower = part(self.device(step)), part(self.device(-step))
            if step == far - 1:
                upper = jnp.concatenate([upper[:half] + above.astype(F32), upper[half:].astype(F32)])
                lower = jnp.concatenate([lower[:half].astype(F32), lower[half:] + below.astype(F32)])
            else:
                upper = upper + above.astype(F32)
                lower = lower + below.astype(F32)
            above = self.send_up(upper.astype(BF16))
            below = self.send_down(lower.astype(BF16))
        return part(self.device(0)) + above.astype(F32) + below.astype(F32)


def across(value, bit):
    return lax.ppermute(value, "dp", [(i, i ^ bit) for i in range(N_DP)])


def gather_packs(value):
    far = across(value, 2)
    return [value, far, across(value, 1), across(far, 1)]


def sum_packs(parts):
    own = parts[0].astype(F32) + across(parts[2].astype(BF16), 1).astype(F32)
    far = parts[1].astype(F32) + across(parts[3].astype(BF16), 1).astype(F32)
    return own + across(far.astype(BF16), 2).astype(F32)


def in_order(blocks):
    member = lax.axis_index("dp")
    stacked = jnp.stack(blocks)
    place = jnp.array([0, 2, 1, 3], jnp.int32)
    return jnp.stack(
        [lax.dynamic_index_in_dim(stacked, place[member ^ i], 0, False) for i in range(N_DP)]
    )


def gather_small(value, axis_name):
    size = lax.axis_size(axis_name)
    return lax.all_to_all(
        jnp.broadcast_to(value[None], (size,) + value.shape), axis_name, 0, 0, tiled=True
    )


def exchange(value):
    return lax.all_to_all(value, "sp", 0, 0, tiled=True)


def turn(values, cos, sin):
    half = HD // 2
    a, b = values[:half], values[half:]
    return jnp.concatenate([a * cos - b * sin, a * sin + b * cos], axis=0)


def turn_back(grads, cos, sin):
    half = HD // 2
    a, b = grads[:half], grads[half:]
    return jnp.concatenate([a * cos + b * sin, b * cos - a * sin], axis=0)


def head_inverse(values):
    return lax.rsqrt(jnp.mean(values * values, axis=0, keepdims=True) + EPSILON)


def project_kernel(x_ref, shift_ref, scale_ref, w_ref, cos_ref, sin_ref, in_ref, out_ref, raw_ref):
    heads = w_ref.shape[0] // (3 * HD)
    half = x_ref.shape[1] // 2
    for clip in range(CLIPS):
        x = x_ref[0, clip * half : (clip + 1) * half, :].astype(F32)
        inverse = lax.rsqrt(jnp.mean(x * x, axis=-1, keepdims=True) + EPSILON)
        block = x * inverse * (1.0 + scale_ref[clip : clip + 1, :]) + shift_ref[clip : clip + 1, :]
        block = block.astype(BF16)
        in_ref[clip] = block
        raw = dot(w_ref[...], block, NT)
        raw_ref[clip] = raw[: 2 * heads * HD]
        cos, sin = cos_ref[clip], sin_ref[clip]
        for head in range(2 * heads):
            rows = raw[head * HD : (head + 1) * HD]
            rotated = turn(rows * head_inverse(rows), cos, sin)
            out_ref[clip, head * HD : (head + 1) * HD, :] = rotated.astype(BF16)
        out_ref[clip, 2 * heads * HD :, :] = raw[2 * heads * HD :].astype(BF16)


def project(tokens, shift, scale, weight, cos, sin):
    devices, rows, width = tokens.shape
    half = rows // 2
    columns = weight.shape[0]
    length = devices * half
    return pl.pallas_call(
        project_kernel,
        grid=(devices,),
        in_specs=[
            pl.BlockSpec((1, rows, width), lambda i: (i, 0, 0)),
            pl.BlockSpec((CLIPS, width), lambda i: (0, 0)),
            pl.BlockSpec((CLIPS, width), lambda i: (0, 0)),
            pl.BlockSpec((columns, width), lambda i: (0, 0)),
            pl.BlockSpec((CLIPS, HD // 2, half), lambda i: (0, 0, i)),
            pl.BlockSpec((CLIPS, HD // 2, half), lambda i: (0, 0, i)),
        ],
        out_specs=[
            pl.BlockSpec((CLIPS, half, width), lambda i: (0, i, 0)),
            pl.BlockSpec((CLIPS, columns, half), lambda i: (0, 0, i)),
            pl.BlockSpec((CLIPS, 2 * columns // 3, half), lambda i: (0, 0, i)),
        ],
        out_shape=[
            jax.ShapeDtypeStruct((CLIPS, length, width), BF16),
            jax.ShapeDtypeStruct((CLIPS, columns, length), BF16),
            jax.ShapeDtypeStruct((CLIPS, 2 * columns // 3, length), F32),
        ],
        compiler_params=pltpu.CompilerParams(vmem_limit_bytes=VMEM_BYTES),
        cost_estimate=pl.CostEstimate(
            flops=2 * CLIPS * length * width * columns,
            bytes_accessed=4 * CLIPS * length * width + 8 * CLIPS * length * columns,
            transcendentals=0,
        ),
    )(tokens, shift, scale, weight, cos, sin)


def cross_probabilities(cap_key, query):
    scores = dot(cap_key, query, TN) * HD**-0.5
    grown = jnp.exp(scores - jnp.max(scores, axis=0, keepdims=True))
    return grown / jnp.sum(grown, axis=0, keepdims=True)


def attend_kernel(
    gate_ref, q_ref, k_ref, v_ref, ck_ref, cv_ref, mixed_ref, self_ref, cross_ref, log_ref, *, block
):
    length = q_ref.shape[2]
    half = mixed_ref.shape[2]
    gate = gate_ref[pl.program_id(1)]
    keys = k_ref[0]
    for start in range(0, length, block):
        query = q_ref[0, :, start : start + block]
        grown = jnp.exp(dot(keys, query, TN) * HD**-0.5)
        total = jnp.sum(grown, axis=0, keepdims=True)
        self_out = dot(v_ref[0], grown.astype(BF16)) / total
        probs = cross_probabilities(ck_ref[...], query)
        cross_out = dot(cv_ref[...], probs.astype(BF16))
        self_ref[0, :, start : start + block] = self_out
        cross_ref[0, :, start : start + block] = cross_out
        log_ref[0, 0, :, start : start + block] = jnp.log(total)
        mixed = (self_out + gate * cross_out).astype(BF16)
        for piece in range(block // half):
            mixed_ref[start // half + piece] = mixed[:, piece * half : (piece + 1) * half]


def attend(gate, qkv, cap_key, cap_value, half):
    clips, columns, length = qkv.shape
    heads = columns // (3 * HD)
    head_spec = lambda first: pl.BlockSpec((1, HD, length), lambda c, h: (c, first * heads + h, 0))
    cap_spec = pl.BlockSpec((HD, CAP), lambda c, h: (h, c))
    own_spec = pl.BlockSpec((1, HD, length), lambda c, h: (c, h, 0))
    return pl.pallas_call(
        functools.partial(attend_kernel, block=2 * half),
        grid=(clips, heads),
        in_specs=[
            pl.BlockSpec(memory_space=pltpu.SMEM),
            head_spec(0),
            head_spec(1),
            head_spec(2),
            cap_spec,
            cap_spec,
        ],
        out_specs=[
            pl.BlockSpec((length // half, HD, half), lambda c, h: (0, h, c)),
            own_spec,
            own_spec,
            pl.BlockSpec((1, 1, 1, length), lambda c, h: (c, h, 0, 0)),
        ],
        out_shape=[
            jax.ShapeDtypeStruct((length // half, heads * HD, clips * half), BF16),
            jax.ShapeDtypeStruct((clips, heads * HD, length), F32),
            jax.ShapeDtypeStruct((clips, heads * HD, length), F32),
            jax.ShapeDtypeStruct((clips, heads, 1, length), F32),
        ],
        compiler_params=pltpu.CompilerParams(vmem_limit_bytes=VMEM_BYTES),
        cost_estimate=pl.CostEstimate(
            flops=4 * clips * heads * length * length * HD * 4,
            bytes_accessed=clips * heads * length * HD * 20,
            transcendentals=clips * heads * length * length,
        ),
    )(gate, qkv, qkv, qkv, cap_key, cap_value)


def attend_back_kernel(
    gate_ref,
    q_ref,
    k_ref,
    v_ref,
    ck_ref,
    cv_ref,
    grad_ref,
    self_ref,
    cross_ref,
    log_ref,
    raw_q_ref,
    raw_k_ref,
    cos_ref,
    sin_ref,
    grads_ref,
    cap_ref,
    gate_grad_ref,
    key_acc,
    value_acc,
    *,
    block,
):
    length = q_ref.shape[2]
    half = grad_ref.shape[2]
    score_scale = HD**-0.5
    gate = gate_ref[pl.program_id(1)]
    keys, values = k_ref[0], v_ref[0]
    cap_key, cap_value = ck_ref[...], cv_ref[...]
    cap_key_grad = jnp.zeros((HD, CAP), F32)
    cap_value_grad = jnp.zeros((HD, CAP), F32)
    for start in range(0, length, block):
        span = slice(start, start + block)
        query = q_ref[0, :, span]
        grad = jnp.concatenate(
            [grad_ref[start // half + piece] for piece in range(block // half)], axis=1
        )
        wide = grad.astype(F32)
        delta = jnp.sum(wide * self_ref[0, :, span], axis=0, keepdims=True)
        gate_grad_ref[0, 0, :, span] = jnp.sum(
            wide * cross_ref[0, :, span], axis=0, keepdims=True
        )
        probs = jnp.exp(dot(keys, query, TN) * score_scale - log_ref[0, 0, :, span])
        score_grad = (probs * (dot(values, grad, TN) - delta)).astype(BF16)
        value_part = dot(grad, probs.astype(BF16), NT)
        key_part = dot(query, score_grad, NT)
        if start == 0:
            value_acc[...] = value_part
            key_acc[...] = key_part
        else:
            value_acc[...] += value_part
            key_acc[...] += key_part
        query_grad = dot(keys, score_grad)
        cross_grad = (gate * wide).astype(BF16)
        cross_probs = cross_probabilities(cap_key, query)
        cross_dp = dot(cap_value, cross_grad, TN)
        cross_score = cross_probs * (
            cross_dp - jnp.sum(cross_probs * cross_dp, axis=0, keepdims=True)
        )
        cross_score = cross_score.astype(BF16)
        cap_value_grad += dot(cross_grad, cross_probs.astype(BF16), NT)
        cap_key_grad += dot(query, cross_score, NT)
        query_grad = (query_grad + dot(cap_key, cross_score)) * score_scale
        raw = raw_q_ref[0, :, span]
        inverse = head_inverse(raw)
        normed = raw * inverse
        turned = turn_back(query_grad, cos_ref[0, :, span], sin_ref[0, :, span])
        mean = jnp.mean(turned * normed, axis=0, keepdims=True)
        grads_ref[0, 0, :, span] = (inverse * (turned - normed * mean)).astype(BF16)
    for start in range(0, length, block):
        span = slice(start, start + block)
        raw = raw_k_ref[0, :, span]
        inverse = head_inverse(raw)
        normed = raw * inverse
        turned = turn_back(
            key_acc[:, span] * score_scale, cos_ref[0, :, span], sin_ref[0, :, span]
        )
        mean = jnp.mean(turned * normed, axis=0, keepdims=True)
        grads_ref[0, 1, :, span] = (inverse * (turned - normed * mean)).astype(BF16)
        grads_ref[0, 2, :, span] = value_acc[:, span].astype(BF16)
    cap_ref[0] = (cap_key_grad * score_scale).astype(BF16)
    cap_ref[1] = cap_value_grad.astype(BF16)


def attend_back(gate, qkv, cap_key, cap_value, grad, self_out, cross_out, log_total, raw, cos, sin):
    clips, columns, length = qkv.shape
    heads = columns // (3 * HD)
    half = length // grad.shape[0]
    head_spec = lambda first: pl.BlockSpec((1, HD, length), lambda c, h: (c, first * heads + h, 0))
    cap_spec = pl.BlockSpec((HD, CAP), lambda c, h: (h, c))
    table_spec = pl.BlockSpec((1, HD // 2, length), lambda c, h: (c, 0, 0))
    row_spec = pl.BlockSpec((1, 1, 1, length), lambda c, h: (c, h, 0, 0))
    return pl.pallas_call(
        functools.partial(attend_back_kernel, block=2 * half),
        grid=(clips, heads),
        in_specs=[
            pl.BlockSpec(memory_space=pltpu.SMEM),
            head_spec(0),
            head_spec(1),
            head_spec(2),
            cap_spec,
            cap_spec,
            pl.BlockSpec((length // half, HD, half), lambda c, h: (0, h, c)),
            head_spec(0),
            head_spec(0),
            row_spec,
            head_spec(0),
            head_spec(1),
            table_spec,
            table_spec,
        ],
        out_specs=[
            pl.BlockSpec((1, 3, HD, length), lambda c, h: (c, 0, h, 0)),
            pl.BlockSpec((2, HD, CAP), lambda c, h: (0, h, c)),
            row_spec,
        ],
        out_shape=[
            jax.ShapeDtypeStruct((clips, 3, heads * HD, length), BF16),
            jax.ShapeDtypeStruct((2, heads * HD, clips * CAP), BF16),
            jax.ShapeDtypeStruct((clips, heads, 1, length), F32),
        ],
        scratch_shapes=[pltpu.VMEM((HD, length), F32), pltpu.VMEM((HD, length), F32)],
        compiler_params=pltpu.CompilerParams(vmem_limit_bytes=VMEM_BYTES),
        cost_estimate=pl.CostEstimate(
            flops=10 * clips * heads * length * length * HD * 4,
            bytes_accessed=clips * heads * length * HD * 32,
            transcendentals=clips * heads * length * length,
        ),
    )(
        gate,
        qkv,
        qkv,
        qkv,
        cap_key,
        cap_value,
        grad,
        self_out,
        cross_out,
        log_total,
        raw,
        raw,
        cos,
        sin,
    )


def clip_sums(values):
    return jnp.sum(values.reshape(CLIPS, -1, values.shape[-1]), axis=1)


def split_heads(
    tokens,
    cotangent,
    captions,
    conditioning,
    clip_lens,
    w_ada,
    b_ada,
    w_query,
    w_key,
    w_value,
    w_out,
    gate_cross,
    w_text_key,
    w_text_value,
    w_gate,
    w_up,
    w_down,
):
    shard = lax.axis_index("sp")
    member = lax.axis_index("dp")
    size = lax.axis_size("sp")
    ring = Ring(size)
    rows = tokens.shape[1]
    half = rows // 2
    own_cols = D // size
    heads = HEADS // size
    ff = w_gate.shape[1]
    ff_rows = ff // size
    ff_part = ff_rows // N_DP
    k_rows = D // size
    k_part = k_rows // N_DP
    text_rows = w_text_key.shape[0]

    inputs = tokens[0].astype(F32)
    out_grad = cotangent[0].astype(F32)

    cond_row = conditioning[0]
    cond_act = jax.nn.silu(cond_row).astype(BF16)
    mod_part = dot(cond_act, w_ada) + b_ada[None, :]
    modulation = jnp.transpose(gather_small(mod_part, "sp"), (1, 0, 2)).reshape(CLIPS, -1)
    shift_one, scale_one, gate_one, shift_two, scale_two, gate_two = jnp.split(modulation, 6, axis=1)

    def by_row(values):
        return jnp.repeat(values, half, axis=0)

    start = member * k_part
    quarter = jnp.stack(
        [
            lax.dynamic_slice(w, (start, 0), (k_part, D)).reshape(k_part, size, own_cols)
            for w in (w_query, w_key, w_value)
        ],
        axis=2,
    )
    quarter = jnp.transpose(quarter, (1, 0, 2, 3)).reshape(size, k_part, 3 * own_cols)
    w_qkv = in_order(gather_packs(exchange(quarter)))
    w_qkv = jnp.transpose(w_qkv, (3, 1, 0, 2)).reshape(3 * own_cols, D)

    cap_part = captions[0].reshape(-1, size, text_rows)
    caption_cols = exchange(jnp.transpose(cap_part, (1, 0, 2)))
    caption_cols = (
        caption_cols.reshape(size, CLIPS, -1, text_rows).transpose(1, 0, 2, 3).reshape(-1, text_rows)
    )
    cap_terms = jnp.stack(
        [
            dot(w, caption_cols, (((0,), (1,)), ((), ()))).astype(BF16)
            for w in (w_text_key, w_text_value)
        ]
    )

    token_blocks = ring.gather_whole(tokens[0])

    cap_heads = ring.scatter(
        lambda device: jnp.transpose(
            lax.dynamic_slice(
                cap_terms, (0, device * own_cols, 0), (2, own_cols, CLIPS * CAP)
            ),
            (1, 0, 2),
        )
    ).astype(BF16)
    cap_key, cap_value = cap_heads[:, 0], cap_heads[:, 1]

    lane = jnp.arange(size * half, dtype=jnp.int32)
    mirrored = (size - 1 - lane // half) * half + lane % half
    freq = 10000.0 ** (-(jnp.arange(HD // 2, dtype=F32) * 2.0 / HD))
    angle = jnp.stack([lane, mirrored]).astype(F32)[:, None, :] * freq[None, :, None]
    cos, sin = jnp.cos(angle), jnp.sin(angle)

    block_in, qkv, raw = project(token_blocks, shift_one, scale_one, w_qkv, cos, sin)

    out_piece = lax.dynamic_slice(w_out, (0, member * (D // N_DP)), (k_rows, D // N_DP))
    gate_piece = jnp.concatenate(
        [
            lax.dynamic_slice(w, (0, i * ff_rows + member * ff_part), (k_rows, ff_part))
            for w in (w_gate, w_up)
            for i in range(size)
        ],
        axis=1,
    )
    down_piece = lax.dynamic_slice(w_down, (member * ff_part, 0), (ff_part, D))
    token_blocks, out_piece, gate_piece, down_piece = lax.optimization_barrier(
        (token_blocks, out_piece, gate_piece, down_piece)
    )
    out_cols = ring.gather_whole(out_piece).reshape(D, D // N_DP)
    out_full = jnp.transpose(in_order(gather_packs(out_cols)), (1, 0, 2)).reshape(D, D)
    gate_up = ring.gather_whole(gate_piece).reshape(D, 2 * ff // N_DP)
    down = ring.gather_whole(down_piece).reshape(ff // N_DP, D)

    tanh_gate = jnp.tanh(gate_cross)
    own_gate = lax.dynamic_slice(tanh_gate, (shard * heads,), (heads,))
    mixed_blocks, self_out, cross_out, log_total = attend(own_gate, qkv, cap_key, cap_value, half)
    mixed = exchange(mixed_blocks).reshape(D, rows)
    attn_out = dot(mixed, out_full, TN)

    inverse_one = inverse_rms(inputs)
    normed_one = inputs * inverse_one
    middle = inputs + by_row(gate_one) * attn_out
    inverse_two = inverse_rms(middle)
    normed_two = middle * inverse_two
    ffn_in = (normed_two * (1.0 + by_row(scale_two)) + by_row(shift_two)).astype(BF16)
    branch_grad = (by_row(gate_two) * out_grad).astype(BF16)
    branch_grads = jnp.concatenate(gather_packs(branch_grad))
    ffn_ins = jnp.concatenate(gather_packs(ffn_in))
    hidden_units = ff // N_DP
    gate_proj = dot(ffn_ins, gate_up[:, :hidden_units])
    up_proj = dot(ffn_ins, gate_up[:, hidden_units:])
    sigmoid_gate = jax.nn.sigmoid(gate_proj)
    silu_gate = gate_proj * sigmoid_gate
    hidden = (silu_gate * up_proj).astype(BF16)
    hidden_grad = dot(branch_grads, down, NT)
    gate_grad = (
        hidden_grad * up_proj * sigmoid_gate * (1.0 + gate_proj * (1.0 - sigmoid_gate))
    ).astype(BF16)
    up_grad = (hidden_grad * silu_gate).astype(BF16)
    ffn_terms = dot(gate_grad, gate_up[:, :hidden_units], NT) + dot(
        up_grad, gate_up[:, hidden_units:], NT
    )
    ffn_in_grad = sum_packs([ffn_terms[i * rows : (i + 1) * rows] for i in range(N_DP)])
    branch_terms = dot(hidden, down)
    branch = sum_packs([branch_terms[i * rows : (i + 1) * rows] for i in range(N_DP)])
    result = (middle + by_row(gate_two) * branch).astype(BF16)
    grad_down = dot(hidden, branch_grads, TN).astype(BF16)
    grad_gate = dot(ffn_ins, gate_grad, TN).astype(BF16)
    grad_up = dot(ffn_ins, up_grad, TN).astype(BF16)

    middle_grad = out_grad + norm_back(
        ffn_in_grad * (1.0 + by_row(scale_two)), normed_two, inverse_two
    )
    attn_grad = (by_row(gate_one) * middle_grad).astype(BF16)
    mixed_grad = dot(out_full, attn_grad, NT).astype(BF16).reshape(size, own_cols, rows)
    grad_out = dot(mixed, attn_grad).astype(BF16)
    head_grad = exchange(mixed_grad)

    grads, cap_grads, gate_rows = attend_back(
        own_gate, qkv, cap_key, cap_value, head_grad, self_out, cross_out, log_total, raw, cos, sin
    )
    grads = grads.reshape(CLIPS, 3 * own_cols, size * half)

    def token_grad(device):
        columns = lax.dynamic_slice(
            grads, (0, 0, device * half), (CLIPS, 3 * own_cols, half)
        )
        return jnp.concatenate([dot(columns[c], w_qkv, TN) for c in range(CLIPS)])

    block_in_grad = ring.scatter(token_grad)
    grad_qkv = (
        dot(block_in[0], grads[0], (((0,), (1,)), ((), ())))
        + dot(block_in[1], grads[1], (((0,), (1,)), ((), ())))
    ).astype(BF16)

    inputs_grad = middle_grad + norm_back(
        block_in_grad * (1.0 + by_row(scale_one)), normed_one, inverse_one
    )

    mod_terms = jnp.concatenate(
        [
            clip_sums(block_in_grad),
            clip_sums(block_in_grad * normed_one),
            clip_sums(middle_grad * attn_out),
            clip_sums(ffn_in_grad),
            clip_sums(ffn_in_grad * normed_two),
            clip_sums(out_grad * branch),
        ],
        axis=1,
    )
    mod_terms = jnp.transpose(mod_terms.reshape(CLIPS, size, -1), (1, 0, 2))
    mod_low = jnp.sum(exchange(mod_terms), axis=0).astype(BF16)
    cond_part = dot(mod_low, w_ada, NT)
    cond_sum = jnp.sum(gather_small(cond_part, "sp"), axis=0)
    sigmoid_cond = jax.nn.sigmoid(cond_row)
    cond_grad = cond_sum * sigmoid_cond * (1.0 + cond_row * (1.0 - sigmoid_cond))
    both = jnp.concatenate([cond_act, mod_low], axis=1)
    both_all = gather_small(both, "dp").reshape(N_DP * CLIPS, -1)
    cond_all, mod_all = both_all[:, : cond_act.shape[1]], both_all[:, cond_act.shape[1] :]
    d_ada = dot(cond_all, mod_all, TN)
    d_bias = jnp.sum(mod_all.astype(F32), axis=0)
    gate_own = jnp.sum(gate_rows, axis=(0, 2, 3))
    gate_all = jnp.sum(
        gather_small(gather_small(gate_own, "sp").reshape(-1), "dp"), axis=0
    )
    d_gate_cross = gate_all * (1.0 - tanh_gate * tanh_gate)

    cap_all = ring.gather_whole(jnp.transpose(cap_grads, (1, 0, 2)))
    cap_all = cap_all.reshape(D, 2, CLIPS * CAP)
    caption_grad = dot(w_text_key, cap_all[:, 0]) + dot(w_text_value, cap_all[:, 1])
    caption_grad = caption_grad.astype(BF16).reshape(text_rows, CLIPS, size, -1)
    caption_grad = exchange(jnp.transpose(caption_grad, (2, 1, 3, 0)))
    caption_grad = (
        jnp.transpose(caption_grad, (1, 2, 0, 3)).reshape(CLIPS, -1, size * text_rows).astype(F32)
    )
    text_terms = [
        dot(caption_cols, cap_all[:, i], (((0,), (1,)), ((), ()))).astype(BF16) for i in range(2)
    ]
    text_rows_part = text_rows // N_DP
    text_terms = jnp.concatenate(text_terms, axis=1)

    def rows_for(offset):
        return lax.dynamic_slice(
            text_terms, ((member ^ offset) * text_rows_part, 0), (text_rows_part, 2 * D)
        )

    text_home = sum_packs([rows_for(offset) for offset in (0, 2, 1, 3)]).astype(BF16)
    text_home = in_order(gather_packs(text_home)).reshape(text_rows, 2 * D).astype(F32)
    d_text_key, d_text_value = text_home[:, :D], text_home[:, D:]

    down_home = ring.scatter(
        lambda device: lax.dynamic_slice(grad_down, (device * ff_part, 0), (ff_part, D))
    ).astype(BF16)
    d_down = in_order(gather_packs(down_home)).reshape(ff_rows, D).astype(F32)

    def gate_home(terms):
        home = ring.scatter(
            lambda device: lax.dynamic_slice(
                terms, (device * k_rows, 0), (k_rows, hidden_units)
            )
        ).astype(BF16)
        whole = in_order(gather_packs(home.reshape(k_rows, size, ff_part)))
        return jnp.transpose(whole, (1, 2, 0, 3)).reshape(k_rows, ff).astype(F32)

    d_gate_w = gate_home(grad_gate)
    d_up_w = gate_home(grad_up)

    out_cols_part = D // N_DP

    def cols_for(offset):
        return lax.dynamic_slice(grad_out, (0, (member ^ offset) * out_cols_part), (D, out_cols_part))

    out_sum = sum_packs([cols_for(offset) for offset in (0, 2, 1, 3)])
    out_home = ring.scatter(
        lambda device: lax.dynamic_slice(out_sum, (device * k_rows, 0), (k_rows, out_cols_part))
    ).astype(BF16)
    d_out = jnp.transpose(in_order(gather_packs(out_home)), (1, 0, 2)).reshape(k_rows, D).astype(F32)

    grad_qkv = grad_qkv.reshape(size, N_DP, k_part, 3 * own_cols)

    def quarter_for(offset):
        return lax.dynamic_index_in_dim(grad_qkv, member ^ offset, 1, False)

    qkv_sum = sum_packs([quarter_for(offset) for offset in (0, 2, 1, 3)]).astype(BF16)
    qkv_home = in_order(gather_packs(exchange(qkv_sum)))
    qkv_home = qkv_home.reshape(N_DP, size, k_part, 3, own_cols)
    qkv_home = jnp.transpose(qkv_home, (3, 0, 2, 1, 4)).reshape(3, k_rows, D).astype(F32)
    return (
        result[None],
        inputs_grad[None],
        caption_grad[None],
        cond_grad[None],
        d_ada,
        d_bias,
        qkv_home[0],
        qkv_home[1],
        qkv_home[2],
        d_out,
        d_gate_cross,
        d_text_key,
        d_text_value,
        d_gate_w,
        d_up_w,
        d_down,
    )


def layer(*arrays):
    tokens, clip_lens = arrays[0], arrays[4]
    size = lax.axis_size("sp")
    pack = tokens.shape[1] * size
    even = HEADS % size == 0 and size % 2 == 0 and size >= 4
    fixed = pack == clip_lens.shape[1] * MIN_CLIP and tokens.shape[1] % 256 == 0
    if even and fixed and lax.axis_size("dp") == N_DP:
        return split_heads(*arrays)
    return local(*arrays)


def solution(mesh):
    return jax.shard_map(
        layer,
        mesh=mesh,
        in_specs=(
            P("dp", "sp", None),
            P("dp", "sp", None),
            P("dp", None, "sp", None),
            P("dp", None, None),
            P("dp", None),
            P(None, "sp"),
            P("sp"),
            P("sp", None),
            P("sp", None),
            P("sp", None),
            P("sp", None),
            P(),
            P("sp", None),
            P("sp", None),
            P("sp", None),
            P("sp", None),
            P("sp", None),
        ),
        out_specs=(
            P("dp", "sp", None),
            P("dp", "sp", None),
            P("dp", None, "sp", None),
            P("dp", None, None),
            P(None, "sp"),
            P("sp"),
            P("sp", None),
            P("sp", None),
            P("sp", None),
            P("sp", None),
            P(),
            P("sp", None),
            P("sp", None),
            P("sp", None),
            P("sp", None),
            P("sp", None),
        ),
        check_vma=False,
    )
```

```python
import functools

import jax
import jax.numpy as jnp
from jax import lax
from jax.experimental import pallas as pl
from jax.experimental.pallas import tpu as pltpu
from jax.sharding import PartitionSpec as P

D = 1536
HEADS = 24
HD = 64
TEXT = 4096
CAP = 128
CLIPS = 2


EPSILON = 1e-06
MASKED = -1e30
HIGHEST = lax.Precision.HIGHEST


def rope_tables(positions):
    half_width = HD // 2
    freq = 10000.0 ** (-(jnp.arange(half_width, dtype=jnp.float32) * 2.0 / HD))
    angle = positions.astype(jnp.float32)[:, None] * freq[None, :]
    return (jnp.cos(angle)[:, None, :], jnp.sin(angle)[:, None, :])


def rotate(values, cos_table, sin_table):
    half_width = values.shape[-1] // 2
    first_half = values[..., :half_width]
    second_half = values[..., half_width:]
    return jnp.concatenate(
        [
            first_half * cos_table - second_half * sin_table,
            first_half * sin_table + second_half * cos_table,
        ],
        axis=-1,
    )


def rotate_back(grads, cos_table, sin_table):
    half_width = grads.shape[-1] // 2
    first_half = grads[..., :half_width]
    second_half = grads[..., half_width:]
    return jnp.concatenate(
        [
            first_half * cos_table + second_half * sin_table,
            second_half * cos_table - first_half * sin_table,
        ],
        axis=-1,
    )


def inverse_rms(values):
    return lax.rsqrt(jnp.mean(values * values, axis=-1, keepdims=True) + EPSILON)


def norm_back(grads, normed, inverse):
    return inverse * (grads - normed * jnp.mean(grads * normed, axis=-1, keepdims=True))


def per_clip(select, values):
    return jnp.einsum("tc,td->cd", select, values, precision=HIGHEST)


def local(
    tokens,
    cotangent,
    captions,
    conditioning,
    clip_lens,
    w_ada,
    b_ada,
    w_query,
    w_key,
    w_value,
    w_out,
    gate_cross,
    w_text_key,
    w_text_value,
    w_gate,
    w_up,
    w_down,
):
    shard = lax.axis_index("sp")
    cycle_size = lax.axis_size("sp")
    tok_rows = tokens.shape[1]
    half_rows = tok_rows // 2
    score_scale = HD ** (-0.5)
    row_index = jnp.arange(tok_rows, dtype=jnp.int32)
    logical_block = jnp.where(row_index < half_rows, shard, 2 * cycle_size - 1 - shard)
    logical = logical_block * half_rows + row_index % half_rows
    lengths = clip_lens[0]
    clip_ends = jnp.cumsum(lengths)
    clip_starts = clip_ends - lengths
    clip_index = 0
    segment = (logical >= clip_ends[clip_index]).astype(jnp.int32)
    offset = jnp.zeros((tok_rows,), jnp.int32)
    for clip_index in range(CLIPS):
        offset = offset + jnp.where(segment == clip_index, clip_starts[clip_index], 0)
    positions = logical - offset
    inputs = tokens[0].astype(jnp.float32)
    cond_row = conditioning[0]
    cond_act = jax.nn.silu(cond_row).astype(jnp.bfloat16)
    mod_part = jnp.dot(cond_act, w_ada, preferred_element_type=jnp.float32) + b_ada[None, :]
    modulation = lax.all_gather(mod_part, "sp", axis=1, tiled=True)
    select = (segment[:, None] == jnp.arange(CLIPS, dtype=jnp.int32)[None, :]).astype(jnp.float32)
    per_token = jnp.dot(select, modulation, precision=HIGHEST)
    shift_one, scale_one, gate_one, shift_two, scale_two, gate_two = jnp.split(per_token, 6, axis=1)
    weights_full = (
        lax.all_gather(w_query, "sp", axis=0, tiled=True),
        lax.all_gather(w_key, "sp", axis=0, tiled=True),
        lax.all_gather(w_value, "sp", axis=0, tiled=True),
        lax.all_gather(w_out, "sp", axis=0, tiled=True),
        lax.all_gather(w_gate, "sp", axis=0, tiled=True),
        lax.all_gather(w_up, "sp", axis=0, tiled=True),
        lax.all_gather(w_down, "sp", axis=0, tiled=True),
        lax.all_gather(w_text_key, "sp", axis=0, tiled=True),
        lax.all_gather(w_text_value, "sp", axis=0, tiled=True),
    )
    (
        query_full,
        key_full,
        value_full,
        out_full,
        gate_full,
        up_full,
        down_full,
        text_key_full,
        text_value_full,
    ) = weights_full
    inverse_one = inverse_rms(inputs)
    normed_one = inputs * inverse_one
    block_in = (normed_one * (1.0 + scale_one) + shift_one).astype(jnp.bfloat16)
    cos_table, sin_table = rope_tables(positions)

    def project(weight):
        return jnp.dot(block_in, weight, preferred_element_type=jnp.float32).reshape(
            tok_rows, HEADS, HD
        )

    query_raw = project(query_full)
    inverse_query = inverse_rms(query_raw)
    query_normed = query_raw * inverse_query
    query_rot = rotate(query_normed, cos_table, sin_table).astype(jnp.bfloat16)
    key_raw = project(key_full)
    inverse_key = inverse_rms(key_raw)
    key_normed = key_raw * inverse_key
    key_rot = rotate(key_normed, cos_table, sin_table).astype(jnp.bfloat16)
    value_rows = project(value_full).astype(jnp.bfloat16)
    caption_feats = captions[0]
    flat_caption = caption_feats.reshape(-1, TEXT)
    cap_key_part = (
        jnp.dot(flat_caption, text_key_full, preferred_element_type=jnp.float32)
        .astype(jnp.bfloat16)
        .reshape(CLIPS, -1, D)
    )
    cap_value_part = (
        jnp.dot(flat_caption, text_value_full, preferred_element_type=jnp.float32)
        .astype(jnp.bfloat16)
        .reshape(CLIPS, -1, D)
    )
    cap_key_all, cap_value_all = (
        lax.all_gather(cap_key_part, "sp", axis=1, tiled=True),
        lax.all_gather(cap_value_part, "sp", axis=1, tiled=True),
    )
    cap_key_heads = cap_key_all.reshape(CLIPS * CAP, HEADS, HD)
    cap_value_heads = cap_value_all.reshape(CLIPS * CAP, HEADS, HD)
    caption_clip = jnp.arange(CLIPS * CAP, dtype=jnp.int32) // CAP
    run_max = jnp.full((HEADS, tok_rows), MASKED, jnp.float32)
    key_piece = lax.all_gather(key_rot, "sp", axis=0, tiled=True)
    value_piece = lax.all_gather(value_rows, "sp", axis=0, tiled=True)
    segment_piece = lax.all_gather(segment, "sp", axis=0, tiled=True)
    scores = (
        jnp.einsum("qhd,khd->hqk", query_rot, key_piece, preferred_element_type=jnp.float32)
        * score_scale
    )
    allowed = (segment[:, None] == segment_piece[None, :])[None]
    scores = jnp.where(allowed, scores, MASKED)
    new_max = jnp.maximum(run_max, jnp.max(scores, axis=-1))
    weights_exp = jnp.where(allowed, jnp.exp(scores - new_max[:, :, None]), 0.0)
    new_total = jnp.sum(weights_exp, axis=-1)
    new_acc = jnp.einsum(
        "hqk,khd->qhd",
        weights_exp.astype(jnp.bfloat16),
        value_piece,
        preferred_element_type=jnp.float32,
    )
    self_out = new_acc / jnp.transpose(new_total)[:, :, None]
    log_total = jnp.transpose(new_max + jnp.log(new_total))
    cross_scores = (
        jnp.einsum("qhd,khd->hqk", query_rot, cap_key_heads, preferred_element_type=jnp.float32)
        * score_scale
    )
    own_clip = (segment[:, None] == caption_clip[None, :])[None]
    cross_probs = jax.nn.softmax(jnp.where(own_clip, cross_scores, MASKED), axis=-1)
    cross_low = cross_probs.astype(jnp.bfloat16)
    cross_out = jnp.einsum(
        "hqk,khd->qhd", cross_low, cap_value_heads, preferred_element_type=jnp.float32
    )
    tanh_gate = jnp.tanh(gate_cross)
    mixed = (
        (self_out + tanh_gate[None, :, None] * cross_out).astype(jnp.bfloat16).reshape(tok_rows, D)
    )
    attn_out = jnp.dot(mixed, out_full, preferred_element_type=jnp.float32)
    middle = inputs + gate_one * attn_out
    inverse_two = inverse_rms(middle)
    normed_two = middle * inverse_two
    ffn_in = (normed_two * (1.0 + scale_two) + shift_two).astype(jnp.bfloat16)
    gate_proj = jnp.dot(ffn_in, gate_full, preferred_element_type=jnp.float32)
    up_proj = jnp.dot(ffn_in, up_full, preferred_element_type=jnp.float32)
    sigmoid_gate = jax.nn.sigmoid(gate_proj)
    silu_gate = jax.nn.silu(gate_proj)
    hidden = (silu_gate * up_proj).astype(jnp.bfloat16)
    branch = jnp.dot(hidden, down_full, preferred_element_type=jnp.float32)
    result = (middle + gate_two * branch).astype(jnp.bfloat16)
    out_grad = cotangent[0].astype(jnp.float32)
    branch_grad = (gate_two * out_grad).astype(jnp.bfloat16)
    hidden_grad = jnp.einsum(
        "td,fd->tf", branch_grad, down_full, preferred_element_type=jnp.float32
    )
    grad_down = jnp.einsum("tf,td->fd", hidden, branch_grad, preferred_element_type=jnp.float32)
    gate_grad = (
        hidden_grad * up_proj * sigmoid_gate * (1.0 + gate_proj * (1.0 - sigmoid_gate))
    ).astype(jnp.bfloat16)
    up_grad = (hidden_grad * silu_gate).astype(jnp.bfloat16)
    ffn_in_grad = jnp.einsum(
        "tf,df->td", gate_grad, gate_full, preferred_element_type=jnp.float32
    ) + jnp.einsum("tf,df->td", up_grad, up_full, preferred_element_type=jnp.float32)
    grad_gate_w = jnp.einsum("td,tf->df", ffn_in, gate_grad, preferred_element_type=jnp.float32)
    grad_up_w = jnp.einsum("td,tf->df", ffn_in, up_grad, preferred_element_type=jnp.float32)
    gate_two_tok = out_grad * branch
    scale_two_tok = ffn_in_grad * normed_two
    middle_grad = out_grad + norm_back(ffn_in_grad * (1.0 + scale_two), normed_two, inverse_two)
    attn_grad = (gate_one * middle_grad).astype(jnp.bfloat16)
    gate_one_tok = middle_grad * attn_out
    grad_out_w = jnp.einsum("td,te->de", mixed, attn_grad, preferred_element_type=jnp.float32)
    mixed_grad = jnp.einsum(
        "te,de->td", attn_grad, out_full, preferred_element_type=jnp.float32
    ).reshape(tok_rows, HEADS, HD)
    gate_cross_part = jnp.sum(mixed_grad * cross_out, axis=(0, 2)) * (1.0 - tanh_gate * tanh_gate)
    self_grad = mixed_grad.astype(jnp.bfloat16)
    cross_grad = (tanh_gate[None, :, None] * mixed_grad).astype(jnp.bfloat16)
    cross_dp = jnp.einsum(
        "qhd,khd->hqk", cross_grad, cap_value_heads, preferred_element_type=jnp.float32
    )
    cap_value_grad = jnp.einsum(
        "hqk,qhd->khd", cross_low, cross_grad, preferred_element_type=jnp.float32
    )
    cross_ds = (
        cross_probs * (cross_dp - jnp.sum(cross_probs * cross_dp, axis=-1, keepdims=True))
    ).astype(jnp.bfloat16)
    query_grad_cross = jnp.einsum(
        "hqk,khd->qhd", cross_ds, cap_key_heads, preferred_element_type=jnp.float32
    )
    cap_key_grad = (
        jnp.einsum("hqk,qhd->khd", cross_ds, query_rot, preferred_element_type=jnp.float32)
        * score_scale
    )
    row_delta = jnp.sum(self_grad.astype(jnp.float32) * self_out, axis=-1)
    query_piece = lax.all_gather(query_rot, "sp", axis=0, tiled=True)
    grad_piece = lax.all_gather(self_grad, "sp", axis=0, tiled=True)
    log_piece = lax.all_gather(log_total.astype(jnp.bfloat16), "sp", axis=0, tiled=True).astype(
        jnp.float32
    )
    delta_piece = lax.all_gather(row_delta.astype(jnp.bfloat16), "sp", axis=0, tiled=True).astype(
        jnp.float32
    )
    segment_piece = lax.all_gather(segment, "sp", axis=0, tiled=True)
    scores = (
        jnp.einsum("qhd,khd->hqk", query_piece, key_rot, preferred_element_type=jnp.float32)
        * score_scale
    )
    allowed = (segment_piece[:, None] == segment[None, :])[None]
    probs = jnp.where(allowed, jnp.exp(scores - jnp.transpose(log_piece)[:, :, None]), 0.0)
    value_acc = jnp.einsum(
        "hqk,qhd->khd", probs.astype(jnp.bfloat16), grad_piece, preferred_element_type=jnp.float32
    )
    prob_grad = jnp.einsum(
        "qhd,khd->hqk", grad_piece, value_rows, preferred_element_type=jnp.float32
    )
    score_grad = (probs * (prob_grad - jnp.transpose(delta_piece)[:, :, None])).astype(jnp.bfloat16)
    key_acc = jnp.einsum(
        "hqk,qhd->khd", score_grad, query_piece, preferred_element_type=jnp.float32
    )
    key_acc, value_acc = (key_acc, value_acc)
    key_piece = lax.all_gather(key_rot, "sp", axis=0, tiled=True)
    value_piece = lax.all_gather(value_rows, "sp", axis=0, tiled=True)
    segment_piece = lax.all_gather(segment, "sp", axis=0, tiled=True)
    scores = (
        jnp.einsum("qhd,khd->hqk", query_rot, key_piece, preferred_element_type=jnp.float32)
        * score_scale
    )
    allowed = (segment[:, None] == segment_piece[None, :])[None]
    probs = jnp.where(allowed, jnp.exp(scores - jnp.transpose(log_total)[:, :, None]), 0.0)
    prob_grad = jnp.einsum(
        "qhd,khd->hqk", self_grad, value_piece, preferred_element_type=jnp.float32
    )
    score_grad = (probs * (prob_grad - jnp.transpose(row_delta)[:, :, None])).astype(jnp.bfloat16)
    query_acc = jnp.einsum(
        "hqk,khd->qhd", score_grad, key_piece, preferred_element_type=jnp.float32
    )
    query_rot_grad = (query_acc + query_grad_cross) * score_scale
    key_rot_grad = key_acc * score_scale
    query_raw_grad = (
        norm_back(rotate_back(query_rot_grad, cos_table, sin_table), query_normed, inverse_query)
        .astype(jnp.bfloat16)
        .reshape(tok_rows, D)
    )
    key_raw_grad = (
        norm_back(rotate_back(key_rot_grad, cos_table, sin_table), key_normed, inverse_key)
        .astype(jnp.bfloat16)
        .reshape(tok_rows, D)
    )
    value_raw_grad = value_acc.astype(jnp.bfloat16).reshape(tok_rows, D)
    block_in_grad = (
        jnp.einsum("te,de->td", query_raw_grad, query_full, preferred_element_type=jnp.float32)
        + jnp.einsum("te,de->td", key_raw_grad, key_full, preferred_element_type=jnp.float32)
        + jnp.einsum("te,de->td", value_raw_grad, value_full, preferred_element_type=jnp.float32)
    )
    grad_query_w = jnp.einsum(
        "td,te->de", block_in, query_raw_grad, preferred_element_type=jnp.float32
    )
    grad_key_w = jnp.einsum("td,te->de", block_in, key_raw_grad, preferred_element_type=jnp.float32)
    grad_value_w = jnp.einsum(
        "td,te->de", block_in, value_raw_grad, preferred_element_type=jnp.float32
    )
    scale_one_tok = block_in_grad * normed_one
    inputs_grad = middle_grad + norm_back(
        block_in_grad * (1.0 + scale_one), normed_one, inverse_one
    )
    mod_grad_part = jnp.concatenate(
        [
            per_clip(select, block_in_grad),
            per_clip(select, scale_one_tok),
            per_clip(select, gate_one_tok),
            per_clip(select, ffn_in_grad),
            per_clip(select, scale_two_tok),
            per_clip(select, gate_two_tok),
        ],
        axis=1,
    )
    cap_key_home, cap_value_home, mod_grad = (
        lax.psum_scatter(
            cap_key_grad.reshape(CLIPS, CAP, D).astype(jnp.bfloat16),
            "sp",
            scatter_dimension=1,
            tiled=True,
        ).astype(jnp.float32),
        lax.psum_scatter(
            cap_value_grad.reshape(CLIPS, CAP, D).astype(jnp.bfloat16),
            "sp",
            scatter_dimension=1,
            tiled=True,
        ).astype(jnp.float32),
        lax.psum_scatter(
            mod_grad_part.astype(jnp.bfloat16), "sp", scatter_dimension=1, tiled=True
        ).astype(jnp.float32),
    )
    cap_key_low = cap_key_home.astype(jnp.bfloat16)
    cap_value_low = cap_value_home.astype(jnp.bfloat16)
    mod_low = mod_grad.astype(jnp.bfloat16)
    caption_grad = jnp.einsum(
        "cpd,ed->cpe", cap_key_low, text_key_full, preferred_element_type=jnp.float32
    ) + jnp.einsum(
        "cpd,ed->cpe", cap_value_low, text_value_full, preferred_element_type=jnp.float32
    )
    grad_text_key = jnp.einsum(
        "cpe,cpd->ed", caption_feats, cap_key_low, preferred_element_type=jnp.float32
    )
    grad_text_value = jnp.einsum(
        "cpe,cpd->ed", caption_feats, cap_value_low, preferred_element_type=jnp.float32
    )
    grad_ada = jnp.einsum("cu,cv->uv", cond_act, mod_low, preferred_element_type=jnp.float32)
    grad_bias = jnp.sum(mod_low.astype(jnp.float32), axis=0)
    cond_part = jnp.einsum("cv,uv->cu", mod_low, w_ada, preferred_element_type=jnp.float32)
    cond_sum, gate_sum = lax.psum((cond_part, gate_cross_part), "sp")
    sigmoid_cond = jax.nn.sigmoid(cond_row)
    cond_grad = cond_sum * sigmoid_cond * (1.0 + cond_row * (1.0 - sigmoid_cond))
    home = (
        lax.psum_scatter(
            grad_query_w.astype(jnp.bfloat16), "sp", scatter_dimension=0, tiled=True
        ).astype(jnp.float32),
        lax.psum_scatter(
            grad_key_w.astype(jnp.bfloat16), "sp", scatter_dimension=0, tiled=True
        ).astype(jnp.float32),
        lax.psum_scatter(
            grad_value_w.astype(jnp.bfloat16), "sp", scatter_dimension=0, tiled=True
        ).astype(jnp.float32),
        lax.psum_scatter(
            grad_out_w.astype(jnp.bfloat16), "sp", scatter_dimension=0, tiled=True
        ).astype(jnp.float32),
        lax.psum_scatter(
            grad_gate_w.astype(jnp.bfloat16), "sp", scatter_dimension=0, tiled=True
        ).astype(jnp.float32),
        lax.psum_scatter(
            grad_up_w.astype(jnp.bfloat16), "sp", scatter_dimension=0, tiled=True
        ).astype(jnp.float32),
        lax.psum_scatter(
            grad_down.astype(jnp.bfloat16), "sp", scatter_dimension=0, tiled=True
        ).astype(jnp.float32),
        lax.psum_scatter(
            grad_text_key.astype(jnp.bfloat16), "sp", scatter_dimension=0, tiled=True
        ).astype(jnp.float32),
        lax.psum_scatter(
            grad_text_value.astype(jnp.bfloat16), "sp", scatter_dimension=0, tiled=True
        ).astype(jnp.float32),
    )
    totals = (
        lax.psum(home[0].astype(jnp.bfloat16), "dp").astype(jnp.float32),
        lax.psum(home[1].astype(jnp.bfloat16), "dp").astype(jnp.float32),
        lax.psum(home[2].astype(jnp.bfloat16), "dp").astype(jnp.float32),
        lax.psum(home[3].astype(jnp.bfloat16), "dp").astype(jnp.float32),
        lax.psum(home[4].astype(jnp.bfloat16), "dp").astype(jnp.float32),
        lax.psum(home[5].astype(jnp.bfloat16), "dp").astype(jnp.float32),
        lax.psum(home[6].astype(jnp.bfloat16), "dp").astype(jnp.float32),
        lax.psum(home[7].astype(jnp.bfloat16), "dp").astype(jnp.float32),
        lax.psum(home[8].astype(jnp.bfloat16), "dp").astype(jnp.float32),
        lax.psum(grad_ada.astype(jnp.bfloat16), "dp").astype(jnp.float32),
        lax.psum(grad_bias.astype(jnp.bfloat16), "dp").astype(jnp.float32),
        lax.psum(gate_sum.astype(jnp.bfloat16), "dp").astype(jnp.float32),
    )
    (
        d_query,
        d_key,
        d_value,
        d_out,
        d_gate_w,
        d_up_w,
        d_down_w,
        d_text_key,
        d_text_value,
        d_ada,
        d_bias,
        d_gate_cross,
    ) = totals
    return (
        result[None],
        inputs_grad[None],
        caption_grad[None],
        cond_grad[None],
        d_ada,
        d_bias,
        d_query,
        d_key,
        d_value,
        d_out,
        d_gate_cross,
        d_text_key,
        d_text_value,
        d_gate_w,
        d_up_w,
        d_down_w,
    )


MIN_CLIP = 1024
N_DP = 4
OFFSETS = (0, 2, 1, 3)
VMEM_BYTES = 48 * 1024 * 1024
NT = (((1,), (1,)), ((), ()))
TN = (((0,), (0,)), ((), ()))
F32 = jnp.float32
BF16 = jnp.bfloat16


def dot(left, right, dims=(((1,), (0,)), ((), ()))):
    return lax.dot_general(left, right, dims, preferred_element_type=F32)


def ordered(tree):
    arrays, shape = jax.tree.flatten(tree)
    spec = pl.BlockSpec(memory_space=pl.ANY)
    out = pl.pallas_call(
        lambda *refs: None,
        in_specs=[spec] * len(arrays),
        out_specs=[spec] * len(arrays),
        out_shape=[jax.ShapeDtypeStruct(a.shape, a.dtype) for a in arrays],
        input_output_aliases={i: i for i in range(len(arrays))},
        cost_estimate=pl.CostEstimate(flops=0, bytes_accessed=0, transcendentals=0),
    )(*arrays)
    return jax.tree.unflatten(shape, out)


class Ring:
    def __init__(self, size):
        self.size = size
        self.far = size // 2
        self.order = list(range(0, size, 2)) + list(range(size - 1, 0, -2))
        self.up = [(self.order[i], self.order[(i + 1) % size]) for i in range(size)]
        self.down = [(b, a) for a, b in self.up]
        shifts = [0]
        for step in range(1, self.far):
            shifts += [-step, step]
        shifts += [self.far]
        self.spots = {shift: i for i, shift in enumerate(shifts)}
        rows = [None] * size
        for spot, device in enumerate(self.order):
            devices = [self.order[(spot + shift) % size] for shift in shifts]
            rows[device] = [devices + [m ^ offset for offset in OFFSETS] for m in range(N_DP)]
        table = jnp.array(rows, jnp.int32).reshape(size * N_DP, -1)
        index = lax.axis_index("sp") * N_DP + lax.axis_index("dp")
        self.table = lax.dynamic_index_in_dim(table, index, 0, False)

    def send_up(self, values):
        return [lax.ppermute(v, "sp", self.up) for v in values]

    def send_down(self, values):
        return [lax.ppermute(v, "sp", self.down) for v in values]


class Gather:
    def __init__(self, ring, own):
        self.ring, self.own = ring, own
        self.step, self.live = 0, (own, own)
        self.blocks = [(0, own)]

    def send(self):
        ring = self.ring
        self.step += 1
        above, below = self.live
        if self.step == ring.far:
            above = [v[: v.shape[0] // 2] for v in above]
            below = [v[v.shape[0] // 2 :] for v in below]
        self.live = ring.send_up(above), ring.send_down(below)

    def keep(self):
        above, below = self.live
        if self.step == self.ring.far:
            self.halves = above, below
        else:
            self.blocks += [(-self.step, above), (self.step, below)]


def across(value, bit):
    return lax.ppermute(value, "dp", [(i, i ^ bit) for i in range(N_DP)])


def gather_packs(value):
    far = across(value, 2)
    return [value, far, across(value, 1), across(far, 1)]


def sum_packs_near(parts):
    own = parts[0].astype(F32) + across(parts[2].astype(BF16), 1).astype(F32)
    far = parts[1].astype(F32) + across(parts[3].astype(BF16), 1).astype(F32)
    return own, far.astype(BF16)


def gather_small(value, axis_name):
    size = lax.axis_size(axis_name)
    return lax.all_to_all(
        jnp.broadcast_to(value[None], (size,) + value.shape), axis_name, 0, 0, tiled=True
    )


def exchange(value):
    return lax.all_to_all(value, "sp", 0, 0, tiled=True)


def aligned(index, by):
    return index if isinstance(index, int) else pl.multiple_of(index, by)


def place(ring, write, blocks, shapes):
    first = ring.size
    listed = isinstance(blocks, list)
    arrays = blocks if listed else [blocks]

    def kernel(index_ref, *refs):
        for i in range(N_DP):
            if listed:
                write(refs[i], index_ref[first + i], refs[N_DP:])
            else:
                write(refs[0].at[i], i, refs[1:])

    vmem = pl.BlockSpec(memory_space=pltpu.VMEM)
    return pl.pallas_call(
        kernel,
        in_specs=[pl.BlockSpec(memory_space=pltpu.SMEM)] + [vmem] * len(arrays),
        out_specs=[vmem] * len(shapes),
        out_shape=shapes,
        compiler_params=pltpu.CompilerParams(vmem_limit_bytes=VMEM_BYTES),
        cost_estimate=pl.CostEstimate(
            flops=0,
            bytes_accessed=sum(s.size * s.dtype.itemsize for s in [*arrays, *shapes]),
            transcendentals=0,
        ),
    )(ring.table, *arrays)


def place_units(block_ref, index, out_refs):
    columns = block_ref.shape[1] - FOLD
    groups = columns // (2 * 128)
    for i, out_ref in enumerate(out_refs[:2]):
        for group in range(groups):
            start = unit_column(i, group)
            spot = pl.ds(aligned((group * N_DP + index) * 128, 128), 128)
            out_ref[:, spot] = block_ref[:, start : start + 128].astype(out_ref.dtype)
    for row, column, there_row, there_column, height, wide in folded():
        spot = pl.ds(aligned(index * 128 + row, 64), height)
        out_refs[2][spot, column : column + wide] = block_ref[
            there_row : there_row + height,
            columns + there_column : columns + there_column + wide,
        ].astype(out_refs[2].dtype)


def place_heads(block_ref, index, out_refs):
    groups, rows, width = block_ref.shape
    width = width // len(out_refs)
    spot = pl.ds(aligned(index * rows, rows), rows)
    for i, out_ref in enumerate(out_refs):
        for group in range(0, groups, 2):
            pair = [
                block_ref[group + k, :, i * width : (i + 1) * width].astype(F32) for k in range(2)
            ]
            columns = slice(group * width, (group + 2) * width)
            out_ref[spot, columns] = jnp.concatenate(pair, axis=1).astype(out_ref.dtype)


def join_projections(ring, blocks):
    size, part, columns = blocks[0].shape
    width = size * part * N_DP

    def kernel(index_ref, *refs):
        out_ref, turned_ref = refs[N_DP:]
        for i in range(N_DP):
            for device in range(size):
                start = (device * N_DP + index_ref[size + i]) * part
                out_ref[pl.ds(aligned(start, part), part), :] = refs[i][device]
        turned_ref[...] = jnp.transpose(out_ref[...])

    vmem = pl.BlockSpec(memory_space=pltpu.VMEM)
    return pl.pallas_call(
        kernel,
        in_specs=[pl.BlockSpec(memory_space=pltpu.SMEM)] + [vmem] * N_DP,
        out_specs=[vmem] * 2,
        out_shape=[
            jax.ShapeDtypeStruct((width, columns), BF16),
            jax.ShapeDtypeStruct((columns, width), BF16),
        ],
        compiler_params=pltpu.CompilerParams(vmem_limit_bytes=VMEM_BYTES),
        cost_estimate=pl.CostEstimate(
            flops=0, bytes_accessed=6 * width * columns, transcendentals=0
        ),
    )(ring.table, *blocks)


def caption_terms(w_key, w_value, captions):
    features, width = w_key.shape
    tokens = captions.shape[0]
    size = lax.axis_size("sp")
    columns = width // size

    def kernel(key_ref, value_ref, cap_ref, out_ref):
        for i, ref in enumerate((key_ref, value_ref)):
            total = jnp.transpose(dot(cap_ref[...], ref[...])).astype(BF16)
            for device in range(size):
                out_ref[device, :, i * tokens : (i + 1) * tokens] = total[
                    device * columns : (device + 1) * columns
                ]

    vmem = pl.BlockSpec(memory_space=pltpu.VMEM)
    return pl.pallas_call(
        kernel,
        in_specs=[vmem] * 3,
        out_specs=vmem,
        out_shape=jax.ShapeDtypeStruct((size, columns, 2 * tokens), BF16),
        compiler_params=pltpu.CompilerParams(vmem_limit_bytes=VMEM_BYTES),
        cost_estimate=pl.CostEstimate(
            flops=4 * tokens * features * width,
            bytes_accessed=4 * (features + tokens) * width,
            transcendentals=0,
        ),
    )(w_key, w_value, captions)


def text_grads(ring, captions, grads):
    width, columns = grads[0].shape
    tokens = columns // 2
    features = captions.shape[1]
    size = ring.size

    def kernel(index_ref, cap_ref, *refs):
        caps = [
            jnp.transpose(cap_ref[pl.ds(aligned(index_ref[size + i] * tokens, tokens), tokens), :])
            for i in range(N_DP)
        ]
        for which, out_ref in enumerate(refs[N_DP:]):
            total = None
            for i in range(N_DP):
                grad = refs[i][:, which * tokens : (which + 1) * tokens]
                term = dot(caps[i], jnp.transpose(grad))
                total = term if total is None else total + term
            out_ref[...] = total

    vmem = pl.BlockSpec(memory_space=pltpu.VMEM)
    return pl.pallas_call(
        kernel,
        in_specs=[pl.BlockSpec(memory_space=pltpu.SMEM)] + [vmem] * (1 + N_DP),
        out_specs=[vmem] * 2,
        out_shape=[jax.ShapeDtypeStruct((features, width), F32)] * 2,
        compiler_params=pltpu.CompilerParams(vmem_limit_bytes=VMEM_BYTES),
        cost_estimate=pl.CostEstimate(
            flops=4 * N_DP * tokens * features * width,
            bytes_accessed=8 * features * width + 4 * N_DP * tokens * width,
            transcendentals=0,
        ),
    )(ring.table, captions, *grads)


def out_terms(mixed, grad):
    width, rows = mixed.shape
    columns = width // N_DP

    def kernel(mixed_ref, grad_ref, out_ref):
        out_ref[0] = dot(mixed_ref[...], grad_ref[...]).astype(BF16)

    return pl.pallas_call(
        kernel,
        grid=(N_DP,),
        in_specs=[
            pl.BlockSpec((width, rows), lambda i: (0, 0)),
            pl.BlockSpec((rows, columns), lambda i: (0, i)),
        ],
        out_specs=pl.BlockSpec((1, width, columns), lambda i: (i, 0, 0)),
        out_shape=jax.ShapeDtypeStruct((N_DP, width, columns), BF16),
        compiler_params=pltpu.CompilerParams(vmem_limit_bytes=VMEM_BYTES),
        cost_estimate=pl.CostEstimate(
            flops=2 * width * width * rows, bytes_accessed=2 * width * width, transcendentals=0
        ),
    )(mixed, grad)


def finish_tokens(terms, received, middle_grad, tokens, scale):
    rows, width = tokens.shape
    half = rows // CLIPS
    last = terms.shape[0] // rows - 1

    def kernel(terms_ref, above_ref, below_ref, middle_ref, x_ref, scale_ref, out_ref, sums_ref):
        for clip in range(CLIPS):
            span = slice(clip * half, (clip + 1) * half)
            grad = (
                terms_ref[span].astype(F32) + above_ref[span].astype(F32) + below_ref[span].astype(F32)
            )
            x = x_ref[span].astype(F32)
            inverse = lax.rsqrt(jnp.mean(x * x, axis=-1, keepdims=True) + EPSILON)
            normed = x * inverse
            scaled = grad * (1.0 + scale_ref[clip : clip + 1, :])
            mean = jnp.mean(scaled * normed, axis=-1, keepdims=True)
            out_ref[span] = middle_ref[span] + inverse * (scaled - normed * mean)
            sums_ref[clip : clip + 1, :width] = jnp.sum(grad, axis=0, keepdims=True)
            sums_ref[clip : clip + 1, width:] = jnp.sum(grad * normed, axis=0, keepdims=True)

    fixed = pl.BlockSpec((rows, width), lambda i: (0, 0))
    return pl.pallas_call(
        kernel,
        grid=(1,),
        in_specs=[pl.BlockSpec((rows, width), lambda i: (last, 0))]
        + [fixed] * 4
        + [pl.BlockSpec((CLIPS, width), lambda i: (0, 0))],
        out_specs=[fixed, pl.BlockSpec((CLIPS, 2 * width), lambda i: (0, 0))],
        out_shape=[
            jax.ShapeDtypeStruct((rows, width), F32),
            jax.ShapeDtypeStruct((CLIPS, 2 * width), F32),
        ],
        compiler_params=pltpu.CompilerParams(vmem_limit_bytes=VMEM_BYTES),
        cost_estimate=pl.CostEstimate(
            flops=0, bytes_accessed=16 * rows * width, transcendentals=0
        ),
    )(terms, *received, middle_grad, tokens, scale)


def place_columns(block_ref, index, out_refs):
    width = block_ref.shape[1]
    out_refs[0][:, pl.ds(aligned(index * width, 128), width)] = block_ref[...].astype(
        out_refs[0].dtype
    )


UNITS = 512


HELD = 32


def pack_tokens(tokens, w_out):
    rows, width = tokens.shape
    half = rows // 2
    columns = width // N_DP
    k_rows = w_out.shape[0]
    part = k_rows // N_DP
    member = jnp.reshape(lax.axis_index("dp"), (1,)).astype(jnp.int32)

    def kernel(member_ref, tokens_ref, w_ref, out_ref):
        spot = pl.ds(aligned(member_ref[0] * columns, 128), columns)
        for clip in range(CLIPS):
            start = clip * (half + HELD)
            out_ref[start : start + half] = tokens_ref[clip * half : (clip + 1) * half]
            count = min(part - clip * HELD, HELD)
            for group in range(N_DP):
                top = group * part + clip * HELD
                out_ref[
                    start + half : start + half + count, group * columns : (group + 1) * columns
                ] = w_ref[top : top + count, spot]
            if count < HELD:
                out_ref[start + half + count : start + half + HELD] = jnp.zeros(
                    (HELD - count, width), BF16
                )

    vmem = pl.BlockSpec(memory_space=pltpu.VMEM)
    return pl.pallas_call(
        kernel,
        in_specs=[pl.BlockSpec(memory_space=pltpu.SMEM), vmem, vmem],
        out_specs=vmem,
        out_shape=jax.ShapeDtypeStruct((rows + CLIPS * HELD, width), BF16),
        compiler_params=pltpu.CompilerParams(vmem_limit_bytes=VMEM_BYTES),
        cost_estimate=pl.CostEstimate(
            flops=0, bytes_accessed=6 * rows * width, transcendentals=0
        ),
    )(member, tokens, w_out)


def unpack_w_out(ring, flow, half):
    width = flow.own[0].shape[1]
    columns = width // N_DP
    k_rows = width // ring.size
    part = k_rows // N_DP
    block = (half + HELD) // HELD
    groups = [[arrays[0]] for _, arrays in flow.blocks]
    groups += [[flow.halves[0][0], flow.halves[1][0]]]
    spots = [ring.spots[shift] for shift, _ in flow.blocks] + [ring.spots[ring.far]]
    operands, specs = [], []
    for group in groups:
        for clip in range(CLIPS):
            operands.append(group[clip] if len(group) > 1 else group[0])
            index = block - 1 if len(group) > 1 else (clip + 1) * block - 1
            specs.append(pl.BlockSpec((HELD, width), lambda i, index=index: (index, 0)))

    def kernel(index_ref, *refs):
        for i, spot in enumerate(spots):
            for clip in range(CLIPS):
                count = min(part - clip * HELD, HELD)
                for group in range(N_DP):
                    top = index_ref[spot] * k_rows + group * part + clip * HELD
                    refs[-1][pl.ds(aligned(top, 16), count), :] = refs[CLIPS * i + clip][
                        :count, group * columns : (group + 1) * columns
                    ]

    return pl.pallas_call(
        kernel,
        grid=(1,),
        in_specs=[pl.BlockSpec(memory_space=pltpu.SMEM)] + specs,
        out_specs=pl.BlockSpec((width, columns), lambda i: (0, 0)),
        out_shape=jax.ShapeDtypeStruct((width, columns), BF16),
        compiler_params=pltpu.CompilerParams(vmem_limit_bytes=VMEM_BYTES),
        cost_estimate=pl.CostEstimate(
            flops=0, bytes_accessed=4 * width * columns, transcendentals=0
        ),
    )(ring.table, *operands)


def unit_pieces(w_gate, w_up, w_down, after):
    rows, columns = w_gate.shape
    groups = columns // (N_DP * 128)
    member = jnp.reshape(lax.axis_index("dp"), (1,)).astype(jnp.int32)
    first = 2 * groups * 128
    width = first + FOLD

    def kernel(member_ref, gate_ref, up_ref, down_ref, after_ref, out_ref):
        for i, ref in enumerate((gate_ref, up_ref)):
            for group in range(groups):
                spot = aligned((group * N_DP + member_ref[0]) * 128, 128)
                start = unit_column(i, group)
                out_ref[:, start : start + 128] = ref[:, pl.ds(spot, 128)]
        spot = aligned(member_ref[0] * 128, 128)
        for row, column, there_row, there_column, height, wide in folded():
            out_ref[there_row : there_row + height, first + there_column : first + there_column + wide] = (
                down_ref[pl.ds(aligned(spot + row, 32), height), column : column + wide]
            )

    vmem = pl.BlockSpec(memory_space=pltpu.VMEM)
    return pl.pallas_call(
        kernel,
        in_specs=[pl.BlockSpec(memory_space=pltpu.SMEM), vmem, vmem, vmem, pl.BlockSpec(memory_space=pl.ANY)],
        out_specs=vmem,
        out_shape=jax.ShapeDtypeStruct((rows, width), w_gate.dtype),
        compiler_params=pltpu.CompilerParams(vmem_limit_bytes=VMEM_BYTES),
        cost_estimate=pl.CostEstimate(
            flops=0, bytes_accessed=8 * rows * columns, transcendentals=0
        ),
    )(member, w_gate, w_up, w_down, after)


FOLD = 1024


def folded(low=0, high=192):
    spots = []
    if low < 128:
        end = min(high, 128)
        spots.append((low, 0, 0, 0, end - low, FOLD))
    if high > 128:
        start = max(low, 128) - 128
        count = high - 128 - start
        for side in range(2):
            spots.append(
                (64 * side + start, FOLD, 128 + start - low, 512 * side, count, 512)
            )
    return spots


def unit_column(which, group):
    per_tile = UNITS // 128
    tile, rest = divmod(group, per_tile)
    return tile * 2 * UNITS + which * UNITS + rest * 128


def pack_first(w_query, w_key, w_value, captions, modulation):
    k_rows, width = w_query.shape
    size = width // k_rows
    part = k_rows // N_DP
    tokens, features = captions.shape
    columns = 3 * k_rows
    clips, own_mod = modulation.shape
    pieces = own_mod // columns
    mod_rows = 2 * clips * pieces
    member = jnp.reshape(lax.axis_index("dp"), (1,)).astype(jnp.int32)
    rows = part + tokens + 16

    def kernel(member_ref, q_ref, k_ref, v_ref, cap_ref, mod_ref, out_ref):
        spot = pl.ds(aligned(member_ref[0] * part, part), part)
        mod = jnp.concatenate(
            [mod_ref[:, i * columns : (i + 1) * columns] for i in range(pieces)], axis=0
        )
        high = mod.astype(BF16).astype(F32)
        fill = jnp.zeros((16 - mod_rows, columns), F32)
        mod = jnp.concatenate([high, mod - high, fill], axis=0).astype(BF16)
        each = features // size
        fill = jnp.zeros((tokens, columns - each), BF16)
        for device in range(size):
            own = slice(device * k_rows, (device + 1) * k_rows)
            row = [ref[spot, own].astype(F32) for ref in (q_ref, k_ref, v_ref)]
            out_ref[device, :part] = jnp.concatenate(row, axis=1).astype(BF16)
            cap = cap_ref[:, device * each : (device + 1) * each]
            out_ref[device, part : part + tokens] = jnp.concatenate([cap, fill], axis=1)
            out_ref[device, part + tokens :] = mod

    vmem = pl.BlockSpec(memory_space=pltpu.VMEM)
    return pl.pallas_call(
        kernel,
        in_specs=[pl.BlockSpec(memory_space=pltpu.SMEM)] + [vmem] * 5,
        out_specs=vmem,
        out_shape=jax.ShapeDtypeStruct((size, rows, columns), BF16),
        compiler_params=pltpu.CompilerParams(vmem_limit_bytes=VMEM_BYTES),
        cost_estimate=pl.CostEstimate(
            flops=0, bytes_accessed=8 * size * rows * columns, transcendentals=0
        ),
    )(member, w_query, w_key, w_value, captions, modulation)


def unpack_first(packed, part, tokens, features, clips, own_mod):
    size, _, columns = packed.shape
    pieces = own_mod // columns
    each = tokens // clips

    def kernel(in_ref, quarter_ref, cap_ref, mod_ref):
        for device in range(size):
            quarter_ref[device] = in_ref[device, :part]
            for clip in range(clips):
                start = part + clip * each
                cap_ref[clip, device * each : (device + 1) * each] = in_ref[
                    device, start : start + each, :features
                ]
            mod = in_ref[device, part + tokens :].astype(F32)
            count = clips * pieces
            mod = mod[:count] + mod[count : 2 * count]
            mod = [mod[i * clips : (i + 1) * clips] for i in range(pieces)]
            mod_ref[:, device * own_mod : (device + 1) * own_mod] = jnp.concatenate(mod, axis=1)

    vmem = pl.BlockSpec(memory_space=pltpu.VMEM)
    return pl.pallas_call(
        kernel,
        in_specs=[vmem],
        out_specs=[vmem] * 3,
        out_shape=[
            jax.ShapeDtypeStruct((size, part, columns), BF16),
            jax.ShapeDtypeStruct((clips, size * each, features), BF16),
            jax.ShapeDtypeStruct((clips, size * own_mod), F32),
        ],
        compiler_params=pltpu.CompilerParams(vmem_limit_bytes=VMEM_BYTES),
        cost_estimate=pl.CostEstimate(
            flops=0, bytes_accessed=4 * packed.size, transcendentals=0
        ),
    )(packed)


def feed_kernel(ids_ref, *refs, size, places):
    count = len(places)
    x_refs, grad_ref = refs[:N_DP], refs[N_DP]
    piece_refs = refs[N_DP + 1 : N_DP + 1 + count]
    hidden_ref, grads_ref, near_ref, far_ref = refs[N_DP + 1 + count : N_DP + 5 + count]
    down_out, x_out = refs[N_DP + 5 + count : N_DP + 7 + count]
    x_all, grad_all, w_all, down_all, total, sems, out_sems = refs[N_DP + 7 + count :]
    rows = x_refs[0].shape[0]
    columns = w_all.shape[1]
    tile = pl.program_id(0)
    last = pl.num_programs(0) - 1

    def spot(i):
        return pl.ds(aligned(ids_ref[size + i] * rows, rows), rows)

    def copies(first, end=None):
        pairs = []
        for i in range(N_DP):
            pairs.append((x_refs[i], x_all.at[spot(i)]))
        for i, (place_, start, height) in enumerate(places):
            top = aligned(ids_ref[place_] * 192 + start, 32)
            pairs.append((piece_refs[i].at[:, pl.ds(0, columns)], w_all.at[pl.ds(top, height)]))
        pairs.append((grad_ref, grad_all))
        for i, (place_, start, height) in enumerate(places):
            for row, column, there_row, there_column, high, wide in folded(start, start + height):
                top = aligned(ids_ref[place_] * 128 + row, 32)
                pairs.append(
                    (
                        piece_refs[i].at[
                            pl.ds(there_row, high), pl.ds(columns + there_column, wide)
                        ],
                        down_all.at[pl.ds(top, high), pl.ds(column, wide)],
                    )
                )
        numbered = list(enumerate(pairs))[first:end]
        return [pltpu.make_async_copy(a, b, sems.at[i]) for i, (a, b) in numbered]

    def keep(i):
        source, there = ((x_all, x_out), (down_all, down_out))[i]
        return pltpu.make_async_copy(source, there, out_sems.at[i])

    early = N_DP + count

    @pl.when(tile == 0)
    def _():
        for copy in copies(0):
            copy.start()
        for copy in copies(0, early):
            copy.wait()
        keep(0).start()

    weight = w_all[:, pl.ds(aligned(tile * 2 * UNITS, 2 * UNITS), 2 * UNITS)]
    both = dot(x_all[...], weight)
    gate, up = both[:, :UNITS], both[:, UNITS:]

    @pl.when(tile == 0)
    def _():
        for copy in copies(early):
            copy.wait()
        keep(1).start()

    down = down_all[pl.ds(aligned(tile * UNITS, UNITS), UNITS), :]
    hidden_grad = dot(grad_all[...], down, NT)
    sigmoid = jax.nn.sigmoid(gate)
    silu = gate * sigmoid
    hidden_ref[...] = (silu * up).astype(BF16)
    gate_grad = hidden_grad * up * sigmoid * (1.0 + gate * (1.0 - sigmoid))
    grads = jnp.concatenate([gate_grad.astype(BF16), (hidden_grad * silu).astype(BF16)], axis=1)
    grads_ref[...] = grads
    term = dot(grads, weight, NT)

    @pl.when(tile == 0)
    def _():
        total[...] = term

    @pl.when(tile > 0)
    def _():
        total[...] += term

    @pl.when(tile == last)
    def _():
        for i, out_ref in enumerate((near_ref, far_ref)):
            out_ref[:rows] = total[spot(i), :].astype(BF16)
            out_ref[rows:] = total[spot(2 + i), :].astype(BF16)
        keep(0).wait()
        keep(1).wait()


def feed(ring, xs, grads, pieces):
    rows, width = xs[0].shape
    units = (pieces[0][2].shape[1] - FOLD) // 2
    places = tuple((ring.spots[shift], start, piece.shape[0]) for shift, start, piece in pieces)
    copies = N_DP + 1 + len(pieces)
    copies += sum(len(folded(start, start + height)) for _, start, height in places)
    anywhere = pl.BlockSpec(memory_space=pl.ANY)
    return pl.pallas_call(
        functools.partial(feed_kernel, size=ring.size, places=places),
        grid_spec=pltpu.PrefetchScalarGridSpec(
            num_scalar_prefetch=1,
            grid=(units // UNITS,),
            in_specs=[anywhere] * (N_DP + 1 + len(pieces)),
            out_specs=[
                pl.BlockSpec((N_DP * rows, UNITS), lambda t, ids: (0, t)),
                pl.BlockSpec((N_DP * rows, 2 * UNITS), lambda t, ids: (0, t)),
                pl.BlockSpec((2 * rows, width), lambda t, ids: (0, 0)),
                pl.BlockSpec((2 * rows, width), lambda t, ids: (0, 0)),
                anywhere,
                anywhere,
            ],
            scratch_shapes=[
                pltpu.VMEM((N_DP * rows, width), BF16),
                pltpu.VMEM((N_DP * rows, width), BF16),
                pltpu.VMEM((width, 2 * units), BF16),
                pltpu.VMEM((units, width), BF16),
                pltpu.VMEM((N_DP * rows, width), F32),
                pltpu.SemaphoreType.DMA((copies,)),
                pltpu.SemaphoreType.DMA((2,)),
            ],
        ),
        out_shape=[
            jax.ShapeDtypeStruct((N_DP * rows, units), BF16),
            jax.ShapeDtypeStruct((N_DP * rows, 2 * units), BF16),
            jax.ShapeDtypeStruct((2 * rows, width), BF16),
            jax.ShapeDtypeStruct((2 * rows, width), BF16),
            jax.ShapeDtypeStruct((units, width), BF16),
            jax.ShapeDtypeStruct((N_DP * rows, width), BF16),
        ],
        compiler_params=pltpu.CompilerParams(vmem_limit_bytes=VMEM_BYTES),
        cost_estimate=pl.CostEstimate(
            flops=10 * N_DP * rows * width * units,
            bytes_accessed=24 * N_DP * rows * width,
            transcendentals=N_DP * rows * units,
        ),
    )(ring.table, *xs, grads, *[piece for _, _, piece in pieces])


def add_units(table, spots, d_weight, d_down, received, shape):
    units, width = d_down.shape
    columns = d_weight.shape[1]
    rows = width // lax.axis_size("sp")
    half = rows // 2
    sides = 1 if shape == "home" else 2
    heights = [rows] * 2 if shape == "whole" else [half] * 2

    def kernel(ids_ref, *refs):
        own, arrived = refs[: 2 * sides], refs[2 * sides : 2 * sides + len(received)]
        out, whole = refs[2 * sides + len(received) : -1], refs[-1]
        for side in range(sides):
            whole[:, :columns] = own[2 * side][...].astype(F32)
            for row, column, there_row, there_column, height, wide in folded(0, rows):
                whole[
                    there_row : there_row + height,
                    columns + there_column : columns + there_column + wide,
                ] = own[2 * side + 1][row : row + height, column : column + wide].astype(F32)
            if shape == "home":
                value = whole[...] + arrived[0][...].astype(F32) + arrived[1][...].astype(F32)
                out[0][...] = value.astype(BF16)
            elif shape == "halves":
                out[side][...] = whole[side * half : (side + 1) * half].astype(BF16)
            else:
                count = arrived[side].shape[0]
                start = side * half if count < rows else 0
                span = slice(start, start + count)
                whole[span] += arrived[side][...].astype(F32)
                out[side][...] = whole[...].astype(BF16)

    own_specs = []
    for side in range(sides):
        own_specs += [
            pl.BlockSpec((rows, columns), lambda i, ids, side=side: (ids[spots[side]], 0)),
            pl.BlockSpec((128, width), lambda i, ids, side=side: (ids[spots[side]], 0)),
        ]
    whole_spec = lambda height: pl.BlockSpec((height, columns + FOLD), lambda i, ids: (0, 0))
    outs = [rows] if shape == "home" else heights
    return pl.pallas_call(
        kernel,
        grid_spec=pltpu.PrefetchScalarGridSpec(
            num_scalar_prefetch=1,
            grid=(1,),
            in_specs=own_specs + [whole_spec(a.shape[0]) for a in received],
            out_specs=[whole_spec(height) for height in outs],
            scratch_shapes=[pltpu.VMEM((rows, columns + FOLD), F32)],
        ),
        out_shape=[jax.ShapeDtypeStruct((height, columns + FOLD), BF16) for height in outs],
        compiler_params=pltpu.CompilerParams(vmem_limit_bytes=VMEM_BYTES),
        cost_estimate=pl.CostEstimate(
            flops=0, bytes_accessed=12 * rows * (columns + FOLD), transcendentals=0
        ),
    )(table, *([d_weight, d_down] * sides), *received)


def feed_back_kernel(
    x_ref, grad_ref, hidden_ref, grads_ref, down_ref, d_w_ref, d_down_ref, out_ref, x_turned, total
):
    tile = pl.program_id(0)

    @pl.when(tile == 0)
    def _():
        x_turned[...] = jnp.transpose(x_ref[...])

    d_w_ref[...] = dot(x_turned[...], grads_ref[...]).astype(BF16)
    d_down_ref[...] = dot(hidden_ref[...], grad_ref[...], TN).astype(BF16)
    term = dot(hidden_ref[...], down_ref[...])

    @pl.when(tile == 0)
    def _():
        total[...] = term

    @pl.when(tile > 0)
    def _():
        total[...] += term

    @pl.when(tile == pl.num_programs(0) - 1)
    def _():
        out_ref[...] = total[...].astype(BF16)


def feed_back(xs, grads, hidden, unit_grads, down):
    rows, width = xs.shape
    units = down.shape[0]
    fixed = pl.BlockSpec((rows, width), lambda t: (0, 0))
    return pl.pallas_call(
        feed_back_kernel,
        grid=(units // UNITS,),
        in_specs=[
            fixed,
            fixed,
            pl.BlockSpec((rows, UNITS), lambda t: (0, t)),
            pl.BlockSpec((rows, 2 * UNITS), lambda t: (0, t)),
            pl.BlockSpec((UNITS, width), lambda t: (t, 0)),
        ],
        out_specs=[
            pl.BlockSpec((width, 2 * UNITS), lambda t: (0, t)),
            pl.BlockSpec((UNITS, width), lambda t: (t, 0)),
            fixed,
        ],
        out_shape=[
            jax.ShapeDtypeStruct((width, 2 * units), BF16),
            jax.ShapeDtypeStruct((units, width), BF16),
            jax.ShapeDtypeStruct((rows, width), BF16),
        ],
        scratch_shapes=[pltpu.VMEM((width, rows), BF16), pltpu.VMEM((rows, width), F32)],
        compiler_params=pltpu.CompilerParams(vmem_limit_bytes=VMEM_BYTES),
        cost_estimate=pl.CostEstimate(
            flops=8 * rows * width * units, bytes_accessed=24 * rows * width, transcendentals=0
        ),
    )(xs, grads, hidden, unit_grads, down)


def token_terms(table, first, count, grads, weight, apart):
    clips, columns, length = grads.shape
    width = weight.shape[1]
    half = length // lax.axis_size("sp")

    def kernel(ids_ref, grads_ref, w_ref, *out_refs):
        for clip in range(clips):
            value = dot(jnp.transpose(grads_ref[clip]), w_ref[...]).astype(BF16)
            if apart:
                out_refs[clip][...] = value
            else:
                out_refs[0][clip * half : (clip + 1) * half] = value

    outs, rows = (clips, half) if apart else (1, clips * half)
    return pl.pallas_call(
        kernel,
        grid_spec=pltpu.PrefetchScalarGridSpec(
            num_scalar_prefetch=1,
            grid=(count,),
            in_specs=[
                pl.BlockSpec((clips, columns, half), lambda i, ids: (0, 0, ids[first - i])),
                pl.BlockSpec((columns, width), lambda i, ids: (0, 0)),
            ],
            out_specs=[pl.BlockSpec((rows, width), lambda i, ids: (i, 0))] * outs,
        ),
        out_shape=[jax.ShapeDtypeStruct((count * rows, width), BF16)] * outs,
        compiler_params=pltpu.CompilerParams(vmem_limit_bytes=VMEM_BYTES),
        cost_estimate=pl.CostEstimate(
            flops=2 * clips * count * half * columns * width,
            bytes_accessed=2 * clips * count * half * (columns + width) + 2 * width * columns,
            transcendentals=0,
        ),
    )(table, grads, weight)


def add_received(index, terms, received):
    width = terms.shape[1]
    rows = terms.shape[0] // (2 * (lax.axis_size("sp") // 2 - 1) + 1)
    half = rows // 2

    def kernel(*refs):
        for side in range(2):
            own, arrived, out = refs[side], refs[2 + side], refs[4 + side]
            value = own[...].astype(F32)
            if arrived.shape[0] == rows:
                out[...] = (value + arrived[...].astype(F32)).astype(BF16)
            else:
                span = slice(side * half, (side + 1) * half)
                rest = slice((1 - side) * half, (2 - side) * half)
                out[span] = (value[span] + arrived[...].astype(F32)).astype(BF16)
                out[rest] = own[rest]

    def spec(height, block=0):
        return pl.BlockSpec((height, width), lambda i: (block, 0))

    return pl.pallas_call(
        kernel,
        grid=(1,),
        in_specs=[spec(rows, index[0]), spec(rows, index[1])]
        + [spec(a.shape[0]) for a in received],
        out_specs=[spec(rows)] * 2,
        out_shape=[jax.ShapeDtypeStruct((rows, width), BF16)] * 2,
        compiler_params=pltpu.CompilerParams(vmem_limit_bytes=VMEM_BYTES),
        cost_estimate=pl.CostEstimate(
            flops=0, bytes_accessed=12 * rows * width, transcendentals=0
        ),
    )(terms, terms, *received)


def head_weight_terms(block_in, grads):
    clips, length, width = block_in.shape
    columns = grads.shape[1]
    size = lax.axis_size("sp")
    k_rows = width // size
    part = k_rows // N_DP
    tile = 2 * k_rows

    def kernel(in_ref, grads_ref, out_ref):
        total = dot(grads_ref[0], in_ref[0])
        for clip in range(1, clips):
            total = total + dot(grads_ref[clip], in_ref[clip])
        turned = jnp.transpose(total).astype(BF16)
        for member in range(N_DP):
            for shard in range(2):
                start = shard * k_rows + member * part
                out_ref[member, shard] = turned[start : start + part]

    return pl.pallas_call(
        kernel,
        grid=(width // tile,),
        in_specs=[
            pl.BlockSpec((clips, length, tile), lambda t: (0, 0, t)),
            pl.BlockSpec((clips, columns, length), lambda t: (0, 0, 0)),
        ],
        out_specs=pl.BlockSpec((N_DP, 2, part, columns), lambda t: (0, t, 0, 0)),
        out_shape=jax.ShapeDtypeStruct((N_DP, size, part, columns), BF16),
        compiler_params=pltpu.CompilerParams(vmem_limit_bytes=VMEM_BYTES),
        cost_estimate=pl.CostEstimate(
            flops=2 * clips * length * width * columns,
            bytes_accessed=2 * clips * length * (width + columns) + 2 * width * columns,
            transcendentals=0,
        ),
    )(block_in, grads)


def turn(values, cos, sin):
    half = HD // 2
    a, b = values[:half], values[half:]
    return jnp.concatenate([a * cos - b * sin, a * sin + b * cos], axis=0)


def turn_back(grads, cos, sin):
    half = HD // 2
    a, b = grads[:half], grads[half:]
    return jnp.concatenate([a * cos + b * sin, b * cos - a * sin], axis=0)


def head_inverse(values):
    return lax.rsqrt(jnp.mean(values * values, axis=0, keepdims=True) + EPSILON)


def project_kernel(place_ref, *refs, sizes):
    count = sum(sizes)
    blocks = refs[:count]
    shift_ref, scale_ref, w_ref, cos_ref, sin_ref = refs[count : count + 5]
    in_ref, out_ref, raw_ref = refs[-3:]
    half = in_ref.shape[1]
    heads = w_ref.shape[1] // (3 * HD)

    def run(x, clip):
        x = x.astype(F32)
        inverse = lax.rsqrt(jnp.mean(x * x, axis=-1, keepdims=True) + EPSILON)
        block = x * inverse * (1.0 + scale_ref[clip : clip + 1, :]) + shift_ref[clip : clip + 1, :]
        block = block.astype(BF16)
        in_ref[clip] = block
        raw = jnp.transpose(dot(block, w_ref[...]))
        raw_ref[clip] = raw[: 2 * heads * HD]
        cos, sin = cos_ref[clip], sin_ref[clip]
        for head in range(2 * heads):
            rows = raw[head * HD : (head + 1) * HD]
            rotated = turn(rows * head_inverse(rows), cos, sin)
            out_ref[clip, head * HD : (head + 1) * HD, :] = rotated.astype(BF16)
        out_ref[clip, 2 * heads * HD :, :] = raw[2 * heads * HD :].astype(BF16)

    first = 0
    for step, size in enumerate(sizes):
        group = blocks[first : first + size]
        first += size

        @pl.when(pl.program_id(0) == step)
        def _(group=group):
            for clip in range(CLIPS):
                if len(group) == 1:
                    start = clip * (half + HELD)
                    run(group[0][start : start + half, :], clip)
                else:
                    run(group[clip][:half], clip)


def project(table, first, groups, shift, scale, weight, cos, sin, before):
    sizes = tuple(len(g) for g in groups)
    blocks = [b for g in groups for b in g]
    width, columns = weight.shape
    length = cos.shape[2]
    half = groups[0][0].shape[0] * len(groups[0]) // CLIPS - HELD
    fixed = lambda a: pl.BlockSpec(a.shape, lambda i, ids: (0,) * a.ndim)
    out_shape = [
        jax.ShapeDtypeStruct((CLIPS, length, width), BF16),
        jax.ShapeDtypeStruct((CLIPS, columns, length), BF16),
        jax.ShapeDtypeStruct((CLIPS, 2 * columns // 3, length), F32),
    ]
    in_specs = [fixed(a) for a in (*blocks, shift, scale, weight)]
    in_specs += [pl.BlockSpec((CLIPS, HD // 2, half), lambda i, ids: (0, 0, ids[first + i]))] * 2
    operands = [*blocks, shift, scale, weight, cos, sin]
    aliases = {}
    if before is not None:
        aliases = {1 + len(operands) + i: i for i in range(3)}
        in_specs += [pl.BlockSpec(memory_space=pl.ANY)] * 3
        operands += before
    rows = CLIPS * half * len(groups)
    return pl.pallas_call(
        functools.partial(project_kernel, sizes=sizes),
        grid_spec=pltpu.PrefetchScalarGridSpec(
            num_scalar_prefetch=1,
            grid=(len(groups),),
            in_specs=in_specs,
            out_specs=[
                pl.BlockSpec((CLIPS, half, width), lambda i, ids: (0, ids[first + i], 0)),
                pl.BlockSpec((CLIPS, columns, half), lambda i, ids: (0, 0, ids[first + i])),
                pl.BlockSpec((CLIPS, 2 * columns // 3, half), lambda i, ids: (0, 0, ids[first + i])),
            ],
        ),
        out_shape=out_shape,
        input_output_aliases=aliases,
        compiler_params=pltpu.CompilerParams(vmem_limit_bytes=VMEM_BYTES),
        cost_estimate=pl.CostEstimate(
            flops=2 * rows * width * columns,
            bytes_accessed=4 * rows * width + 8 * rows * columns + 2 * width * columns,
            transcendentals=0,
        ),
    )(table, *operands)


def cross_probabilities(cap_key, query):
    scores = dot(cap_key, query, TN) * HD**-0.5
    grown = jnp.exp(scores - jnp.max(scores, axis=0, keepdims=True))
    return grown / jnp.sum(grown, axis=0, keepdims=True)


def attend_kernel(
    gate_ref, q_ref, k_ref, v_ref, ck_ref, cv_ref, mixed_ref, self_ref, cross_ref, log_ref, *, block
):
    length = q_ref.shape[2]
    half = mixed_ref.shape[2]
    gate = gate_ref[pl.program_id(1)]
    keys = jnp.transpose(k_ref[0])
    for start in range(0, length, block):
        query = q_ref[0, :, start : start + block]
        grown = jnp.exp(dot(keys, query) * HD**-0.5)
        total = jnp.sum(grown, axis=0, keepdims=True)
        self_out = dot(v_ref[0], grown.astype(BF16)) / total
        probs = cross_probabilities(ck_ref[...], query)
        cross_out = dot(cv_ref[...], probs.astype(BF16))
        self_ref[0, :, start : start + block] = self_out
        cross_ref[0, :, start : start + block] = cross_out
        log_ref[0, 0, :, start : start + block] = jnp.log(total)
        mixed = (self_out + gate * cross_out).astype(BF16)
        for piece in range(block // half):
            mixed_ref[start // half + piece] = mixed[:, piece * half : (piece + 1) * half]


def attend(gate, qkv, cap_key, cap_value, half):
    clips, columns, length = qkv.shape
    heads = columns // (3 * HD)
    head_spec = lambda first: pl.BlockSpec((1, HD, length), lambda c, h: (c, first * heads + h, 0))
    cap_spec = pl.BlockSpec((HD, CAP), lambda c, h: (h, c))
    own_spec = pl.BlockSpec((1, HD, length), lambda c, h: (c, h, 0))
    return pl.pallas_call(
        functools.partial(attend_kernel, block=length),
        grid=(clips, heads),
        in_specs=[
            pl.BlockSpec(memory_space=pltpu.SMEM),
            head_spec(0),
            head_spec(1),
            head_spec(2),
            cap_spec,
            cap_spec,
        ],
        out_specs=[
            pl.BlockSpec((length // half, HD, half), lambda c, h: (0, h, c)),
            own_spec,
            own_spec,
            pl.BlockSpec((1, 1, 1, length), lambda c, h: (c, h, 0, 0)),
        ],
        out_shape=[
            jax.ShapeDtypeStruct((length // half, heads * HD, clips * half), BF16),
            jax.ShapeDtypeStruct((clips, heads * HD, length), F32),
            jax.ShapeDtypeStruct((clips, heads * HD, length), F32),
            jax.ShapeDtypeStruct((clips, heads, 1, length), F32),
        ],
        compiler_params=pltpu.CompilerParams(vmem_limit_bytes=VMEM_BYTES),
        cost_estimate=pl.CostEstimate(
            flops=4 * clips * heads * length * length * HD * 4,
            bytes_accessed=clips * heads * length * HD * 20,
            transcendentals=clips * heads * length * length,
        ),
    )(gate, qkv, qkv, qkv, cap_key, cap_value)


def attend_back_kernel(
    gate_ref,
    q_ref,
    k_ref,
    v_ref,
    ck_ref,
    cv_ref,
    grad_ref,
    self_ref,
    cross_ref,
    log_ref,
    raw_q_ref,
    raw_k_ref,
    cos_ref,
    sin_ref,
    grads_ref,
    cap_ref,
    gate_grad_ref,
    key_acc,
    value_acc,
    *,
    block,
):
    length = q_ref.shape[2]
    half = grad_ref.shape[2]
    score_scale = HD**-0.5
    gate = gate_ref[pl.program_id(1)]
    keys, values = k_ref[0], v_ref[0]
    keys_turned, values_turned = jnp.transpose(keys), jnp.transpose(values)
    cap_key, cap_value = ck_ref[...], cv_ref[...]
    cap_key_grad = jnp.zeros((HD, CAP), F32)
    cap_value_grad = jnp.zeros((HD, CAP), F32)
    for start in range(0, length, block):
        span = slice(start, start + block)
        query = q_ref[0, :, span]
        grad = jnp.concatenate(
            [grad_ref[start // half + piece] for piece in range(block // half)], axis=1
        )
        wide = grad.astype(F32)
        delta = jnp.sum(wide * self_ref[0, :, span], axis=0, keepdims=True)
        gate_grad_ref[0, 0, :, span] = jnp.sum(
            wide * cross_ref[0, :, span], axis=0, keepdims=True
        )
        probs = jnp.exp(dot(keys_turned, query) * score_scale - log_ref[0, 0, :, span])
        score_grad = (probs * (dot(values_turned, grad) - delta)).astype(BF16)
        value_part = jnp.transpose(dot(probs.astype(BF16), jnp.transpose(grad)))
        key_part = jnp.transpose(dot(score_grad, jnp.transpose(query)))
        if start == 0:
            value_acc[...] = value_part
            key_acc[...] = key_part
        else:
            value_acc[...] += value_part
            key_acc[...] += key_part
        query_grad = dot(keys, score_grad)
        cross_grad = (gate * wide).astype(BF16)
        cross_probs = cross_probabilities(cap_key, query)
        cross_dp = dot(cap_value, cross_grad, TN)
        cross_score = cross_probs * (
            cross_dp - jnp.sum(cross_probs * cross_dp, axis=0, keepdims=True)
        )
        cross_score = cross_score.astype(BF16)
        cap_value_grad += dot(cross_grad, cross_probs.astype(BF16), NT)
        cap_key_grad += dot(query, cross_score, NT)
        query_grad = (query_grad + dot(cap_key, cross_score)) * score_scale
        raw = raw_q_ref[0, :, span]
        inverse = head_inverse(raw)
        normed = raw * inverse
        turned = turn_back(query_grad, cos_ref[0, :, span], sin_ref[0, :, span])
        mean = jnp.mean(turned * normed, axis=0, keepdims=True)
        grads_ref[0, 0, :, span] = (inverse * (turned - normed * mean)).astype(BF16)
    for start in range(0, length, block):
        span = slice(start, start + block)
        raw = raw_k_ref[0, :, span]
        inverse = head_inverse(raw)
        normed = raw * inverse
        turned = turn_back(
            key_acc[:, span] * score_scale, cos_ref[0, :, span], sin_ref[0, :, span]
        )
        mean = jnp.mean(turned * normed, axis=0, keepdims=True)
        grads_ref[0, 1, :, span] = (inverse * (turned - normed * mean)).astype(BF16)
        grads_ref[0, 2, :, span] = value_acc[:, span].astype(BF16)
    cap_ref[0] = (cap_key_grad * score_scale).astype(BF16)
    cap_ref[1] = cap_value_grad.astype(BF16)


def attend_back(gate, qkv, cap_key, cap_value, grad, self_out, cross_out, log_total, raw, cos, sin):
    clips, columns, length = qkv.shape
    heads = columns // (3 * HD)
    half = length // grad.shape[0]
    head_spec = lambda first: pl.BlockSpec((1, HD, length), lambda c, h: (c, first * heads + h, 0))
    cap_spec = pl.BlockSpec((HD, CAP), lambda c, h: (h, c))
    table_spec = pl.BlockSpec((1, HD // 2, length), lambda c, h: (c, 0, 0))
    row_spec = pl.BlockSpec((1, 1, 1, length), lambda c, h: (c, h, 0, 0))
    return pl.pallas_call(
        functools.partial(attend_back_kernel, block=length // 2),
        grid=(clips, heads),
        in_specs=[
            pl.BlockSpec(memory_space=pltpu.SMEM),
            head_spec(0),
            head_spec(1),
            head_spec(2),
            cap_spec,
            cap_spec,
            pl.BlockSpec((length // half, HD, half), lambda c, h: (0, h, c)),
            head_spec(0),
            head_spec(0),
            row_spec,
            head_spec(0),
            head_spec(1),
            table_spec,
            table_spec,
        ],
        out_specs=[
            pl.BlockSpec((1, 3, HD, length), lambda c, h: (c, 0, h, 0)),
            pl.BlockSpec((2, HD, CAP), lambda c, h: (0, h, c)),
            row_spec,
        ],
        out_shape=[
            jax.ShapeDtypeStruct((clips, 3, heads * HD, length), BF16),
            jax.ShapeDtypeStruct((2, heads * HD, clips * CAP), BF16),
            jax.ShapeDtypeStruct((clips, heads, 1, length), F32),
        ],
        scratch_shapes=[pltpu.VMEM((HD, length), F32), pltpu.VMEM((HD, length), F32)],
        compiler_params=pltpu.CompilerParams(vmem_limit_bytes=VMEM_BYTES),
        cost_estimate=pl.CostEstimate(
            flops=10 * clips * heads * length * length * HD * 4,
            bytes_accessed=clips * heads * length * HD * 32,
            transcendentals=clips * heads * length * length,
        ),
    )(
        gate,
        qkv,
        qkv,
        qkv,
        cap_key,
        cap_value,
        grad,
        self_out,
        cross_out,
        log_total,
        raw,
        raw,
        cos,
        sin,
    )


def clip_sums(values):
    return jnp.sum(values.reshape(CLIPS, -1, values.shape[-1]), axis=1)


def split_heads(
    tokens,
    cotangent,
    captions,
    conditioning,
    clip_lens,
    w_ada,
    b_ada,
    w_query,
    w_key,
    w_value,
    w_out,
    gate_cross,
    w_text_key,
    w_text_value,
    w_gate,
    w_up,
    w_down,
):
    shard = lax.axis_index("sp")
    member = lax.axis_index("dp")
    size = lax.axis_size("sp")
    ring = Ring(size)
    rows = tokens.shape[1]
    half = rows // 2
    own_cols = D // size
    heads = HEADS // size
    ff = w_gate.shape[1]
    ff_rows = ff // size
    ff_part = ff_rows // N_DP
    k_rows = D // size
    k_part = k_rows // N_DP
    text_rows = w_text_key.shape[0]

    inputs = tokens[0].astype(F32)
    out_grad = cotangent[0].astype(F32)
    hidden_units = ff // N_DP

    def by_row(values):
        return jnp.repeat(values, half, axis=0)

    far = size // 2
    out_cols_part = D // N_DP
    table = ring.table
    tanh_gate = jnp.tanh(gate_cross)
    own_gate = lax.dynamic_slice(tanh_gate, (shard * heads,), (heads,))

    token_flow = Gather(ring, [pack_tokens(tokens[0], w_out)])
    token_flow.send()
    cond_row = conditioning[0]
    cond_act = jax.nn.silu(cond_row).astype(BF16)
    mod_part = dot(cond_act, w_ada) + b_ada[None, :]
    flat_caption = captions[0].reshape(-1, size * text_rows)
    packed = exchange(pack_first(w_query, w_key, w_value, flat_caption, mod_part))
    token_flow.live, packed = ordered((token_flow.live, packed))
    token_flow.keep()

    token_flow.send()
    quarter, caption_cols, modulation = unpack_first(
        packed, k_part, flat_caption.shape[0], text_rows, CLIPS, mod_part.shape[1]
    )
    caption_cols = caption_cols.reshape(-1, text_rows)
    quarter_far = across(quarter, 2)
    cap_terms = caption_terms(w_text_key, w_text_value, caption_cols)
    caption_all = lax.all_gather(caption_cols, "dp", axis=0, tiled=True)
    token_flow.live, quarter, quarter_far, modulation, cap_terms = ordered(
        (token_flow.live, quarter, quarter_far, modulation, cap_terms)
    )
    token_flow.keep()

    token_flow.send()
    quarters = [quarter, quarter_far, across(quarter, 1), across(quarter_far, 1)]
    w_qkv, w_turned = join_projections(ring, quarters)
    cap_terms = exchange(cap_terms)
    shift_one, scale_one, gate_one, shift_two, scale_two, gate_two = jnp.split(modulation, 6, axis=1)
    branch_grad = (by_row(gate_two) * out_grad).astype(BF16)
    branch_grads = lax.all_gather(branch_grad, "dp", axis=0, tiled=True)
    lane = jnp.arange(size * half, dtype=jnp.int32)
    mirrored = (size - 1 - lane // half) * half + lane % half
    freq = 10000.0 ** (-(jnp.arange(HD // 2, dtype=F32) * 2.0 / HD))
    angle = jnp.stack([lane, mirrored]).astype(F32)[:, None, :] * freq[None, :, None]
    cos, sin = jnp.cos(angle), jnp.sin(angle)
    token_flow.live, w_qkv = ordered((token_flow.live, w_qkv))
    token_flow.keep()

    def project_some(first, groups, before):
        return project(table, first, groups, shift_one, scale_one, w_qkv, cos, sin, before)

    token_flow.send()
    blocks = [b for _, b in token_flow.blocks]
    projected = project_some(0, blocks[:5], None)
    token_flow.live, projected, cap_terms = ordered((token_flow.live, projected, cap_terms))
    token_flow.keep()

    weight_flow = Gather(ring, [unit_pieces(w_gate, w_up, w_down, token_flow.halves[0][0])])
    weight_flow.send()
    out_cols = unpack_w_out(ring, token_flow, half)
    out_full = lax.all_gather(out_cols, "dp", axis=1, tiled=True)
    halves = token_flow.halves
    block_in, qkv, raw = project_some(
        5, [*blocks[5:], [halves[0][0], halves[1][0]]], projected
    )
    cap_heads = jnp.sum(cap_terms.astype(F32), axis=0).astype(BF16)
    cap_key, cap_value = cap_heads[:, : CLIPS * CAP], cap_heads[:, CLIPS * CAP :]
    weight_flow.live, block_in, qkv, raw, cap_key, cap_value = ordered(
        (weight_flow.live, block_in, qkv, raw, cap_key, cap_value)
    )
    weight_flow.keep()

    weight_flow.send()
    mixed_blocks, self_out, cross_out, log_total = attend(own_gate, qkv, cap_key, cap_value, half)
    weight_flow.live, mixed_blocks = ordered((weight_flow.live, mixed_blocks))
    weight_flow.keep()

    mixed = exchange(mixed_blocks)
    inverse_one = inverse_rms(inputs)
    normed_one = inputs * inverse_one
    mixed, out_full = ordered((mixed, out_full))

    weight_flow.send()
    mixed = mixed.reshape(D, rows)
    attn_out = dot(mixed, out_full, TN)
    middle = inputs + by_row(gate_one) * attn_out
    inverse_two = inverse_rms(middle)
    normed_two = middle * inverse_two
    ffn_in = (normed_two * (1.0 + by_row(scale_two)) + by_row(shift_two)).astype(BF16)
    ffn_far = across(ffn_in, 2)
    weight_flow.live, ffn_in, ffn_far, branch_grads = ordered(
        (weight_flow.live, ffn_in, ffn_far, branch_grads)
    )
    weight_flow.keep()

    weight_flow.send()
    weight_flow.keep()
    pieces = [(shift, 0, arrays[0]) for shift, arrays in weight_flow.blocks]
    pieces += [(far, 0, weight_flow.halves[0][0])]
    pieces += [(far, k_rows // 2, weight_flow.halves[1][0])]
    hidden, unit_grads, ffn_own, ffn_next, down, ffn_ins = feed(
        ring, [ffn_in, ffn_far, across(ffn_in, 1), across(ffn_far, 1)], branch_grads, pieces
    )
    near = across(jnp.concatenate([ffn_own[rows:], ffn_next[rows:]]), 1)
    ffn_far = (ffn_next[:rows].astype(F32) + near[rows:].astype(F32)).astype(BF16)
    ffn_own = ffn_own[:rows].astype(F32) + near[:rows].astype(F32)
    ffn_own, ffn_far, hidden, unit_grads = ordered((ffn_own, ffn_far, hidden, unit_grads))

    ffn_far = across(ffn_far, 2)
    d_units, d_down_units, branch_terms = feed_back(
        ffn_ins, branch_grads, hidden, unit_grads, down
    )
    ffn_far, d_units, d_down_units, branch_terms = ordered(
        (ffn_far, d_units, d_down_units, branch_terms)
    )

    def add_unit_step(step, received):
        shift = far - step
        spots = (ring.spots[shift], ring.spots[-shift if step else shift])
        kind = "halves" if step == 0 else "whole"
        return add_units(table, spots, d_units, d_down_units, received, kind)

    def send(values):
        return ring.send_up(values[:1]) + ring.send_down(values[1:])

    unit_back = send(add_unit_step(0, []))
    branch = lax.psum_scatter(branch_terms, "dp", scatter_dimension=0, tiled=True)
    ffn_in_grad = ffn_own + ffn_far.astype(F32)
    middle_grad = out_grad + norm_back(
        ffn_in_grad * (1.0 + by_row(scale_two)), normed_two, inverse_two
    )
    attn_grad = (by_row(gate_one) * middle_grad).astype(BF16)
    mixed_grad = dot(out_full, attn_grad, NT).astype(BF16).reshape(size, own_cols, rows)
    unit_back, mixed_grad, mixed, attn_grad = ordered((unit_back, mixed_grad, mixed, attn_grad))

    head_grad = exchange(mixed_grad)
    unit_back = add_unit_step(1, unit_back)
    grad_out = out_terms(mixed, attn_grad)
    unit_back, head_grad, grad_out = ordered((unit_back, head_grad, grad_out))

    unit_back = send(unit_back)
    out_sum = lax.psum_scatter(grad_out, "dp", scatter_dimension=0, tiled=True)
    grads, cap_grads, gate_rows = attend_back(
        own_gate, qkv, cap_key, cap_value, head_grad, self_out, cross_out, log_total, raw, cos, sin
    )
    unit_back, grads, cap_grads = ordered((unit_back, grads, cap_grads))
    grads = grads.reshape(CLIPS, 3 * own_cols, size * half)

    token_back = send(token_terms(table, ring.spots[far], 1, grads, w_turned, True))
    unit_back = send(add_unit_step(2, unit_back))
    last = ring.spots[far - 1]
    (terms,) = token_terms(table, last, last + 1, grads, w_turned, False)
    token_back, terms, grads, cap_grads = ordered((token_back, terms, grads, cap_grads))

    def add_token_step(step, received):
        return add_received((2 * step, 2 * step + 1), terms, received)

    token_back = send(add_token_step(0, token_back))
    cap_all = jnp.transpose(cap_grads, (1, 0, 2)).reshape(own_cols, 2 * CLIPS * CAP)
    cap_all = gather_small(cap_all, "sp").reshape(D, 2 * CLIPS * CAP)
    qkv_sum = head_weight_terms(block_in, grads)
    token_back, unit_back, qkv_sum = ordered((token_back, unit_back, qkv_sum))

    token_back = send(add_token_step(1, token_back))
    unit_back = send(add_unit_step(3, unit_back))
    qkv_sum = lax.psum_scatter(qkv_sum, "dp", scatter_dimension=0, tiled=True)[0]
    token_back, unit_back, cap_all, branch, out_sum = ordered(
        (token_back, unit_back, cap_all, branch, out_sum)
    )

    token_back = send(add_token_step(2, token_back))
    cap_far = across(cap_all, 2)
    spot = ring.spots[0]
    (unit_home,) = add_units(table, (spot,), d_units, d_down_units, unit_back, "home")
    unit_far = across(unit_home, 2)
    qkv_home = exchange(qkv_sum)
    result = (middle + by_row(gate_two) * branch.astype(F32)).astype(BF16)
    sums = [
        clip_sums(middle_grad * attn_out),
        clip_sums(ffn_in_grad),
        clip_sums(ffn_in_grad * normed_two),
        clip_sums(out_grad * branch.astype(F32)),
    ]
    token_back, sums, cap_all, cap_far, unit_home, unit_far, qkv_home, out_sum = ordered(
        (token_back, sums, cap_all, cap_far, unit_home, unit_far, qkv_home, out_sum)
    )

    inputs_grad, own_sums = finish_tokens(terms, token_back, middle_grad, tokens[0], scale_one)

    mod_terms = jnp.concatenate([own_sums, *sums], axis=1)
    mod_terms = jnp.transpose(mod_terms.reshape(CLIPS, size, -1), (1, 0, 2))
    gate_own = jnp.sum(gate_rows, axis=(2, 3))
    gate_own = jnp.broadcast_to(gate_own[None], (size, CLIPS, heads))
    mod_terms = jnp.concatenate([mod_terms, gate_own], axis=2)
    mod_terms, cap_all, cap_far, unit_home, unit_far, qkv_home, out_sum = ordered(
        (mod_terms, cap_all, cap_far, unit_home, unit_far, qkv_home, out_sum)
    )

    arrived = exchange(mod_terms)
    out_home = exchange(out_sum.reshape(size, k_rows, out_cols_part))
    unit_blocks = [unit_home, unit_far, across(unit_home, 1), across(unit_far, 1)]
    cap_blocks = [cap_all, cap_far, across(cap_all, 1), across(cap_far, 1)]
    qkv_far = across(qkv_home, 2)
    shape = lambda *dims: jax.ShapeDtypeStruct(dims, F32)
    d_gate_w, d_up_w, d_down = place(
        ring, place_units, unit_blocks, [shape(k_rows, ff), shape(k_rows, ff), shape(ff_rows, D)]
    )
    d_text_key, d_text_value = text_grads(ring, caption_all, cap_blocks)
    arrived, out_home, qkv_home, qkv_far = ordered((arrived, out_home, qkv_home, qkv_far))

    own_mod = w_ada.shape[1]
    mod_low = jnp.sum(arrived[:, :, :own_mod], axis=0).astype(BF16)
    gate_all = jnp.transpose(arrived[:, :, own_mod:], (1, 0, 2)).reshape(CLIPS, HEADS)
    cond_part = dot(mod_low, w_ada, NT)
    cond_sum = jnp.sum(gather_small(cond_part, "sp"), axis=0)
    sigmoid_cond = jax.nn.sigmoid(cond_row)
    cond_grad = cond_sum * sigmoid_cond * (1.0 + cond_row * (1.0 - sigmoid_cond))
    both = jnp.concatenate([cond_act.astype(F32), mod_low.astype(F32), gate_all], axis=1)
    both_all = gather_small(both, "dp").reshape(N_DP * CLIPS, -1)
    cond_size = cond_act.shape[1]
    cond_all = both_all[:, :cond_size].astype(BF16)
    mod_all = both_all[:, cond_size : cond_size + own_mod].astype(BF16)
    d_ada = dot(cond_all, mod_all, TN)
    d_bias = jnp.sum(mod_all.astype(F32), axis=0)
    d_gate_cross = jnp.sum(both_all[:, cond_size + own_mod :], axis=0) * (
        1.0 - tanh_gate * tanh_gate
    )

    caption_grad = dot(cap_all[:, : CLIPS * CAP], w_text_key, (((0,), (1,)), ((), ()))) + dot(
        cap_all[:, CLIPS * CAP :], w_text_value, (((0,), (1,)), ((), ()))
    )
    caption_grad = caption_grad.astype(BF16).reshape(CLIPS, size, -1, text_rows)
    caption_grad = exchange(jnp.transpose(caption_grad, (1, 0, 2, 3)))
    caption_grad = (
        jnp.transpose(caption_grad, (1, 2, 0, 3)).reshape(CLIPS, -1, size * text_rows).astype(F32)
    )

    out_home = jnp.sum(out_home.astype(F32), axis=0).astype(BF16)
    (d_out,) = place(ring, place_columns, gather_packs(out_home), [shape(k_rows, D)])
    qkv_blocks = [qkv_home, qkv_far, across(qkv_home, 1), across(qkv_far, 1)]
    d_query, d_key, d_value = place(ring, place_heads, qkv_blocks, [shape(k_rows, D)] * 3)
    return (
        result[None],
        inputs_grad[None],
        caption_grad[None],
        cond_grad[None],
        d_ada,
        d_bias,
        d_query,
        d_key,
        d_value,
        d_out,
        d_gate_cross,
        d_text_key,
        d_text_value,
        d_gate_w,
        d_up_w,
        d_down,
    )


def layer(*arrays):
    tokens, clip_lens = arrays[0], arrays[4]
    size = lax.axis_size("sp")
    pack = tokens.shape[1] * size
    even = HEADS % size == 0 and size % 2 == 0 and size >= 4
    fixed = pack == clip_lens.shape[1] * MIN_CLIP and tokens.shape[1] % 256 == 0
    if even and fixed and lax.axis_size("dp") == N_DP:
        return split_heads(*arrays)
    return local(*arrays)


def solution(mesh):
    return jax.shard_map(
        layer,
        mesh=mesh,
        in_specs=(
            P("dp", "sp", None),
            P("dp", "sp", None),
            P("dp", None, "sp", None),
            P("dp", None, None),
            P("dp", None),
            P(None, "sp"),
            P("sp"),
            P("sp", None),
            P("sp", None),
            P("sp", None),
            P("sp", None),
            P(),
            P("sp", None),
            P("sp", None),
            P("sp", None),
            P("sp", None),
            P("sp", None),
        ),
        out_specs=(
            P("dp", "sp", None),
            P("dp", "sp", None),
            P("dp", None, "sp", None),
            P("dp", None, None),
            P(None, "sp"),
            P("sp"),
            P("sp", None),
            P("sp", None),
            P("sp", None),
            P("sp", None),
            P(),
            P("sp", None),
            P("sp", None),
            P("sp", None),
            P("sp", None),
            P("sp", None),
        ),
        check_vma=False,
    )
```

```python
import functools

import jax
import jax.numpy as jnp
from jax import lax
from jax.experimental import pallas as pl
from jax.experimental.pallas import tpu as pltpu
from jax.sharding import PartitionSpec as P

D = 1536
HEADS = 24
HD = 64
TEXT = 4096
CAP = 128
CLIPS = 2


EPSILON = 1e-06
MASKED = -1e30
HIGHEST = lax.Precision.HIGHEST


def rope_tables(positions):
    half_width = HD // 2
    freq = 10000.0 ** (-(jnp.arange(half_width, dtype=jnp.float32) * 2.0 / HD))
    angle = positions.astype(jnp.float32)[:, None] * freq[None, :]
    return (jnp.cos(angle)[:, None, :], jnp.sin(angle)[:, None, :])


def rotate(values, cos_table, sin_table):
    half_width = values.shape[-1] // 2
    first_half = values[..., :half_width]
    second_half = values[..., half_width:]
    return jnp.concatenate(
        [
            first_half * cos_table - second_half * sin_table,
            first_half * sin_table + second_half * cos_table,
        ],
        axis=-1,
    )


def rotate_back(grads, cos_table, sin_table):
    half_width = grads.shape[-1] // 2
    first_half = grads[..., :half_width]
    second_half = grads[..., half_width:]
    return jnp.concatenate(
        [
            first_half * cos_table + second_half * sin_table,
            second_half * cos_table - first_half * sin_table,
        ],
        axis=-1,
    )


def inverse_rms(values):
    return lax.rsqrt(jnp.mean(values * values, axis=-1, keepdims=True) + EPSILON)


def norm_back(grads, normed, inverse):
    return inverse * (grads - normed * jnp.mean(grads * normed, axis=-1, keepdims=True))


def per_clip(select, values):
    return jnp.einsum("tc,td->cd", select, values, precision=HIGHEST)


def local(
    tokens,
    cotangent,
    captions,
    conditioning,
    clip_lens,
    w_ada,
    b_ada,
    w_query,
    w_key,
    w_value,
    w_out,
    gate_cross,
    w_text_key,
    w_text_value,
    w_gate,
    w_up,
    w_down,
):
    shard = lax.axis_index("sp")
    cycle_size = lax.axis_size("sp")
    tok_rows = tokens.shape[1]
    half_rows = tok_rows // 2
    score_scale = HD ** (-0.5)
    row_index = jnp.arange(tok_rows, dtype=jnp.int32)
    logical_block = jnp.where(row_index < half_rows, shard, 2 * cycle_size - 1 - shard)
    logical = logical_block * half_rows + row_index % half_rows
    lengths = clip_lens[0]
    clip_ends = jnp.cumsum(lengths)
    clip_starts = clip_ends - lengths
    clip_index = 0
    segment = (logical >= clip_ends[clip_index]).astype(jnp.int32)
    offset = jnp.zeros((tok_rows,), jnp.int32)
    for clip_index in range(CLIPS):
        offset = offset + jnp.where(segment == clip_index, clip_starts[clip_index], 0)
    positions = logical - offset
    inputs = tokens[0].astype(jnp.float32)
    cond_row = conditioning[0]
    cond_act = jax.nn.silu(cond_row).astype(jnp.bfloat16)
    mod_part = jnp.dot(cond_act, w_ada, preferred_element_type=jnp.float32) + b_ada[None, :]
    modulation = lax.all_gather(mod_part, "sp", axis=1, tiled=True)
    select = (segment[:, None] == jnp.arange(CLIPS, dtype=jnp.int32)[None, :]).astype(jnp.float32)
    per_token = jnp.dot(select, modulation, precision=HIGHEST)
    shift_one, scale_one, gate_one, shift_two, scale_two, gate_two = jnp.split(per_token, 6, axis=1)
    weights_full = (
        lax.all_gather(w_query, "sp", axis=0, tiled=True),
        lax.all_gather(w_key, "sp", axis=0, tiled=True),
        lax.all_gather(w_value, "sp", axis=0, tiled=True),
        lax.all_gather(w_out, "sp", axis=0, tiled=True),
        lax.all_gather(w_gate, "sp", axis=0, tiled=True),
        lax.all_gather(w_up, "sp", axis=0, tiled=True),
        lax.all_gather(w_down, "sp", axis=0, tiled=True),
        lax.all_gather(w_text_key, "sp", axis=0, tiled=True),
        lax.all_gather(w_text_value, "sp", axis=0, tiled=True),
    )
    (
        query_full,
        key_full,
        value_full,
        out_full,
        gate_full,
        up_full,
        down_full,
        text_key_full,
        text_value_full,
    ) = weights_full
    inverse_one = inverse_rms(inputs)
    normed_one = inputs * inverse_one
    block_in = (normed_one * (1.0 + scale_one) + shift_one).astype(jnp.bfloat16)
    cos_table, sin_table = rope_tables(positions)

    def project(weight):
        return jnp.dot(block_in, weight, preferred_element_type=jnp.float32).reshape(
            tok_rows, HEADS, HD
        )

    query_raw = project(query_full)
    inverse_query = inverse_rms(query_raw)
    query_normed = query_raw * inverse_query
    query_rot = rotate(query_normed, cos_table, sin_table).astype(jnp.bfloat16)
    key_raw = project(key_full)
    inverse_key = inverse_rms(key_raw)
    key_normed = key_raw * inverse_key
    key_rot = rotate(key_normed, cos_table, sin_table).astype(jnp.bfloat16)
    value_rows = project(value_full).astype(jnp.bfloat16)
    caption_feats = captions[0]
    flat_caption = caption_feats.reshape(-1, TEXT)
    cap_key_part = (
        jnp.dot(flat_caption, text_key_full, preferred_element_type=jnp.float32)
        .astype(jnp.bfloat16)
        .reshape(CLIPS, -1, D)
    )
    cap_value_part = (
        jnp.dot(flat_caption, text_value_full, preferred_element_type=jnp.float32)
        .astype(jnp.bfloat16)
        .reshape(CLIPS, -1, D)
    )
    cap_key_all, cap_value_all = (
        lax.all_gather(cap_key_part, "sp", axis=1, tiled=True),
        lax.all_gather(cap_value_part, "sp", axis=1, tiled=True),
    )
    cap_key_heads = cap_key_all.reshape(CLIPS * CAP, HEADS, HD)
    cap_value_heads = cap_value_all.reshape(CLIPS * CAP, HEADS, HD)
    caption_clip = jnp.arange(CLIPS * CAP, dtype=jnp.int32) // CAP
    run_max = jnp.full((HEADS, tok_rows), MASKED, jnp.float32)
    key_piece = lax.all_gather(key_rot, "sp", axis=0, tiled=True)
    value_piece = lax.all_gather(value_rows, "sp", axis=0, tiled=True)
    segment_piece = lax.all_gather(segment, "sp", axis=0, tiled=True)
    scores = (
        jnp.einsum("qhd,khd->hqk", query_rot, key_piece, preferred_element_type=jnp.float32)
        * score_scale
    )
    allowed = (segment[:, None] == segment_piece[None, :])[None]
    scores = jnp.where(allowed, scores, MASKED)
    new_max = jnp.maximum(run_max, jnp.max(scores, axis=-1))
    weights_exp = jnp.where(allowed, jnp.exp(scores - new_max[:, :, None]), 0.0)
    new_total = jnp.sum(weights_exp, axis=-1)
    new_acc = jnp.einsum(
        "hqk,khd->qhd",
        weights_exp.astype(jnp.bfloat16),
        value_piece,
        preferred_element_type=jnp.float32,
    )
    self_out = new_acc / jnp.transpose(new_total)[:, :, None]
    log_total = jnp.transpose(new_max + jnp.log(new_total))
    cross_scores = (
        jnp.einsum("qhd,khd->hqk", query_rot, cap_key_heads, preferred_element_type=jnp.float32)
        * score_scale
    )
    own_clip = (segment[:, None] == caption_clip[None, :])[None]
    cross_probs = jax.nn.softmax(jnp.where(own_clip, cross_scores, MASKED), axis=-1)
    cross_low = cross_probs.astype(jnp.bfloat16)
    cross_out = jnp.einsum(
        "hqk,khd->qhd", cross_low, cap_value_heads, preferred_element_type=jnp.float32
    )
    tanh_gate = jnp.tanh(gate_cross)
    mixed = (
        (self_out + tanh_gate[None, :, None] * cross_out).astype(jnp.bfloat16).reshape(tok_rows, D)
    )
    attn_out = jnp.dot(mixed, out_full, preferred_element_type=jnp.float32)
    middle = inputs + gate_one * attn_out
    inverse_two = inverse_rms(middle)
    normed_two = middle * inverse_two
    ffn_in = (normed_two * (1.0 + scale_two) + shift_two).astype(jnp.bfloat16)
    gate_proj = jnp.dot(ffn_in, gate_full, preferred_element_type=jnp.float32)
    up_proj = jnp.dot(ffn_in, up_full, preferred_element_type=jnp.float32)
    sigmoid_gate = jax.nn.sigmoid(gate_proj)
    silu_gate = jax.nn.silu(gate_proj)
    hidden = (silu_gate * up_proj).astype(jnp.bfloat16)
    branch = jnp.dot(hidden, down_full, preferred_element_type=jnp.float32)
    result = (middle + gate_two * branch).astype(jnp.bfloat16)
    out_grad = cotangent[0].astype(jnp.float32)
    branch_grad = (gate_two * out_grad).astype(jnp.bfloat16)
    hidden_grad = jnp.einsum(
        "td,fd->tf", branch_grad, down_full, preferred_element_type=jnp.float32
    )
    grad_down = jnp.einsum("tf,td->fd", hidden, branch_grad, preferred_element_type=jnp.float32)
    gate_grad = (
        hidden_grad * up_proj * sigmoid_gate * (1.0 + gate_proj * (1.0 - sigmoid_gate))
    ).astype(jnp.bfloat16)
    up_grad = (hidden_grad * silu_gate).astype(jnp.bfloat16)
    ffn_in_grad = jnp.einsum(
        "tf,df->td", gate_grad, gate_full, preferred_element_type=jnp.float32
    ) + jnp.einsum("tf,df->td", up_grad, up_full, preferred_element_type=jnp.float32)
    grad_gate_w = jnp.einsum("td,tf->df", ffn_in, gate_grad, preferred_element_type=jnp.float32)
    grad_up_w = jnp.einsum("td,tf->df", ffn_in, up_grad, preferred_element_type=jnp.float32)
    gate_two_tok = out_grad * branch
    scale_two_tok = ffn_in_grad * normed_two
    middle_grad = out_grad + norm_back(ffn_in_grad * (1.0 + scale_two), normed_two, inverse_two)
    attn_grad = (gate_one * middle_grad).astype(jnp.bfloat16)
    gate_one_tok = middle_grad * attn_out
    grad_out_w = jnp.einsum("td,te->de", mixed, attn_grad, preferred_element_type=jnp.float32)
    mixed_grad = jnp.einsum(
        "te,de->td", attn_grad, out_full, preferred_element_type=jnp.float32
    ).reshape(tok_rows, HEADS, HD)
    gate_cross_part = jnp.sum(mixed_grad * cross_out, axis=(0, 2)) * (1.0 - tanh_gate * tanh_gate)
    self_grad = mixed_grad.astype(jnp.bfloat16)
    cross_grad = (tanh_gate[None, :, None] * mixed_grad).astype(jnp.bfloat16)
    cross_dp = jnp.einsum(
        "qhd,khd->hqk", cross_grad, cap_value_heads, preferred_element_type=jnp.float32
    )
    cap_value_grad = jnp.einsum(
        "hqk,qhd->khd", cross_low, cross_grad, preferred_element_type=jnp.float32
    )
    cross_ds = (
        cross_probs * (cross_dp - jnp.sum(cross_probs * cross_dp, axis=-1, keepdims=True))
    ).astype(jnp.bfloat16)
    query_grad_cross = jnp.einsum(
        "hqk,khd->qhd", cross_ds, cap_key_heads, preferred_element_type=jnp.float32
    )
    cap_key_grad = (
        jnp.einsum("hqk,qhd->khd", cross_ds, query_rot, preferred_element_type=jnp.float32)
        * score_scale
    )
    row_delta = jnp.sum(self_grad.astype(jnp.float32) * self_out, axis=-1)
    query_piece = lax.all_gather(query_rot, "sp", axis=0, tiled=True)
    grad_piece = lax.all_gather(self_grad, "sp", axis=0, tiled=True)
    log_piece = lax.all_gather(log_total.astype(jnp.bfloat16), "sp", axis=0, tiled=True).astype(
        jnp.float32
    )
    delta_piece = lax.all_gather(row_delta.astype(jnp.bfloat16), "sp", axis=0, tiled=True).astype(
        jnp.float32
    )
    segment_piece = lax.all_gather(segment, "sp", axis=0, tiled=True)
    scores = (
        jnp.einsum("qhd,khd->hqk", query_piece, key_rot, preferred_element_type=jnp.float32)
        * score_scale
    )
    allowed = (segment_piece[:, None] == segment[None, :])[None]
    probs = jnp.where(allowed, jnp.exp(scores - jnp.transpose(log_piece)[:, :, None]), 0.0)
    value_acc = jnp.einsum(
        "hqk,qhd->khd", probs.astype(jnp.bfloat16), grad_piece, preferred_element_type=jnp.float32
    )
    prob_grad = jnp.einsum(
        "qhd,khd->hqk", grad_piece, value_rows, preferred_element_type=jnp.float32
    )
    score_grad = (probs * (prob_grad - jnp.transpose(delta_piece)[:, :, None])).astype(jnp.bfloat16)
    key_acc = jnp.einsum(
        "hqk,qhd->khd", score_grad, query_piece, preferred_element_type=jnp.float32
    )
    key_acc, value_acc = (key_acc, value_acc)
    key_piece = lax.all_gather(key_rot, "sp", axis=0, tiled=True)
    value_piece = lax.all_gather(value_rows, "sp", axis=0, tiled=True)
    segment_piece = lax.all_gather(segment, "sp", axis=0, tiled=True)
    scores = (
        jnp.einsum("qhd,khd->hqk", query_rot, key_piece, preferred_element_type=jnp.float32)
        * score_scale
    )
    allowed = (segment[:, None] == segment_piece[None, :])[None]
    probs = jnp.where(allowed, jnp.exp(scores - jnp.transpose(log_total)[:, :, None]), 0.0)
    prob_grad = jnp.einsum(
        "qhd,khd->hqk", self_grad, value_piece, preferred_element_type=jnp.float32
    )
    score_grad = (probs * (prob_grad - jnp.transpose(row_delta)[:, :, None])).astype(jnp.bfloat16)
    query_acc = jnp.einsum(
        "hqk,khd->qhd", score_grad, key_piece, preferred_element_type=jnp.float32
    )
    query_rot_grad = (query_acc + query_grad_cross) * score_scale
    key_rot_grad = key_acc * score_scale
    query_raw_grad = (
        norm_back(rotate_back(query_rot_grad, cos_table, sin_table), query_normed, inverse_query)
        .astype(jnp.bfloat16)
        .reshape(tok_rows, D)
    )
    key_raw_grad = (
        norm_back(rotate_back(key_rot_grad, cos_table, sin_table), key_normed, inverse_key)
        .astype(jnp.bfloat16)
        .reshape(tok_rows, D)
    )
    value_raw_grad = value_acc.astype(jnp.bfloat16).reshape(tok_rows, D)
    block_in_grad = (
        jnp.einsum("te,de->td", query_raw_grad, query_full, preferred_element_type=jnp.float32)
        + jnp.einsum("te,de->td", key_raw_grad, key_full, preferred_element_type=jnp.float32)
        + jnp.einsum("te,de->td", value_raw_grad, value_full, preferred_element_type=jnp.float32)
    )
    grad_query_w = jnp.einsum(
        "td,te->de", block_in, query_raw_grad, preferred_element_type=jnp.float32
    )
    grad_key_w = jnp.einsum("td,te->de", block_in, key_raw_grad, preferred_element_type=jnp.float32)
    grad_value_w = jnp.einsum(
        "td,te->de", block_in, value_raw_grad, preferred_element_type=jnp.float32
    )
    scale_one_tok = block_in_grad * normed_one
    inputs_grad = middle_grad + norm_back(
        block_in_grad * (1.0 + scale_one), normed_one, inverse_one
    )
    mod_grad_part = jnp.concatenate(
        [
            per_clip(select, block_in_grad),
            per_clip(select, scale_one_tok),
            per_clip(select, gate_one_tok),
            per_clip(select, ffn_in_grad),
            per_clip(select, scale_two_tok),
            per_clip(select, gate_two_tok),
        ],
        axis=1,
    )
    cap_key_home, cap_value_home, mod_grad = (
        lax.psum_scatter(
            cap_key_grad.reshape(CLIPS, CAP, D).astype(jnp.bfloat16),
            "sp",
            scatter_dimension=1,
            tiled=True,
        ).astype(jnp.float32),
        lax.psum_scatter(
            cap_value_grad.reshape(CLIPS, CAP, D).astype(jnp.bfloat16),
            "sp",
            scatter_dimension=1,
            tiled=True,
        ).astype(jnp.float32),
        lax.psum_scatter(
            mod_grad_part.astype(jnp.bfloat16), "sp", scatter_dimension=1, tiled=True
        ).astype(jnp.float32),
    )
    cap_key_low = cap_key_home.astype(jnp.bfloat16)
    cap_value_low = cap_value_home.astype(jnp.bfloat16)
    mod_low = mod_grad.astype(jnp.bfloat16)
    caption_grad = jnp.einsum(
        "cpd,ed->cpe", cap_key_low, text_key_full, preferred_element_type=jnp.float32
    ) + jnp.einsum(
        "cpd,ed->cpe", cap_value_low, text_value_full, preferred_element_type=jnp.float32
    )
    grad_text_key = jnp.einsum(
        "cpe,cpd->ed", caption_feats, cap_key_low, preferred_element_type=jnp.float32
    )
    grad_text_value = jnp.einsum(
        "cpe,cpd->ed", caption_feats, cap_value_low, preferred_element_type=jnp.float32
    )
    grad_ada = jnp.einsum("cu,cv->uv", cond_act, mod_low, preferred_element_type=jnp.float32)
    grad_bias = jnp.sum(mod_low.astype(jnp.float32), axis=0)
    cond_part = jnp.einsum("cv,uv->cu", mod_low, w_ada, preferred_element_type=jnp.float32)
    cond_sum, gate_sum = lax.psum((cond_part, gate_cross_part), "sp")
    sigmoid_cond = jax.nn.sigmoid(cond_row)
    cond_grad = cond_sum * sigmoid_cond * (1.0 + cond_row * (1.0 - sigmoid_cond))
    home = (
        lax.psum_scatter(
            grad_query_w.astype(jnp.bfloat16), "sp", scatter_dimension=0, tiled=True
        ).astype(jnp.float32),
        lax.psum_scatter(
            grad_key_w.astype(jnp.bfloat16), "sp", scatter_dimension=0, tiled=True
        ).astype(jnp.float32),
        lax.psum_scatter(
            grad_value_w.astype(jnp.bfloat16), "sp", scatter_dimension=0, tiled=True
        ).astype(jnp.float32),
        lax.psum_scatter(
            grad_out_w.astype(jnp.bfloat16), "sp", scatter_dimension=0, tiled=True
        ).astype(jnp.float32),
        lax.psum_scatter(
            grad_gate_w.astype(jnp.bfloat16), "sp", scatter_dimension=0, tiled=True
        ).astype(jnp.float32),
        lax.psum_scatter(
            grad_up_w.astype(jnp.bfloat16), "sp", scatter_dimension=0, tiled=True
        ).astype(jnp.float32),
        lax.psum_scatter(
            grad_down.astype(jnp.bfloat16), "sp", scatter_dimension=0, tiled=True
        ).astype(jnp.float32),
        lax.psum_scatter(
            grad_text_key.astype(jnp.bfloat16), "sp", scatter_dimension=0, tiled=True
        ).astype(jnp.float32),
        lax.psum_scatter(
            grad_text_value.astype(jnp.bfloat16), "sp", scatter_dimension=0, tiled=True
        ).astype(jnp.float32),
    )
    totals = (
        lax.psum(home[0].astype(jnp.bfloat16), "dp").astype(jnp.float32),
        lax.psum(home[1].astype(jnp.bfloat16), "dp").astype(jnp.float32),
        lax.psum(home[2].astype(jnp.bfloat16), "dp").astype(jnp.float32),
        lax.psum(home[3].astype(jnp.bfloat16), "dp").astype(jnp.float32),
        lax.psum(home[4].astype(jnp.bfloat16), "dp").astype(jnp.float32),
        lax.psum(home[5].astype(jnp.bfloat16), "dp").astype(jnp.float32),
        lax.psum(home[6].astype(jnp.bfloat16), "dp").astype(jnp.float32),
        lax.psum(home[7].astype(jnp.bfloat16), "dp").astype(jnp.float32),
        lax.psum(home[8].astype(jnp.bfloat16), "dp").astype(jnp.float32),
        lax.psum(grad_ada.astype(jnp.bfloat16), "dp").astype(jnp.float32),
        lax.psum(grad_bias.astype(jnp.bfloat16), "dp").astype(jnp.float32),
        lax.psum(gate_sum.astype(jnp.bfloat16), "dp").astype(jnp.float32),
    )
    (
        d_query,
        d_key,
        d_value,
        d_out,
        d_gate_w,
        d_up_w,
        d_down_w,
        d_text_key,
        d_text_value,
        d_ada,
        d_bias,
        d_gate_cross,
    ) = totals
    return (
        result[None],
        inputs_grad[None],
        caption_grad[None],
        cond_grad[None],
        d_ada,
        d_bias,
        d_query,
        d_key,
        d_value,
        d_out,
        d_gate_cross,
        d_text_key,
        d_text_value,
        d_gate_w,
        d_up_w,
        d_down_w,
    )


MIN_CLIP = 1024
N_DP = 4
OFFSETS = (0, 2, 1, 3)
VMEM_BYTES = 48 * 1024 * 1024
NT = (((1,), (1,)), ((), ()))
TN = (((0,), (0,)), ((), ()))
F32 = jnp.float32
BF16 = jnp.bfloat16


def dot(left, right, dims=(((1,), (0,)), ((), ()))):
    return lax.dot_general(left, right, dims, preferred_element_type=F32)


def ordered(tree):
    arrays, shape = jax.tree.flatten(tree)
    spec = pl.BlockSpec(memory_space=pl.ANY)
    out = pl.pallas_call(
        lambda *refs: None,
        in_specs=[spec] * len(arrays),
        out_specs=[spec] * len(arrays),
        out_shape=[jax.ShapeDtypeStruct(a.shape, a.dtype) for a in arrays],
        input_output_aliases={i: i for i in range(len(arrays))},
        cost_estimate=pl.CostEstimate(flops=0, bytes_accessed=0, transcendentals=0),
    )(*arrays)
    return jax.tree.unflatten(shape, out)


class Ring:
    def __init__(self, size):
        self.size = size
        self.far = size // 2
        self.order = list(range(0, size, 2)) + list(range(size - 1, 0, -2))
        self.up = [(self.order[i], self.order[(i + 1) % size]) for i in range(size)]
        self.down = [(b, a) for a, b in self.up]
        shifts = [0]
        for step in range(1, self.far):
            shifts += [-step, step]
        shifts += [self.far]
        self.spots = {shift: i for i, shift in enumerate(shifts)}
        rows = [None] * size
        for spot, device in enumerate(self.order):
            devices = [self.order[(spot + shift) % size] for shift in shifts]
            rows[device] = [devices + [m ^ offset for offset in OFFSETS] for m in range(N_DP)]
        table = jnp.array(rows, jnp.int32).reshape(size * N_DP, -1)
        index = lax.axis_index("sp") * N_DP + lax.axis_index("dp")
        self.table = lax.dynamic_index_in_dim(table, index, 0, False)

    def send_up(self, values):
        return [lax.ppermute(v, "sp", self.up) for v in values]

    def send_down(self, values):
        return [lax.ppermute(v, "sp", self.down) for v in values]


class Gather:
    def __init__(self, ring, own):
        self.ring, self.own = ring, own
        self.step, self.live = 0, (own, own)
        self.blocks = [(0, own)]

    def send(self):
        ring = self.ring
        self.step += 1
        above, below = self.live
        if self.step == ring.far:
            above = [v[: v.shape[0] // 2] for v in above]
            below = [v[v.shape[0] // 2 :] for v in below]
        self.live = ring.send_up(above), ring.send_down(below)

    def keep(self):
        above, below = self.live
        if self.step == self.ring.far:
            self.halves = above, below
        else:
            self.blocks += [(-self.step, above), (self.step, below)]


def across(value, bit):
    return lax.ppermute(value, "dp", [(i, i ^ bit) for i in range(N_DP)])


def gather_packs(value):
    far = across(value, 2)
    return [value, far, across(value, 1), across(far, 1)]


def sum_packs_near(parts):
    own = parts[0].astype(F32) + across(parts[2].astype(BF16), 1).astype(F32)
    far = parts[1].astype(F32) + across(parts[3].astype(BF16), 1).astype(F32)
    return own, far.astype(BF16)


def gather_small(value, axis_name):
    size = lax.axis_size(axis_name)
    return lax.all_to_all(
        jnp.broadcast_to(value[None], (size,) + value.shape), axis_name, 0, 0, tiled=True
    )


def exchange(value):
    return lax.all_to_all(value, "sp", 0, 0, tiled=True)


def aligned(index, by):
    return index if isinstance(index, int) else pl.multiple_of(index, by)


def place(ring, write, blocks, shapes):
    first = ring.size
    listed = isinstance(blocks, list)
    arrays = blocks if listed else [blocks]

    def kernel(index_ref, *refs):
        for i in range(N_DP):
            if listed:
                write(refs[i], index_ref[first + i], refs[N_DP:])
            else:
                write(refs[0].at[i], i, refs[1:])

    vmem = pl.BlockSpec(memory_space=pltpu.VMEM)
    return pl.pallas_call(
        kernel,
        in_specs=[pl.BlockSpec(memory_space=pltpu.SMEM)] + [vmem] * len(arrays),
        out_specs=[vmem] * len(shapes),
        out_shape=shapes,
        compiler_params=pltpu.CompilerParams(vmem_limit_bytes=VMEM_BYTES),
        cost_estimate=pl.CostEstimate(
            flops=0,
            bytes_accessed=sum(s.size * s.dtype.itemsize for s in [*arrays, *shapes]),
            transcendentals=0,
        ),
    )(ring.table, *arrays)


def place_units(block_ref, index, out_refs):
    columns = block_ref.shape[1] - FOLD
    groups = columns // (2 * 128)
    for i, out_ref in enumerate(out_refs[:2]):
        for group in range(groups):
            start = unit_column(i, group)
            spot = pl.ds(aligned((group * N_DP + index) * 128, 128), 128)
            out_ref[:, spot] = block_ref[:, start : start + 128].astype(out_ref.dtype)
    for row, column, there_row, there_column, height, wide in folded():
        spot = pl.ds(aligned(index * 128 + row, 64), height)
        out_refs[2][spot, column : column + wide] = block_ref[
            there_row : there_row + height,
            columns + there_column : columns + there_column + wide,
        ].astype(out_refs[2].dtype)


def place_heads(block_ref, index, out_refs):
    groups, rows, width = block_ref.shape
    width = width // len(out_refs)
    spot = pl.ds(aligned(index * rows, rows), rows)
    for i, out_ref in enumerate(out_refs):
        for group in range(0, groups, 2):
            pair = [
                block_ref[group + k, :, i * width : (i + 1) * width].astype(F32) for k in range(2)
            ]
            columns = slice(group * width, (group + 2) * width)
            out_ref[spot, columns] = jnp.concatenate(pair, axis=1).astype(out_ref.dtype)


def join_projections(ring, blocks):
    size, part, columns = blocks[0].shape
    width = size * part * N_DP

    def kernel(index_ref, *refs):
        out_ref, turned_ref = refs[N_DP:]
        for i in range(N_DP):
            for device in range(size):
                start = (device * N_DP + index_ref[size + i]) * part
                out_ref[pl.ds(aligned(start, part), part), :] = refs[i][device]
        turned_ref[...] = jnp.transpose(out_ref[...])

    vmem = pl.BlockSpec(memory_space=pltpu.VMEM)
    return pl.pallas_call(
        kernel,
        in_specs=[pl.BlockSpec(memory_space=pltpu.SMEM)] + [vmem] * N_DP,
        out_specs=[vmem] * 2,
        out_shape=[
            jax.ShapeDtypeStruct((width, columns), BF16),
            jax.ShapeDtypeStruct((columns, width), BF16),
        ],
        compiler_params=pltpu.CompilerParams(vmem_limit_bytes=VMEM_BYTES),
        cost_estimate=pl.CostEstimate(
            flops=0, bytes_accessed=6 * width * columns, transcendentals=0
        ),
    )(ring.table, *blocks)


def caption_terms(w_key, w_value, captions):
    features, width = w_key.shape
    tokens = captions.shape[0]
    size = lax.axis_size("sp")
    columns = width // size

    def kernel(key_ref, value_ref, cap_ref, out_ref):
        for i, ref in enumerate((key_ref, value_ref)):
            total = jnp.transpose(dot(cap_ref[...], ref[...])).astype(BF16)
            for device in range(size):
                out_ref[device, :, i * tokens : (i + 1) * tokens] = total[
                    device * columns : (device + 1) * columns
                ]

    vmem = pl.BlockSpec(memory_space=pltpu.VMEM)
    return pl.pallas_call(
        kernel,
        in_specs=[vmem] * 3,
        out_specs=vmem,
        out_shape=jax.ShapeDtypeStruct((size, columns, 2 * tokens), BF16),
        compiler_params=pltpu.CompilerParams(vmem_limit_bytes=VMEM_BYTES),
        cost_estimate=pl.CostEstimate(
            flops=4 * tokens * features * width,
            bytes_accessed=4 * (features + tokens) * width,
            transcendentals=0,
        ),
    )(w_key, w_value, captions)


def text_grads(ring, captions, grads):
    width, columns = grads[0].shape
    tokens = columns // 2
    features = captions.shape[1]
    size = ring.size

    def kernel(index_ref, cap_ref, *refs):
        caps = [
            jnp.transpose(cap_ref[pl.ds(aligned(index_ref[size + i] * tokens, tokens), tokens), :])
            for i in range(N_DP)
        ]
        for which, out_ref in enumerate(refs[N_DP:]):
            total = None
            for i in range(N_DP):
                grad = refs[i][:, which * tokens : (which + 1) * tokens]
                term = dot(caps[i], jnp.transpose(grad))
                total = term if total is None else total + term
            out_ref[...] = total

    vmem = pl.BlockSpec(memory_space=pltpu.VMEM)
    return pl.pallas_call(
        kernel,
        in_specs=[pl.BlockSpec(memory_space=pltpu.SMEM)] + [vmem] * (1 + N_DP),
        out_specs=[vmem] * 2,
        out_shape=[jax.ShapeDtypeStruct((features, width), F32)] * 2,
        compiler_params=pltpu.CompilerParams(vmem_limit_bytes=VMEM_BYTES),
        cost_estimate=pl.CostEstimate(
            flops=4 * N_DP * tokens * features * width,
            bytes_accessed=8 * features * width + 4 * N_DP * tokens * width,
            transcendentals=0,
        ),
    )(ring.table, captions, *grads)


def out_terms(mixed, grad):
    width, rows = mixed.shape
    columns = width // N_DP

    def kernel(mixed_ref, grad_ref, out_ref):
        out_ref[0] = dot(mixed_ref[...], grad_ref[...]).astype(BF16)

    return pl.pallas_call(
        kernel,
        grid=(N_DP,),
        in_specs=[
            pl.BlockSpec((width, rows), lambda i: (0, 0)),
            pl.BlockSpec((rows, columns), lambda i: (0, i)),
        ],
        out_specs=pl.BlockSpec((1, width, columns), lambda i: (i, 0, 0)),
        out_shape=jax.ShapeDtypeStruct((N_DP, width, columns), BF16),
        compiler_params=pltpu.CompilerParams(vmem_limit_bytes=VMEM_BYTES),
        cost_estimate=pl.CostEstimate(
            flops=2 * width * width * rows, bytes_accessed=2 * width * width, transcendentals=0
        ),
    )(mixed, grad)


def finish_tokens(terms, received, middle_grad, tokens, scale):
    rows, width = tokens.shape
    half = rows // CLIPS
    last = terms.shape[0] // rows - 1

    def kernel(terms_ref, above_ref, below_ref, middle_ref, x_ref, scale_ref, out_ref, sums_ref):
        for clip in range(CLIPS):
            span = slice(clip * half, (clip + 1) * half)
            grad = (
                terms_ref[span].astype(F32) + above_ref[span].astype(F32) + below_ref[span].astype(F32)
            )
            x = x_ref[span].astype(F32)
            inverse = lax.rsqrt(jnp.mean(x * x, axis=-1, keepdims=True) + EPSILON)
            normed = x * inverse
            scaled = grad * (1.0 + scale_ref[clip : clip + 1, :])
            mean = jnp.mean(scaled * normed, axis=-1, keepdims=True)
            out_ref[span] = middle_ref[span] + inverse * (scaled - normed * mean)
            sums_ref[clip : clip + 1, :width] = jnp.sum(grad, axis=0, keepdims=True)
            sums_ref[clip : clip + 1, width:] = jnp.sum(grad * normed, axis=0, keepdims=True)

    fixed = pl.BlockSpec((rows, width), lambda i: (0, 0))
    return pl.pallas_call(
        kernel,
        grid=(1,),
        in_specs=[pl.BlockSpec((rows, width), lambda i: (last, 0))]
        + [fixed] * 4
        + [pl.BlockSpec((CLIPS, width), lambda i: (0, 0))],
        out_specs=[fixed, pl.BlockSpec((CLIPS, 2 * width), lambda i: (0, 0))],
        out_shape=[
            jax.ShapeDtypeStruct((rows, width), F32),
            jax.ShapeDtypeStruct((CLIPS, 2 * width), F32),
        ],
        compiler_params=pltpu.CompilerParams(vmem_limit_bytes=VMEM_BYTES),
        cost_estimate=pl.CostEstimate(
            flops=0, bytes_accessed=16 * rows * width, transcendentals=0
        ),
    )(terms, *received, middle_grad, tokens, scale)


def place_columns(block_ref, index, out_refs):
    width = block_ref.shape[1]
    out_refs[0][:, pl.ds(aligned(index * width, 128), width)] = block_ref[...].astype(
        out_refs[0].dtype
    )


UNITS = 512


HELD = 32


def pack_tokens(tokens, w_out):
    rows, width = tokens.shape
    half = rows // 2
    columns = width // N_DP
    k_rows = w_out.shape[0]
    part = k_rows // N_DP
    member = jnp.reshape(lax.axis_index("dp"), (1,)).astype(jnp.int32)

    def kernel(member_ref, tokens_ref, w_ref, out_ref):
        spot = pl.ds(aligned(member_ref[0] * columns, 128), columns)
        for clip in range(CLIPS):
            start = clip * (half + HELD)
            out_ref[start : start + half] = tokens_ref[clip * half : (clip + 1) * half]
            count = min(part - clip * HELD, HELD)
            for group in range(N_DP):
                top = group * part + clip * HELD
                out_ref[
                    start + half : start + half + count, group * columns : (group + 1) * columns
                ] = w_ref[top : top + count, spot]
            if count < HELD:
                out_ref[start + half + count : start + half + HELD] = jnp.zeros(
                    (HELD - count, width), BF16
                )

    vmem = pl.BlockSpec(memory_space=pltpu.VMEM)
    return pl.pallas_call(
        kernel,
        in_specs=[pl.BlockSpec(memory_space=pltpu.SMEM), vmem, vmem],
        out_specs=vmem,
        out_shape=jax.ShapeDtypeStruct((rows + CLIPS * HELD, width), BF16),
        compiler_params=pltpu.CompilerParams(vmem_limit_bytes=VMEM_BYTES),
        cost_estimate=pl.CostEstimate(
            flops=0, bytes_accessed=6 * rows * width, transcendentals=0
        ),
    )(member, tokens, w_out)


def unpack_w_out(ring, flow, half):
    width = flow.own[0].shape[1]
    columns = width // N_DP
    k_rows = width // ring.size
    part = k_rows // N_DP
    block = (half + HELD) // HELD
    groups = [[arrays[0]] for _, arrays in flow.blocks]
    groups += [[flow.halves[0][0], flow.halves[1][0]]]
    spots = [ring.spots[shift] for shift, _ in flow.blocks] + [ring.spots[ring.far]]
    operands, specs = [], []
    for group in groups:
        for clip in range(CLIPS):
            operands.append(group[clip] if len(group) > 1 else group[0])
            index = block - 1 if len(group) > 1 else (clip + 1) * block - 1
            specs.append(pl.BlockSpec((HELD, width), lambda i, index=index: (index, 0)))

    def kernel(index_ref, *refs):
        for i, spot in enumerate(spots):
            for clip in range(CLIPS):
                count = min(part - clip * HELD, HELD)
                for group in range(N_DP):
                    top = index_ref[spot] * k_rows + group * part + clip * HELD
                    refs[-1][pl.ds(aligned(top, 16), count), :] = refs[CLIPS * i + clip][
                        :count, group * columns : (group + 1) * columns
                    ]

    return pl.pallas_call(
        kernel,
        grid=(1,),
        in_specs=[pl.BlockSpec(memory_space=pltpu.SMEM)] + specs,
        out_specs=pl.BlockSpec((width, columns), lambda i: (0, 0)),
        out_shape=jax.ShapeDtypeStruct((width, columns), BF16),
        compiler_params=pltpu.CompilerParams(vmem_limit_bytes=VMEM_BYTES),
        cost_estimate=pl.CostEstimate(
            flops=0, bytes_accessed=4 * width * columns, transcendentals=0
        ),
    )(ring.table, *operands)


def unit_pieces(w_gate, w_up, w_down, after):
    rows, columns = w_gate.shape
    groups = columns // (N_DP * 128)
    member = jnp.reshape(lax.axis_index("dp"), (1,)).astype(jnp.int32)
    first = 2 * groups * 128
    width = first + FOLD

    def kernel(member_ref, gate_ref, up_ref, down_ref, after_ref, out_ref):
        for i, ref in enumerate((gate_ref, up_ref)):
            for group in range(groups):
                spot = aligned((group * N_DP + member_ref[0]) * 128, 128)
                start = unit_column(i, group)
                out_ref[:, start : start + 128] = ref[:, pl.ds(spot, 128)]
        spot = aligned(member_ref[0] * 128, 128)
        for row, column, there_row, there_column, height, wide in folded():
            out_ref[there_row : there_row + height, first + there_column : first + there_column + wide] = (
                down_ref[pl.ds(aligned(spot + row, 32), height), column : column + wide]
            )

    vmem = pl.BlockSpec(memory_space=pltpu.VMEM)
    return pl.pallas_call(
        kernel,
        in_specs=[pl.BlockSpec(memory_space=pltpu.SMEM), vmem, vmem, vmem, pl.BlockSpec(memory_space=pl.ANY)],
        out_specs=vmem,
        out_shape=jax.ShapeDtypeStruct((rows, width), w_gate.dtype),
        compiler_params=pltpu.CompilerParams(vmem_limit_bytes=VMEM_BYTES),
        cost_estimate=pl.CostEstimate(
            flops=0, bytes_accessed=8 * rows * columns, transcendentals=0
        ),
    )(member, w_gate, w_up, w_down, after)


FOLD = 1024


def folded(low=0, high=192):
    spots = []
    if low < 128:
        end = min(high, 128)
        spots.append((low, 0, 0, 0, end - low, FOLD))
    if high > 128:
        start = max(low, 128) - 128
        count = high - 128 - start
        for side in range(2):
            spots.append(
                (64 * side + start, FOLD, 128 + start - low, 512 * side, count, 512)
            )
    return spots


def unit_column(which, group):
    per_tile = UNITS // 128
    tile, rest = divmod(group, per_tile)
    return tile * 2 * UNITS + which * UNITS + rest * 128


def pack_first(w_query, w_key, w_value, captions, modulation, after):
    k_rows, width = w_query.shape
    size = width // k_rows
    part = k_rows // N_DP
    tokens, features = captions.shape
    columns = 3 * k_rows
    clips, own_mod = modulation.shape
    pieces = own_mod // columns
    mod_rows = 2 * clips * pieces
    member = jnp.reshape(lax.axis_index("dp"), (1,)).astype(jnp.int32)
    rows = part + tokens + 16

    def kernel(member_ref, q_ref, k_ref, v_ref, cap_ref, mod_ref, after_ref, out_ref):
        spot = pl.ds(aligned(member_ref[0] * part, part), part)
        mod = jnp.concatenate(
            [mod_ref[:, i * columns : (i + 1) * columns] for i in range(pieces)], axis=0
        )
        high = mod.astype(BF16).astype(F32)
        fill = jnp.zeros((16 - mod_rows, columns), F32)
        mod = jnp.concatenate([high, mod - high, fill], axis=0).astype(BF16)
        each = features // size
        fill = jnp.zeros((tokens, columns - each), BF16)
        for device in range(size):
            own = slice(device * k_rows, (device + 1) * k_rows)
            row = [ref[spot, own].astype(F32) for ref in (q_ref, k_ref, v_ref)]
            out_ref[device, :part] = jnp.concatenate(row, axis=1).astype(BF16)
            cap = cap_ref[:, device * each : (device + 1) * each]
            out_ref[device, part : part + tokens] = jnp.concatenate([cap, fill], axis=1)
            out_ref[device, part + tokens :] = mod

    vmem = pl.BlockSpec(memory_space=pltpu.VMEM)
    return pl.pallas_call(
        kernel,
        in_specs=[pl.BlockSpec(memory_space=pltpu.SMEM)] + [vmem] * 5 + [pl.BlockSpec(memory_space=pl.ANY)],
        out_specs=vmem,
        out_shape=jax.ShapeDtypeStruct((size, rows, columns), BF16),
        compiler_params=pltpu.CompilerParams(vmem_limit_bytes=VMEM_BYTES),
        cost_estimate=pl.CostEstimate(
            flops=0, bytes_accessed=8 * size * rows * columns, transcendentals=0
        ),
    )(member, w_query, w_key, w_value, captions, modulation, after)


def unpack_first(packed, part, tokens, features, clips, own_mod):
    size, _, columns = packed.shape
    pieces = own_mod // columns
    each = tokens // clips

    def kernel(in_ref, quarter_ref, cap_ref, mod_ref):
        for device in range(size):
            quarter_ref[device] = in_ref[device, :part]
            for clip in range(clips):
                start = part + clip * each
                cap_ref[clip, device * each : (device + 1) * each] = in_ref[
                    device, start : start + each, :features
                ]
            mod = in_ref[device, part + tokens :].astype(F32)
            count = clips * pieces
            mod = mod[:count] + mod[count : 2 * count]
            mod = [mod[i * clips : (i + 1) * clips] for i in range(pieces)]
            mod_ref[:, device * own_mod : (device + 1) * own_mod] = jnp.concatenate(mod, axis=1)

    vmem = pl.BlockSpec(memory_space=pltpu.VMEM)
    return pl.pallas_call(
        kernel,
        in_specs=[vmem],
        out_specs=[vmem] * 3,
        out_shape=[
            jax.ShapeDtypeStruct((size, part, columns), BF16),
            jax.ShapeDtypeStruct((clips, size * each, features), BF16),
            jax.ShapeDtypeStruct((clips, size * own_mod), F32),
        ],
        compiler_params=pltpu.CompilerParams(vmem_limit_bytes=VMEM_BYTES),
        cost_estimate=pl.CostEstimate(
            flops=0, bytes_accessed=4 * packed.size, transcendentals=0
        ),
    )(packed)


def feed_kernel(ids_ref, *refs, size, places):
    count = len(places)
    x_refs, grad_ref = refs[:N_DP], refs[N_DP]
    piece_refs = refs[N_DP + 1 : N_DP + 1 + count]
    hidden_ref, grads_ref, near_ref, far_ref = refs[N_DP + 1 + count : N_DP + 5 + count]
    down_out, x_out = refs[N_DP + 5 + count : N_DP + 7 + count]
    x_all, grad_all, w_all, down_all, total, sems, out_sems = refs[N_DP + 7 + count :]
    rows = x_refs[0].shape[0]
    columns = w_all.shape[1]
    tile = pl.program_id(0)
    last = pl.num_programs(0) - 1

    def spot(i):
        return pl.ds(aligned(ids_ref[size + i] * rows, rows), rows)

    def copies(first, end=None):
        pairs = []
        for i in range(N_DP):
            pairs.append((x_refs[i], x_all.at[spot(i)]))
        for i, (place_, start, height) in enumerate(places):
            top = aligned(ids_ref[place_] * 192 + start, 32)
            pairs.append((piece_refs[i].at[:, pl.ds(0, columns)], w_all.at[pl.ds(top, height)]))
        pairs.append((grad_ref, grad_all))
        for i, (place_, start, height) in enumerate(places):
            for row, column, there_row, there_column, high, wide in folded(start, start + height):
                top = aligned(ids_ref[place_] * 128 + row, 32)
                pairs.append(
                    (
                        piece_refs[i].at[
                            pl.ds(there_row, high), pl.ds(columns + there_column, wide)
                        ],
                        down_all.at[pl.ds(top, high), pl.ds(column, wide)],
                    )
                )
        numbered = list(enumerate(pairs))[first:end]
        return [pltpu.make_async_copy(a, b, sems.at[i]) for i, (a, b) in numbered]

    def keep(i):
        source, there = ((x_all, x_out), (down_all, down_out))[i]
        return pltpu.make_async_copy(source, there, out_sems.at[i])

    early = N_DP + count

    @pl.when(tile == 0)
    def _():
        for copy in copies(0):
            copy.start()
        for copy in copies(0, early):
            copy.wait()
        keep(0).start()

    weight = w_all[:, pl.ds(aligned(tile * 2 * UNITS, 2 * UNITS), 2 * UNITS)]
    both = dot(x_all[...], weight)
    gate, up = both[:, :UNITS], both[:, UNITS:]

    @pl.when(tile == 0)
    def _():
        for copy in copies(early):
            copy.wait()
        keep(1).start()

    down = down_all[pl.ds(aligned(tile * UNITS, UNITS), UNITS), :]
    hidden_grad = dot(grad_all[...], down, NT)
    sigmoid = jax.nn.sigmoid(gate)
    silu = gate * sigmoid
    hidden_ref[...] = (silu * up).astype(BF16)
    gate_grad = hidden_grad * up * sigmoid * (1.0 + gate * (1.0 - sigmoid))
    grads = jnp.concatenate([gate_grad.astype(BF16), (hidden_grad * silu).astype(BF16)], axis=1)
    grads_ref[...] = grads
    term = dot(grads, weight, NT)

    @pl.when(tile == 0)
    def _():
        total[...] = term

    @pl.when(tile > 0)
    def _():
        total[...] += term

    @pl.when(tile == last)
    def _():
        for i, out_ref in enumerate((near_ref, far_ref)):
            out_ref[:rows] = total[spot(i), :].astype(BF16)
            out_ref[rows:] = total[spot(2 + i), :].astype(BF16)
        keep(0).wait()
        keep(1).wait()


def feed(ring, xs, grads, pieces):
    rows, width = xs[0].shape
    units = (pieces[0][2].shape[1] - FOLD) // 2
    places = tuple((ring.spots[shift], start, piece.shape[0]) for shift, start, piece in pieces)
    copies = N_DP + 1 + len(pieces)
    copies += sum(len(folded(start, start + height)) for _, start, height in places)
    anywhere = pl.BlockSpec(memory_space=pl.ANY)
    return pl.pallas_call(
        functools.partial(feed_kernel, size=ring.size, places=places),
        grid_spec=pltpu.PrefetchScalarGridSpec(
            num_scalar_prefetch=1,
            grid=(units // UNITS,),
            in_specs=[anywhere] * (N_DP + 1 + len(pieces)),
            out_specs=[
                pl.BlockSpec((N_DP * rows, UNITS), lambda t, ids: (0, t)),
                pl.BlockSpec((N_DP * rows, 2 * UNITS), lambda t, ids: (0, t)),
                pl.BlockSpec((2 * rows, width), lambda t, ids: (0, 0)),
                pl.BlockSpec((2 * rows, width), lambda t, ids: (0, 0)),
                anywhere,
                anywhere,
            ],
            scratch_shapes=[
                pltpu.VMEM((N_DP * rows, width), BF16),
                pltpu.VMEM((N_DP * rows, width), BF16),
                pltpu.VMEM((width, 2 * units), BF16),
                pltpu.VMEM((units, width), BF16),
                pltpu.VMEM((N_DP * rows, width), F32),
                pltpu.SemaphoreType.DMA((copies,)),
                pltpu.SemaphoreType.DMA((2,)),
            ],
        ),
        out_shape=[
            jax.ShapeDtypeStruct((N_DP * rows, units), BF16),
            jax.ShapeDtypeStruct((N_DP * rows, 2 * units), BF16),
            jax.ShapeDtypeStruct((2 * rows, width), BF16),
            jax.ShapeDtypeStruct((2 * rows, width), BF16),
            jax.ShapeDtypeStruct((units, width), BF16),
            jax.ShapeDtypeStruct((N_DP * rows, width), BF16),
        ],
        compiler_params=pltpu.CompilerParams(vmem_limit_bytes=VMEM_BYTES),
        cost_estimate=pl.CostEstimate(
            flops=10 * N_DP * rows * width * units,
            bytes_accessed=24 * N_DP * rows * width,
            transcendentals=N_DP * rows * units,
        ),
    )(ring.table, *xs, grads, *[piece for _, _, piece in pieces])


def add_home(terms, received):
    rows, width = received[0].shape
    last = terms.shape[0] // rows - 1

    def kernel(own_ref, above_ref, below_ref, out_ref):
        total = own_ref[...].astype(F32) + above_ref[...].astype(F32) + below_ref[...].astype(F32)
        out_ref[...] = total.astype(BF16)

    fixed = pl.BlockSpec((rows, width), lambda i: (0, 0))
    return pl.pallas_call(
        kernel,
        grid=(1,),
        in_specs=[pl.BlockSpec((rows, width), lambda i: (last, 0)), fixed, fixed],
        out_specs=fixed,
        out_shape=jax.ShapeDtypeStruct((rows, width), BF16),
        compiler_params=pltpu.CompilerParams(vmem_limit_bytes=VMEM_BYTES),
        cost_estimate=pl.CostEstimate(
            flops=0, bytes_accessed=8 * rows * width, transcendentals=0
        ),
    )(terms, *received)


def unit_terms(table, first, count, xs, hidden, unit_grads, grads, apart):
    rows, width = xs.shape
    columns = unit_grads.shape[1]
    k_rows = width // lax.axis_size("sp")
    half = k_rows // 2

    def kernel(ids_ref, x_ref, hidden_ref, units_ref, grads_ref, *refs):
        out_refs, turned, whole = refs[:-2], refs[-2], refs[-1]
        device = ids_ref[first - pl.program_id(0)]
        turned[...] = jnp.transpose(x_ref[...])
        spot = pl.ds(aligned(lax.rem(device, 2) * k_rows, k_rows), k_rows)
        down = dot(hidden_ref[...], grads_ref[...], TN).astype(BF16)
        target = whole if apart else out_refs[0]
        target[:, :columns] = dot(turned[spot, :], units_ref[...]).astype(BF16)
        for row, column, there_row, there_column, height, wide in folded(0, k_rows):
            target[
                there_row : there_row + height,
                columns + there_column : columns + there_column + wide,
            ] = down[row : row + height, column : column + wide]
        if apart:
            out_refs[0][...] = whole[:half]
            out_refs[1][...] = whole[half:]

    outs, height = (2, half) if apart else (1, k_rows)
    return pl.pallas_call(
        kernel,
        grid_spec=pltpu.PrefetchScalarGridSpec(
            num_scalar_prefetch=1,
            grid=(count,),
            in_specs=[
                pl.BlockSpec((rows, 2 * k_rows), lambda i, ids: (0, ids[first - i] // 2)),
                pl.BlockSpec((rows, 128), lambda i, ids: (0, ids[first - i])),
                pl.BlockSpec((rows, columns), lambda i, ids: (0, 0)),
                pl.BlockSpec((rows, width), lambda i, ids: (0, 0)),
            ],
            out_specs=[pl.BlockSpec((height, columns + FOLD), lambda i, ids: (i, 0))] * outs,
            scratch_shapes=[
                pltpu.VMEM((2 * k_rows, rows), BF16),
                pltpu.VMEM((k_rows, columns + FOLD), BF16),
            ],
        ),
        out_shape=[jax.ShapeDtypeStruct((count * height, columns + FOLD), BF16)] * outs,
        compiler_params=pltpu.CompilerParams(vmem_limit_bytes=VMEM_BYTES),
        cost_estimate=pl.CostEstimate(
            flops=2 * count * rows * (k_rows * columns + 128 * width),
            bytes_accessed=4 * rows * columns + 2 * count * k_rows * (columns + FOLD),
            transcendentals=0,
        ),
    )(table, xs, hidden, unit_grads, grads)


def token_terms(table, first, count, grads, weight, apart):
    clips, columns, length = grads.shape
    width = weight.shape[1]
    half = length // lax.axis_size("sp")

    def kernel(ids_ref, grads_ref, w_ref, *out_refs):
        for clip in range(clips):
            value = dot(jnp.transpose(grads_ref[clip]), w_ref[...]).astype(BF16)
            if apart:
                out_refs[clip][...] = value
            else:
                out_refs[0][clip * half : (clip + 1) * half] = value

    outs, rows = (clips, half) if apart else (1, clips * half)
    return pl.pallas_call(
        kernel,
        grid_spec=pltpu.PrefetchScalarGridSpec(
            num_scalar_prefetch=1,
            grid=(count,),
            in_specs=[
                pl.BlockSpec((clips, columns, half), lambda i, ids: (0, 0, ids[first - i])),
                pl.BlockSpec((columns, width), lambda i, ids: (0, 0)),
            ],
            out_specs=[pl.BlockSpec((rows, width), lambda i, ids: (i, 0))] * outs,
        ),
        out_shape=[jax.ShapeDtypeStruct((count * rows, width), BF16)] * outs,
        compiler_params=pltpu.CompilerParams(vmem_limit_bytes=VMEM_BYTES),
        cost_estimate=pl.CostEstimate(
            flops=2 * clips * count * half * columns * width,
            bytes_accessed=2 * clips * count * half * (columns + width) + 2 * width * columns,
            transcendentals=0,
        ),
    )(table, grads, weight)


def add_received(index, terms, received):
    width = terms.shape[1]
    rows = terms.shape[0] // (2 * (lax.axis_size("sp") // 2 - 1) + 1)
    half = rows // 2

    def kernel(*refs):
        for side in range(2):
            own, arrived, out = refs[side], refs[2 + side], refs[4 + side]
            value = own[...].astype(F32)
            if arrived.shape[0] == rows:
                out[...] = (value + arrived[...].astype(F32)).astype(BF16)
            else:
                span = slice(side * half, (side + 1) * half)
                rest = slice((1 - side) * half, (2 - side) * half)
                out[span] = (value[span] + arrived[...].astype(F32)).astype(BF16)
                out[rest] = own[rest]

    def spec(height, block=0):
        return pl.BlockSpec((height, width), lambda i: (block, 0))

    return pl.pallas_call(
        kernel,
        grid=(1,),
        in_specs=[spec(rows, index[0]), spec(rows, index[1])]
        + [spec(a.shape[0]) for a in received],
        out_specs=[spec(rows)] * 2,
        out_shape=[jax.ShapeDtypeStruct((rows, width), BF16)] * 2,
        compiler_params=pltpu.CompilerParams(vmem_limit_bytes=VMEM_BYTES),
        cost_estimate=pl.CostEstimate(
            flops=0, bytes_accessed=12 * rows * width, transcendentals=0
        ),
    )(terms, terms, *received)


def head_weight_terms(ring, block_in, grads):
    clips, length, width = block_in.shape
    columns = grads.shape[1]
    size = ring.size
    k_rows = width // size
    part = k_rows // N_DP
    tile = 2 * k_rows

    def kernel(index_ref, in_ref, grads_ref, *refs):
        out_refs, turned = refs[:N_DP], refs[N_DP]
        total = dot(grads_ref[0], in_ref[0])
        for clip in range(1, clips):
            total = total + dot(grads_ref[clip], in_ref[clip])
        turned[...] = jnp.transpose(total)
        for i, out_ref in enumerate(out_refs):
            for shard in range(2):
                start = shard * k_rows + index_ref[size + i] * part
                out_ref[shard] = turned[pl.ds(aligned(start, part), part), :].astype(BF16)

    return pl.pallas_call(
        kernel,
        grid=(width // tile,),
        in_specs=[
            pl.BlockSpec(memory_space=pltpu.SMEM),
            pl.BlockSpec((clips, length, tile), lambda t: (0, 0, t)),
            pl.BlockSpec((clips, columns, length), lambda t: (0, 0, 0)),
        ],
        out_specs=[pl.BlockSpec((2, part, columns), lambda t: (t, 0, 0))] * N_DP,
        out_shape=[jax.ShapeDtypeStruct((size, part, columns), BF16)] * N_DP,
        scratch_shapes=[pltpu.VMEM((tile, columns), F32)],
        compiler_params=pltpu.CompilerParams(vmem_limit_bytes=VMEM_BYTES),
        cost_estimate=pl.CostEstimate(
            flops=2 * clips * length * width * columns,
            bytes_accessed=2 * clips * length * (width + columns) + 2 * width * columns,
            transcendentals=0,
        ),
    )(ring.table, block_in, grads)


def turn(values, cos, sin):
    half = HD // 2
    a, b = values[:half], values[half:]
    return jnp.concatenate([a * cos - b * sin, a * sin + b * cos], axis=0)


def turn_back(grads, cos, sin):
    half = HD // 2
    a, b = grads[:half], grads[half:]
    return jnp.concatenate([a * cos + b * sin, b * cos - a * sin], axis=0)


def head_inverse(values):
    return lax.rsqrt(jnp.mean(values * values, axis=0, keepdims=True) + EPSILON)


def project_kernel(place_ref, *refs, sizes):
    count = sum(sizes)
    blocks = refs[:count]
    shift_ref, scale_ref, w_ref, cos_ref, sin_ref = refs[count : count + 5]
    in_ref, out_ref, raw_ref = refs[-3:]
    half = in_ref.shape[1]
    heads = w_ref.shape[1] // (3 * HD)

    def run(x, clip):
        x = x.astype(F32)
        inverse = lax.rsqrt(jnp.mean(x * x, axis=-1, keepdims=True) + EPSILON)
        block = x * inverse * (1.0 + scale_ref[clip : clip + 1, :]) + shift_ref[clip : clip + 1, :]
        block = block.astype(BF16)
        in_ref[clip] = block
        raw = jnp.transpose(dot(block, w_ref[...]))
        raw_ref[clip] = raw[: 2 * heads * HD]
        cos, sin = cos_ref[clip], sin_ref[clip]
        for head in range(2 * heads):
            rows = raw[head * HD : (head + 1) * HD]
            rotated = turn(rows * head_inverse(rows), cos, sin)
            out_ref[clip, head * HD : (head + 1) * HD, :] = rotated.astype(BF16)
        out_ref[clip, 2 * heads * HD :, :] = raw[2 * heads * HD :].astype(BF16)

    first = 0
    for step, size in enumerate(sizes):
        group = blocks[first : first + size]
        first += size

        @pl.when(pl.program_id(0) == step)
        def _(group=group):
            for clip in range(CLIPS):
                if len(group) == 1:
                    start = clip * (half + HELD)
                    run(group[0][start : start + half, :], clip)
                else:
                    run(group[clip][:half], clip)


def project(table, first, groups, shift, scale, weight, cos, sin, before):
    sizes = tuple(len(g) for g in groups)
    blocks = [b for g in groups for b in g]
    width, columns = weight.shape
    length = cos.shape[2]
    half = groups[0][0].shape[0] * len(groups[0]) // CLIPS - HELD
    fixed = lambda a: pl.BlockSpec(a.shape, lambda i, ids: (0,) * a.ndim)
    out_shape = [
        jax.ShapeDtypeStruct((CLIPS, length, width), BF16),
        jax.ShapeDtypeStruct((CLIPS, columns, length), BF16),
        jax.ShapeDtypeStruct((CLIPS, 2 * columns // 3, length), F32),
    ]
    in_specs = [fixed(a) for a in (*blocks, shift, scale, weight)]
    in_specs += [pl.BlockSpec((CLIPS, HD // 2, half), lambda i, ids: (0, 0, ids[first + i]))] * 2
    operands = [*blocks, shift, scale, weight, cos, sin]
    aliases = {}
    if before is not None:
        aliases = {1 + len(operands) + i: i for i in range(3)}
        in_specs += [pl.BlockSpec(memory_space=pl.ANY)] * 3
        operands += before
    rows = CLIPS * half * len(groups)
    return pl.pallas_call(
        functools.partial(project_kernel, sizes=sizes),
        grid_spec=pltpu.PrefetchScalarGridSpec(
            num_scalar_prefetch=1,
            grid=(len(groups),),
            in_specs=in_specs,
            out_specs=[
                pl.BlockSpec((CLIPS, half, width), lambda i, ids: (0, ids[first + i], 0)),
                pl.BlockSpec((CLIPS, columns, half), lambda i, ids: (0, 0, ids[first + i])),
                pl.BlockSpec((CLIPS, 2 * columns // 3, half), lambda i, ids: (0, 0, ids[first + i])),
            ],
        ),
        out_shape=out_shape,
        input_output_aliases=aliases,
        compiler_params=pltpu.CompilerParams(vmem_limit_bytes=VMEM_BYTES),
        cost_estimate=pl.CostEstimate(
            flops=2 * rows * width * columns,
            bytes_accessed=4 * rows * width + 8 * rows * columns + 2 * width * columns,
            transcendentals=0,
        ),
    )(table, *operands)


def cross_probabilities(cap_key, query):
    scores = dot(cap_key, query, TN) * HD**-0.5
    grown = jnp.exp(scores - jnp.max(scores, axis=0, keepdims=True))
    return grown / jnp.sum(grown, axis=0, keepdims=True)


def attend_kernel(
    gate_ref, q_ref, k_ref, v_ref, ck_ref, cv_ref, mixed_ref, self_ref, cross_ref, log_ref, *, block
):
    length = q_ref.shape[2]
    half = mixed_ref.shape[2]
    gate = gate_ref[pl.program_id(1)]
    keys = jnp.transpose(k_ref[0])
    for start in range(0, length, block):
        query = q_ref[0, :, start : start + block]
        grown = jnp.exp(dot(keys, query) * HD**-0.5)
        total = jnp.sum(grown, axis=0, keepdims=True)
        self_out = dot(v_ref[0], grown.astype(BF16)) / total
        probs = cross_probabilities(ck_ref[...], query)
        cross_out = dot(cv_ref[...], probs.astype(BF16))
        self_ref[0, :, start : start + block] = self_out
        cross_ref[0, :, start : start + block] = cross_out
        log_ref[0, 0, :, start : start + block] = jnp.log(total)
        mixed = (self_out + gate * cross_out).astype(BF16)
        for piece in range(block // half):
            mixed_ref[start // half + piece] = mixed[:, piece * half : (piece + 1) * half]


def attend(gate, qkv, cap_key, cap_value, half):
    clips, columns, length = qkv.shape
    heads = columns // (3 * HD)
    head_spec = lambda first: pl.BlockSpec((1, HD, length), lambda c, h: (c, first * heads + h, 0))
    cap_spec = pl.BlockSpec((HD, CAP), lambda c, h: (h, c))
    own_spec = pl.BlockSpec((1, HD, length), lambda c, h: (c, h, 0))
    return pl.pallas_call(
        functools.partial(attend_kernel, block=length),
        grid=(clips, heads),
        in_specs=[
            pl.BlockSpec(memory_space=pltpu.SMEM),
            head_spec(0),
            head_spec(1),
            head_spec(2),
            cap_spec,
            cap_spec,
        ],
        out_specs=[
            pl.BlockSpec((length // half, HD, half), lambda c, h: (0, h, c)),
            own_spec,
            own_spec,
            pl.BlockSpec((1, 1, 1, length), lambda c, h: (c, h, 0, 0)),
        ],
        out_shape=[
            jax.ShapeDtypeStruct((length // half, heads * HD, clips * half), BF16),
            jax.ShapeDtypeStruct((clips, heads * HD, length), F32),
            jax.ShapeDtypeStruct((clips, heads * HD, length), F32),
            jax.ShapeDtypeStruct((clips, heads, 1, length), F32),
        ],
        compiler_params=pltpu.CompilerParams(vmem_limit_bytes=VMEM_BYTES),
        cost_estimate=pl.CostEstimate(
            flops=4 * clips * heads * length * length * HD * 4,
            bytes_accessed=clips * heads * length * HD * 20,
            transcendentals=clips * heads * length * length,
        ),
    )(gate, qkv, qkv, qkv, cap_key, cap_value)


def attend_back_kernel(
    gate_ref,
    q_ref,
    k_ref,
    v_ref,
    ck_ref,
    cv_ref,
    grad_ref,
    self_ref,
    cross_ref,
    log_ref,
    raw_q_ref,
    raw_k_ref,
    cos_ref,
    sin_ref,
    grads_ref,
    cap_ref,
    gate_grad_ref,
    key_acc,
    value_acc,
    *,
    block,
):
    length = q_ref.shape[2]
    half = grad_ref.shape[2]
    score_scale = HD**-0.5
    gate = gate_ref[pl.program_id(1)]
    keys, values = k_ref[0], v_ref[0]
    keys_turned, values_turned = jnp.transpose(keys), jnp.transpose(values)
    cap_key, cap_value = ck_ref[...], cv_ref[...]
    cap_key_grad = jnp.zeros((HD, CAP), F32)
    cap_value_grad = jnp.zeros((HD, CAP), F32)
    for start in range(0, length, block):
        span = slice(start, start + block)
        query = q_ref[0, :, span]
        grad = jnp.concatenate(
            [grad_ref[start // half + piece] for piece in range(block // half)], axis=1
        )
        wide = grad.astype(F32)
        delta = jnp.sum(wide * self_ref[0, :, span], axis=0, keepdims=True)
        gate_grad_ref[0, 0, :, span] = jnp.sum(
            wide * cross_ref[0, :, span], axis=0, keepdims=True
        )
        probs = jnp.exp(dot(keys_turned, query) * score_scale - log_ref[0, 0, :, span])
        score_grad = (probs * (dot(values_turned, grad) - delta)).astype(BF16)
        value_part = jnp.transpose(dot(probs.astype(BF16), jnp.transpose(grad)))
        key_part = jnp.transpose(dot(score_grad, jnp.transpose(query)))
        if start == 0:
            value_acc[...] = value_part
            key_acc[...] = key_part
        else:
            value_acc[...] += value_part
            key_acc[...] += key_part
        query_grad = dot(keys, score_grad)
        cross_grad = (gate * wide).astype(BF16)
        cross_probs = cross_probabilities(cap_key, query)
        cross_dp = dot(cap_value, cross_grad, TN)
        cross_score = cross_probs * (
            cross_dp - jnp.sum(cross_probs * cross_dp, axis=0, keepdims=True)
        )
        cross_score = cross_score.astype(BF16)
        cap_value_grad += dot(cross_grad, cross_probs.astype(BF16), NT)
        cap_key_grad += dot(query, cross_score, NT)
        query_grad = (query_grad + dot(cap_key, cross_score)) * score_scale
        raw = raw_q_ref[0, :, span]
        inverse = head_inverse(raw)
        normed = raw * inverse
        turned = turn_back(query_grad, cos_ref[0, :, span], sin_ref[0, :, span])
        mean = jnp.mean(turned * normed, axis=0, keepdims=True)
        grads_ref[0, 0, :, span] = (inverse * (turned - normed * mean)).astype(BF16)
    for start in range(0, length, block):
        span = slice(start, start + block)
        raw = raw_k_ref[0, :, span]
        inverse = head_inverse(raw)
        normed = raw * inverse
        turned = turn_back(
            key_acc[:, span] * score_scale, cos_ref[0, :, span], sin_ref[0, :, span]
        )
        mean = jnp.mean(turned * normed, axis=0, keepdims=True)
        grads_ref[0, 1, :, span] = (inverse * (turned - normed * mean)).astype(BF16)
        grads_ref[0, 2, :, span] = value_acc[:, span].astype(BF16)
    cap_ref[0] = (cap_key_grad * score_scale).astype(BF16)
    cap_ref[1] = cap_value_grad.astype(BF16)


def attend_back(gate, qkv, cap_key, cap_value, grad, self_out, cross_out, log_total, raw, cos, sin):
    clips, columns, length = qkv.shape
    heads = columns // (3 * HD)
    half = length // grad.shape[0]
    head_spec = lambda first: pl.BlockSpec((1, HD, length), lambda c, h: (c, first * heads + h, 0))
    cap_spec = pl.BlockSpec((HD, CAP), lambda c, h: (h, c))
    table_spec = pl.BlockSpec((1, HD // 2, length), lambda c, h: (c, 0, 0))
    row_spec = pl.BlockSpec((1, 1, 1, length), lambda c, h: (c, h, 0, 0))
    return pl.pallas_call(
        functools.partial(attend_back_kernel, block=length // 2),
        grid=(clips, heads),
        in_specs=[
            pl.BlockSpec(memory_space=pltpu.SMEM),
            head_spec(0),
            head_spec(1),
            head_spec(2),
            cap_spec,
            cap_spec,
            pl.BlockSpec((length // half, HD, half), lambda c, h: (0, h, c)),
            head_spec(0),
            head_spec(0),
            row_spec,
            head_spec(0),
            head_spec(1),
            table_spec,
            table_spec,
        ],
        out_specs=[
            pl.BlockSpec((1, 3, HD, length), lambda c, h: (c, 0, h, 0)),
            pl.BlockSpec((2, HD, CAP), lambda c, h: (0, h, c)),
            row_spec,
        ],
        out_shape=[
            jax.ShapeDtypeStruct((clips, 3, heads * HD, length), BF16),
            jax.ShapeDtypeStruct((2, heads * HD, clips * CAP), BF16),
            jax.ShapeDtypeStruct((clips, heads, 1, length), F32),
        ],
        scratch_shapes=[pltpu.VMEM((HD, length), F32), pltpu.VMEM((HD, length), F32)],
        compiler_params=pltpu.CompilerParams(vmem_limit_bytes=VMEM_BYTES),
        cost_estimate=pl.CostEstimate(
            flops=10 * clips * heads * length * length * HD * 4,
            bytes_accessed=clips * heads * length * HD * 32,
            transcendentals=clips * heads * length * length,
        ),
    )(
        gate,
        qkv,
        qkv,
        qkv,
        cap_key,
        cap_value,
        grad,
        self_out,
        cross_out,
        log_total,
        raw,
        raw,
        cos,
        sin,
    )


def clip_sums(values):
    return jnp.sum(values.reshape(CLIPS, -1, values.shape[-1]), axis=1)


def split_heads(
    tokens,
    cotangent,
    captions,
    conditioning,
    clip_lens,
    w_ada,
    b_ada,
    w_query,
    w_key,
    w_value,
    w_out,
    gate_cross,
    w_text_key,
    w_text_value,
    w_gate,
    w_up,
    w_down,
):
    shard = lax.axis_index("sp")
    member = lax.axis_index("dp")
    size = lax.axis_size("sp")
    ring = Ring(size)
    rows = tokens.shape[1]
    half = rows // 2
    own_cols = D // size
    heads = HEADS // size
    ff = w_gate.shape[1]
    ff_rows = ff // size
    ff_part = ff_rows // N_DP
    k_rows = D // size
    k_part = k_rows // N_DP
    text_rows = w_text_key.shape[0]

    inputs = tokens[0].astype(F32)
    out_grad = cotangent[0].astype(F32)
    hidden_units = ff // N_DP

    def by_row(values):
        return jnp.repeat(values, half, axis=0)

    far = size // 2
    out_cols_part = D // N_DP
    table = ring.table
    tanh_gate = jnp.tanh(gate_cross)
    own_gate = lax.dynamic_slice(tanh_gate, (shard * heads,), (heads,))

    token_rows = pack_tokens(tokens[0], w_out)
    token_flow = Gather(ring, [token_rows])
    token_flow.send()
    cond_row = conditioning[0]
    cond_act = jax.nn.silu(cond_row).astype(BF16)
    mod_part = dot(cond_act, w_ada) + b_ada[None, :]
    flat_caption = captions[0].reshape(-1, size * text_rows)
    packed = exchange(pack_first(w_query, w_key, w_value, flat_caption, mod_part, token_rows))
    token_flow.live, packed = ordered((token_flow.live, packed))
    token_flow.keep()

    token_flow.send()
    quarter, caption_cols, modulation = unpack_first(
        packed, k_part, flat_caption.shape[0], text_rows, CLIPS, mod_part.shape[1]
    )
    caption_cols = caption_cols.reshape(-1, text_rows)
    quarter_far = across(quarter, 2)
    cap_terms = caption_terms(w_text_key, w_text_value, caption_cols)
    caption_all = lax.all_gather(caption_cols, "dp", axis=0, tiled=True)
    token_flow.live, quarter, quarter_far, modulation, cap_terms = ordered(
        (token_flow.live, quarter, quarter_far, modulation, cap_terms)
    )
    token_flow.keep()

    token_flow.send()
    quarters = [quarter, quarter_far, across(quarter, 1), across(quarter_far, 1)]
    w_qkv, w_turned = join_projections(ring, quarters)
    cap_terms = lax.psum_scatter(cap_terms, "sp", scatter_dimension=0, tiled=True)
    shift_one, scale_one, gate_one, shift_two, scale_two, gate_two = jnp.split(modulation, 6, axis=1)
    branch_grad = (by_row(gate_two) * out_grad).astype(BF16)
    branch_grads = lax.all_gather(branch_grad, "dp", axis=0, tiled=True)
    lane = jnp.arange(size * half, dtype=jnp.int32)
    mirrored = (size - 1 - lane // half) * half + lane % half
    freq = 10000.0 ** (-(jnp.arange(HD // 2, dtype=F32) * 2.0 / HD))
    angle = jnp.stack([lane, mirrored]).astype(F32)[:, None, :] * freq[None, :, None]
    cos, sin = jnp.cos(angle), jnp.sin(angle)
    unit_piece = unit_pieces(w_gate, w_up, w_down, quarter)
    token_flow.live, w_qkv, unit_piece, caption_all = ordered(
        (token_flow.live, w_qkv, unit_piece, caption_all)
    )
    token_flow.keep()

    def project_some(first, groups, before):
        return project(table, first, groups, shift_one, scale_one, w_qkv, cos, sin, before)

    token_flow.send()
    weight_flow = Gather(ring, [unit_piece])
    weight_flow.send()
    blocks = [b for _, b in token_flow.blocks]
    projected = project_some(0, blocks[:5], None)
    token_flow.live, weight_flow.live, projected, cap_terms = ordered(
        (token_flow.live, weight_flow.live, projected, cap_terms)
    )
    token_flow.keep()
    weight_flow.keep()

    weight_flow.send()
    out_cols = unpack_w_out(ring, token_flow, half)
    out_full = lax.all_gather(out_cols, "dp", axis=1, tiled=True)
    halves = token_flow.halves
    block_in, qkv, raw = project_some(
        5, [*blocks[5:], [halves[0][0], halves[1][0]]], projected
    )
    cap_heads = jnp.sum(cap_terms.astype(F32), axis=0).astype(BF16)
    cap_key, cap_value = cap_heads[:, : CLIPS * CAP], cap_heads[:, CLIPS * CAP :]
    mixed_blocks, self_out, cross_out, log_total = attend(own_gate, qkv, cap_key, cap_value, half)
    weight_flow.live, mixed_blocks, branch_grads = ordered(
        (weight_flow.live, mixed_blocks, branch_grads)
    )
    weight_flow.keep()

    mixed = exchange(mixed_blocks)
    inverse_one = inverse_rms(inputs)
    normed_one = inputs * inverse_one
    mixed, out_full = ordered((mixed, out_full))

    weight_flow.send()
    mixed = mixed.reshape(D, rows)
    attn_out = dot(mixed, out_full, TN)
    middle = inputs + by_row(gate_one) * attn_out
    inverse_two = inverse_rms(middle)
    normed_two = middle * inverse_two
    ffn_in = (normed_two * (1.0 + by_row(scale_two)) + by_row(shift_two)).astype(BF16)
    ffn_far = across(ffn_in, 2)
    weight_flow.live, ffn_in, ffn_far = ordered((weight_flow.live, ffn_in, ffn_far))
    weight_flow.keep()

    weight_flow.send()
    weight_flow.keep()
    pieces = [(shift, 0, arrays[0]) for shift, arrays in weight_flow.blocks]
    pieces += [(far, 0, weight_flow.halves[0][0])]
    pieces += [(far, k_rows // 2, weight_flow.halves[1][0])]
    hidden, unit_grads, ffn_own, ffn_next, down, ffn_ins = feed(
        ring, [ffn_in, ffn_far, across(ffn_in, 1), across(ffn_far, 1)], branch_grads, pieces
    )
    near = across(jnp.concatenate([ffn_own[rows:], ffn_next[rows:]]), 1)
    ffn_far = (ffn_next[:rows].astype(F32) + near[rows:].astype(F32)).astype(BF16)
    ffn_own = ffn_own[:rows].astype(F32) + near[:rows].astype(F32)
    ffn_own, ffn_far, hidden, unit_grads = ordered((ffn_own, ffn_far, hidden, unit_grads))

    ffn_far = across(ffn_far, 2)
    last = ring.spots[far - 1]
    unit_args = (ffn_ins, hidden, unit_grads, branch_grads)
    unit_back = unit_terms(table, ring.spots[far], 1, *unit_args, True)

    def send(values):
        return ring.send_up(values[:1]) + ring.send_down(values[1:])

    unit_back = send(unit_back)
    (d_units,) = unit_terms(table, last, last + 1, *unit_args, False)

    def add_step(step, terms, received):
        return add_received((2 * step, 2 * step + 1), terms, received)

    ffn_far, d_units, unit_back, hidden = ordered(
        (ffn_far, d_units, add_step(0, d_units, unit_back), hidden)
    )

    unit_back = send(unit_back)
    ffn_in_grad = ffn_own + ffn_far.astype(F32)
    middle_grad = out_grad + norm_back(
        ffn_in_grad * (1.0 + by_row(scale_two)), normed_two, inverse_two
    )
    attn_grad = (by_row(gate_one) * middle_grad).astype(BF16)
    mixed_grad = dot(out_full, attn_grad, NT).astype(BF16).reshape(size, own_cols, rows)
    mixed_grad, mixed, attn_grad, hidden = ordered((mixed_grad, mixed, attn_grad, hidden))

    head_grad = exchange(mixed_grad)
    branch_terms = dot(hidden, down).astype(BF16)
    grad_out = out_terms(mixed, attn_grad)
    sums = [
        clip_sums(middle_grad * attn_out),
        clip_sums(ffn_in_grad),
        clip_sums(ffn_in_grad * normed_two),
    ]
    head_grad, grad_out, branch_terms, sums = ordered((head_grad, grad_out, branch_terms, sums))

    out_sum = lax.psum_scatter(grad_out, "dp", scatter_dimension=0, tiled=True)
    out_home = lax.psum_scatter(out_sum[0], "sp", scatter_dimension=0, tiled=True)
    grads, cap_grads, gate_rows = attend_back(
        own_gate, qkv, cap_key, cap_value, head_grad, self_out, cross_out, log_total, raw, cos, sin
    )
    grads = grads.reshape(CLIPS, 3 * own_cols, size * half)
    token_back = token_terms(table, ring.spots[far], 1, grads, w_turned, True)
    unit_back, grads, cap_grads, token_back, branch_terms = ordered(
        (unit_back, grads, cap_grads, token_back, branch_terms)
    )

    token_back = send(token_back)
    branch = lax.psum_scatter(branch_terms, "dp", scatter_dimension=0, tiled=True)
    unit_back = send(add_step(1, d_units, unit_back))
    (terms,) = token_terms(table, last, last + 1, grads, w_turned, False)
    qkv_terms = head_weight_terms(ring, block_in, grads)
    cap_all = jnp.transpose(cap_grads, (1, 0, 2)).reshape(own_cols, 2 * CLIPS * CAP)
    cap_all = gather_small(cap_all, "sp").reshape(D, 2 * CLIPS * CAP)
    token_back, unit_back, qkv_terms, cap_all = ordered(
        (add_step(0, terms, token_back), add_step(2, d_units, unit_back), qkv_terms, cap_all)
    )

    token_back = send(token_back)
    unit_back = send(unit_back)
    qkv_own, qkv_far = sum_packs_near(qkv_terms)
    qkv_far = across(qkv_far, 2)
    cap_far = across(cap_all, 2)
    token_back, unit_back, qkv_own, qkv_far, cap_all, cap_far = ordered(
        (add_step(1, terms, token_back), unit_back, qkv_own, qkv_far, cap_all, cap_far)
    )

    token_back = send(token_back)
    unit_home = add_home(d_units, unit_back)
    unit_far = across(unit_home, 2)
    qkv_home = exchange((qkv_own + qkv_far.astype(F32)).astype(BF16))
    cap_blocks = [cap_all, cap_far, across(cap_all, 1), across(cap_far, 1)]
    token_back, unit_home, unit_far, qkv_home, cap_blocks, branch = ordered(
        (add_step(2, terms, token_back), unit_home, unit_far, qkv_home, cap_blocks, branch)
    )
    cap_all = cap_blocks[0]

    token_back = send(token_back)
    qkv_far = across(qkv_home, 2)
    caption_grad = dot(cap_all[:, : CLIPS * CAP], w_text_key, (((0,), (1,)), ((), ()))) + dot(
        cap_all[:, CLIPS * CAP :], w_text_value, (((0,), (1,)), ((), ()))
    )
    caption_grad = caption_grad.astype(BF16).reshape(CLIPS, size, -1, text_rows)
    caption_grad = jnp.transpose(caption_grad, (1, 0, 2, 3))
    d_text_key, d_text_value = text_grads(ring, caption_all, cap_blocks)
    shape = lambda *dims: jax.ShapeDtypeStruct(dims, F32)
    unit_blocks = [unit_home, unit_far, across(unit_home, 1), across(unit_far, 1)]
    d_gate_w, d_up_w, d_down = place(
        ring, place_units, unit_blocks, [shape(k_rows, ff), shape(k_rows, ff), shape(ff_rows, D)]
    )
    result = (middle + by_row(gate_two) * branch.astype(F32)).astype(BF16)
    sums = [*sums, clip_sums(out_grad * branch.astype(F32))]
    token_back, sums, qkv_home, qkv_far, out_home, result, d_down, caption_grad = ordered(
        (token_back, sums, qkv_home, qkv_far, out_home, result, d_down, caption_grad)
    )

    inputs_grad, own_sums = finish_tokens(terms, token_back, middle_grad, tokens[0], scale_one)

    mod_terms = jnp.concatenate([own_sums, *sums], axis=1)
    mod_terms = jnp.transpose(mod_terms.reshape(CLIPS, size, -1), (1, 0, 2))
    gate_own = jnp.sum(gate_rows, axis=(2, 3))
    gate_own = jnp.broadcast_to(gate_own[None], (size, CLIPS, heads))
    mod_terms = jnp.concatenate([mod_terms, gate_own], axis=2)
    mod_terms, qkv_home, qkv_far, out_home = ordered((mod_terms, qkv_home, qkv_far, out_home))

    arrived, caption_grad = ordered((exchange(mod_terms), caption_grad))
    qkv_blocks = [qkv_home, qkv_far, across(qkv_home, 1), across(qkv_far, 1)]
    out_blocks = gather_packs(out_home)

    own_mod = w_ada.shape[1]
    mod_low = jnp.sum(arrived[:, :, :own_mod], axis=0).astype(BF16)
    gate_all = jnp.transpose(arrived[:, :, own_mod:], (1, 0, 2)).reshape(CLIPS, HEADS)
    cond_part = dot(mod_low, w_ada, NT)
    cond_sum = jnp.sum(gather_small(cond_part, "sp"), axis=0)
    sigmoid_cond = jax.nn.sigmoid(cond_row)
    cond_grad = cond_sum * sigmoid_cond * (1.0 + cond_row * (1.0 - sigmoid_cond))
    both = jnp.concatenate([cond_act.astype(F32), mod_low.astype(F32), gate_all], axis=1)
    both_all = gather_small(both, "dp").reshape(N_DP * CLIPS, -1)
    cond_size = cond_act.shape[1]
    cond_all = both_all[:, :cond_size].astype(BF16)
    mod_all = both_all[:, cond_size : cond_size + own_mod].astype(BF16)
    d_ada = dot(cond_all, mod_all, TN)
    d_bias = jnp.sum(mod_all.astype(F32), axis=0)
    d_gate_cross = jnp.sum(both_all[:, cond_size + own_mod :], axis=0) * (
        1.0 - tanh_gate * tanh_gate
    )

    caption_grad = exchange(caption_grad)
    caption_grad = (
        jnp.transpose(caption_grad, (1, 2, 0, 3)).reshape(CLIPS, -1, size * text_rows).astype(F32)
    )

    (d_out,) = place(ring, place_columns, out_blocks, [shape(k_rows, D)])
    d_query, d_key, d_value = place(ring, place_heads, qkv_blocks, [shape(k_rows, D)] * 3)
    return (
        result[None],
        inputs_grad[None],
        caption_grad[None],
        cond_grad[None],
        d_ada,
        d_bias,
        d_query,
        d_key,
        d_value,
        d_out,
        d_gate_cross,
        d_text_key,
        d_text_value,
        d_gate_w,
        d_up_w,
        d_down,
    )


def layer(*arrays):
    tokens, clip_lens = arrays[0], arrays[4]
    size = lax.axis_size("sp")
    pack = tokens.shape[1] * size
    even = HEADS % size == 0 and size % 2 == 0 and size >= 4
    fixed = pack == clip_lens.shape[1] * MIN_CLIP and tokens.shape[1] % 256 == 0
    if even and fixed and lax.axis_size("dp") == N_DP:
        return split_heads(*arrays)
    return local(*arrays)


def solution(mesh):
    return jax.shard_map(
        layer,
        mesh=mesh,
        in_specs=(
            P("dp", "sp", None),
            P("dp", "sp", None),
            P("dp", None, "sp", None),
            P("dp", None, None),
            P("dp", None),
            P(None, "sp"),
            P("sp"),
            P("sp", None),
            P("sp", None),
            P("sp", None),
            P("sp", None),
            P(),
            P("sp", None),
            P("sp", None),
            P("sp", None),
            P("sp", None),
            P("sp", None),
        ),
        out_specs=(
            P("dp", "sp", None),
            P("dp", "sp", None),
            P("dp", None, "sp", None),
            P("dp", None, None),
            P(None, "sp"),
            P("sp"),
            P("sp", None),
            P("sp", None),
            P("sp", None),
            P("sp", None),
            P(),
            P("sp", None),
            P("sp", None),
            P("sp", None),
            P("sp", None),
            P("sp", None),
        ),
        check_vma=False,
    )
```

```python
import functools

import jax
import jax.numpy as jnp
from jax import lax
from jax.experimental import pallas as pl
from jax.experimental.pallas import tpu as pltpu
from jax.sharding import PartitionSpec as P

D = 1536
HEADS = 24
HD = 64
TEXT = 4096
CAP = 128
CLIPS = 2


EPSILON = 1e-06
MASKED = -1e30
HIGHEST = lax.Precision.HIGHEST


def rope_tables(positions):
    half_width = HD // 2
    freq = 10000.0 ** (-(jnp.arange(half_width, dtype=jnp.float32) * 2.0 / HD))
    angle = positions.astype(jnp.float32)[:, None] * freq[None, :]
    return (jnp.cos(angle)[:, None, :], jnp.sin(angle)[:, None, :])


def rotate(values, cos_table, sin_table):
    half_width = values.shape[-1] // 2
    first_half = values[..., :half_width]
    second_half = values[..., half_width:]
    return jnp.concatenate(
        [
            first_half * cos_table - second_half * sin_table,
            first_half * sin_table + second_half * cos_table,
        ],
        axis=-1,
    )


def rotate_back(grads, cos_table, sin_table):
    half_width = grads.shape[-1] // 2
    first_half = grads[..., :half_width]
    second_half = grads[..., half_width:]
    return jnp.concatenate(
        [
            first_half * cos_table + second_half * sin_table,
            second_half * cos_table - first_half * sin_table,
        ],
        axis=-1,
    )


def inverse_rms(values):
    return lax.rsqrt(jnp.mean(values * values, axis=-1, keepdims=True) + EPSILON)


def norm_back(grads, normed, inverse):
    return inverse * (grads - normed * jnp.mean(grads * normed, axis=-1, keepdims=True))


def per_clip(select, values):
    return jnp.einsum("tc,td->cd", select, values, precision=HIGHEST)


def local(
    tokens,
    cotangent,
    captions,
    conditioning,
    clip_lens,
    w_ada,
    b_ada,
    w_query,
    w_key,
    w_value,
    w_out,
    gate_cross,
    w_text_key,
    w_text_value,
    w_gate,
    w_up,
    w_down,
):
    shard = lax.axis_index("sp")
    cycle_size = lax.axis_size("sp")
    tok_rows = tokens.shape[1]
    half_rows = tok_rows // 2
    score_scale = HD ** (-0.5)
    row_index = jnp.arange(tok_rows, dtype=jnp.int32)
    logical_block = jnp.where(row_index < half_rows, shard, 2 * cycle_size - 1 - shard)
    logical = logical_block * half_rows + row_index % half_rows
    lengths = clip_lens[0]
    clip_ends = jnp.cumsum(lengths)
    clip_starts = clip_ends - lengths
    clip_index = 0
    segment = (logical >= clip_ends[clip_index]).astype(jnp.int32)
    offset = jnp.zeros((tok_rows,), jnp.int32)
    for clip_index in range(CLIPS):
        offset = offset + jnp.where(segment == clip_index, clip_starts[clip_index], 0)
    positions = logical - offset
    inputs = tokens[0].astype(jnp.float32)
    cond_row = conditioning[0]
    cond_act = jax.nn.silu(cond_row).astype(jnp.bfloat16)
    mod_part = jnp.dot(cond_act, w_ada, preferred_element_type=jnp.float32) + b_ada[None, :]
    modulation = lax.all_gather(mod_part, "sp", axis=1, tiled=True)
    select = (segment[:, None] == jnp.arange(CLIPS, dtype=jnp.int32)[None, :]).astype(jnp.float32)
    per_token = jnp.dot(select, modulation, precision=HIGHEST)
    shift_one, scale_one, gate_one, shift_two, scale_two, gate_two = jnp.split(per_token, 6, axis=1)
    weights_full = (
        lax.all_gather(w_query, "sp", axis=0, tiled=True),
        lax.all_gather(w_key, "sp", axis=0, tiled=True),
        lax.all_gather(w_value, "sp", axis=0, tiled=True),
        lax.all_gather(w_out, "sp", axis=0, tiled=True),
        lax.all_gather(w_gate, "sp", axis=0, tiled=True),
        lax.all_gather(w_up, "sp", axis=0, tiled=True),
        lax.all_gather(w_down, "sp", axis=0, tiled=True),
        lax.all_gather(w_text_key, "sp", axis=0, tiled=True),
        lax.all_gather(w_text_value, "sp", axis=0, tiled=True),
    )
    (
        query_full,
        key_full,
        value_full,
        out_full,
        gate_full,
        up_full,
        down_full,
        text_key_full,
        text_value_full,
    ) = weights_full
    inverse_one = inverse_rms(inputs)
    normed_one = inputs * inverse_one
    block_in = (normed_one * (1.0 + scale_one) + shift_one).astype(jnp.bfloat16)
    cos_table, sin_table = rope_tables(positions)

    def project(weight):
        return jnp.dot(block_in, weight, preferred_element_type=jnp.float32).reshape(
            tok_rows, HEADS, HD
        )

    query_raw = project(query_full)
    inverse_query = inverse_rms(query_raw)
    query_normed = query_raw * inverse_query
    query_rot = rotate(query_normed, cos_table, sin_table).astype(jnp.bfloat16)
    key_raw = project(key_full)
    inverse_key = inverse_rms(key_raw)
    key_normed = key_raw * inverse_key
    key_rot = rotate(key_normed, cos_table, sin_table).astype(jnp.bfloat16)
    value_rows = project(value_full).astype(jnp.bfloat16)
    caption_feats = captions[0]
    flat_caption = caption_feats.reshape(-1, TEXT)
    cap_key_part = (
        jnp.dot(flat_caption, text_key_full, preferred_element_type=jnp.float32)
        .astype(jnp.bfloat16)
        .reshape(CLIPS, -1, D)
    )
    cap_value_part = (
        jnp.dot(flat_caption, text_value_full, preferred_element_type=jnp.float32)
        .astype(jnp.bfloat16)
        .reshape(CLIPS, -1, D)
    )
    cap_key_all, cap_value_all = (
        lax.all_gather(cap_key_part, "sp", axis=1, tiled=True),
        lax.all_gather(cap_value_part, "sp", axis=1, tiled=True),
    )
    cap_key_heads = cap_key_all.reshape(CLIPS * CAP, HEADS, HD)
    cap_value_heads = cap_value_all.reshape(CLIPS * CAP, HEADS, HD)
    caption_clip = jnp.arange(CLIPS * CAP, dtype=jnp.int32) // CAP
    run_max = jnp.full((HEADS, tok_rows), MASKED, jnp.float32)
    key_piece = lax.all_gather(key_rot, "sp", axis=0, tiled=True)
    value_piece = lax.all_gather(value_rows, "sp", axis=0, tiled=True)
    segment_piece = lax.all_gather(segment, "sp", axis=0, tiled=True)
    scores = (
        jnp.einsum("qhd,khd->hqk", query_rot, key_piece, preferred_element_type=jnp.float32)
        * score_scale
    )
    allowed = (segment[:, None] == segment_piece[None, :])[None]
    scores = jnp.where(allowed, scores, MASKED)
    new_max = jnp.maximum(run_max, jnp.max(scores, axis=-1))
    weights_exp = jnp.where(allowed, jnp.exp(scores - new_max[:, :, None]), 0.0)
    new_total = jnp.sum(weights_exp, axis=-1)
    new_acc = jnp.einsum(
        "hqk,khd->qhd",
        weights_exp.astype(jnp.bfloat16),
        value_piece,
        preferred_element_type=jnp.float32,
    )
    self_out = new_acc / jnp.transpose(new_total)[:, :, None]
    log_total = jnp.transpose(new_max + jnp.log(new_total))
    cross_scores = (
        jnp.einsum("qhd,khd->hqk", query_rot, cap_key_heads, preferred_element_type=jnp.float32)
        * score_scale
    )
    own_clip = (segment[:, None] == caption_clip[None, :])[None]
    cross_probs = jax.nn.softmax(jnp.where(own_clip, cross_scores, MASKED), axis=-1)
    cross_low = cross_probs.astype(jnp.bfloat16)
    cross_out = jnp.einsum(
        "hqk,khd->qhd", cross_low, cap_value_heads, preferred_element_type=jnp.float32
    )
    tanh_gate = jnp.tanh(gate_cross)
    mixed = (
        (self_out + tanh_gate[None, :, None] * cross_out).astype(jnp.bfloat16).reshape(tok_rows, D)
    )
    attn_out = jnp.dot(mixed, out_full, preferred_element_type=jnp.float32)
    middle = inputs + gate_one * attn_out
    inverse_two = inverse_rms(middle)
    normed_two = middle * inverse_two
    ffn_in = (normed_two * (1.0 + scale_two) + shift_two).astype(jnp.bfloat16)
    gate_proj = jnp.dot(ffn_in, gate_full, preferred_element_type=jnp.float32)
    up_proj = jnp.dot(ffn_in, up_full, preferred_element_type=jnp.float32)
    sigmoid_gate = jax.nn.sigmoid(gate_proj)
    silu_gate = jax.nn.silu(gate_proj)
    hidden = (silu_gate * up_proj).astype(jnp.bfloat16)
    branch = jnp.dot(hidden, down_full, preferred_element_type=jnp.float32)
    result = (middle + gate_two * branch).astype(jnp.bfloat16)
    out_grad = cotangent[0].astype(jnp.float32)
    branch_grad = (gate_two * out_grad).astype(jnp.bfloat16)
    hidden_grad = jnp.einsum(
        "td,fd->tf", branch_grad, down_full, preferred_element_type=jnp.float32
    )
    grad_down = jnp.einsum("tf,td->fd", hidden, branch_grad, preferred_element_type=jnp.float32)
    gate_grad = (
        hidden_grad * up_proj * sigmoid_gate * (1.0 + gate_proj * (1.0 - sigmoid_gate))
    ).astype(jnp.bfloat16)
    up_grad = (hidden_grad * silu_gate).astype(jnp.bfloat16)
    ffn_in_grad = jnp.einsum(
        "tf,df->td", gate_grad, gate_full, preferred_element_type=jnp.float32
    ) + jnp.einsum("tf,df->td", up_grad, up_full, preferred_element_type=jnp.float32)
    grad_gate_w = jnp.einsum("td,tf->df", ffn_in, gate_grad, preferred_element_type=jnp.float32)
    grad_up_w = jnp.einsum("td,tf->df", ffn_in, up_grad, preferred_element_type=jnp.float32)
    gate_two_tok = out_grad * branch
    scale_two_tok = ffn_in_grad * normed_two
    middle_grad = out_grad + norm_back(ffn_in_grad * (1.0 + scale_two), normed_two, inverse_two)
    attn_grad = (gate_one * middle_grad).astype(jnp.bfloat16)
    gate_one_tok = middle_grad * attn_out
    grad_out_w = jnp.einsum("td,te->de", mixed, attn_grad, preferred_element_type=jnp.float32)
    mixed_grad = jnp.einsum(
        "te,de->td", attn_grad, out_full, preferred_element_type=jnp.float32
    ).reshape(tok_rows, HEADS, HD)
    gate_cross_part = jnp.sum(mixed_grad * cross_out, axis=(0, 2)) * (1.0 - tanh_gate * tanh_gate)
    self_grad = mixed_grad.astype(jnp.bfloat16)
    cross_grad = (tanh_gate[None, :, None] * mixed_grad).astype(jnp.bfloat16)
    cross_dp = jnp.einsum(
        "qhd,khd->hqk", cross_grad, cap_value_heads, preferred_element_type=jnp.float32
    )
    cap_value_grad = jnp.einsum(
        "hqk,qhd->khd", cross_low, cross_grad, preferred_element_type=jnp.float32
    )
    cross_ds = (
        cross_probs * (cross_dp - jnp.sum(cross_probs * cross_dp, axis=-1, keepdims=True))
    ).astype(jnp.bfloat16)
    query_grad_cross = jnp.einsum(
        "hqk,khd->qhd", cross_ds, cap_key_heads, preferred_element_type=jnp.float32
    )
    cap_key_grad = (
        jnp.einsum("hqk,qhd->khd", cross_ds, query_rot, preferred_element_type=jnp.float32)
        * score_scale
    )
    row_delta = jnp.sum(self_grad.astype(jnp.float32) * self_out, axis=-1)
    query_piece = lax.all_gather(query_rot, "sp", axis=0, tiled=True)
    grad_piece = lax.all_gather(self_grad, "sp", axis=0, tiled=True)
    log_piece = lax.all_gather(log_total.astype(jnp.bfloat16), "sp", axis=0, tiled=True).astype(
        jnp.float32
    )
    delta_piece = lax.all_gather(row_delta.astype(jnp.bfloat16), "sp", axis=0, tiled=True).astype(
        jnp.float32
    )
    segment_piece = lax.all_gather(segment, "sp", axis=0, tiled=True)
    scores = (
        jnp.einsum("qhd,khd->hqk", query_piece, key_rot, preferred_element_type=jnp.float32)
        * score_scale
    )
    allowed = (segment_piece[:, None] == segment[None, :])[None]
    probs = jnp.where(allowed, jnp.exp(scores - jnp.transpose(log_piece)[:, :, None]), 0.0)
    value_acc = jnp.einsum(
        "hqk,qhd->khd", probs.astype(jnp.bfloat16), grad_piece, preferred_element_type=jnp.float32
    )
    prob_grad = jnp.einsum(
        "qhd,khd->hqk", grad_piece, value_rows, preferred_element_type=jnp.float32
    )
    score_grad = (probs * (prob_grad - jnp.transpose(delta_piece)[:, :, None])).astype(jnp.bfloat16)
    key_acc = jnp.einsum(
        "hqk,qhd->khd", score_grad, query_piece, preferred_element_type=jnp.float32
    )
    key_acc, value_acc = (key_acc, value_acc)
    key_piece = lax.all_gather(key_rot, "sp", axis=0, tiled=True)
    value_piece = lax.all_gather(value_rows, "sp", axis=0, tiled=True)
    segment_piece = lax.all_gather(segment, "sp", axis=0, tiled=True)
    scores = (
        jnp.einsum("qhd,khd->hqk", query_rot, key_piece, preferred_element_type=jnp.float32)
        * score_scale
    )
    allowed = (segment[:, None] == segment_piece[None, :])[None]
    probs = jnp.where(allowed, jnp.exp(scores - jnp.transpose(log_total)[:, :, None]), 0.0)
    prob_grad = jnp.einsum(
        "qhd,khd->hqk", self_grad, value_piece, preferred_element_type=jnp.float32
    )
    score_grad = (probs * (prob_grad - jnp.transpose(row_delta)[:, :, None])).astype(jnp.bfloat16)
    query_acc = jnp.einsum(
        "hqk,khd->qhd", score_grad, key_piece, preferred_element_type=jnp.float32
    )
    query_rot_grad = (query_acc + query_grad_cross) * score_scale
    key_rot_grad = key_acc * score_scale
    query_raw_grad = (
        norm_back(rotate_back(query_rot_grad, cos_table, sin_table), query_normed, inverse_query)
        .astype(jnp.bfloat16)
        .reshape(tok_rows, D)
    )
    key_raw_grad = (
        norm_back(rotate_back(key_rot_grad, cos_table, sin_table), key_normed, inverse_key)
        .astype(jnp.bfloat16)
        .reshape(tok_rows, D)
    )
    value_raw_grad = value_acc.astype(jnp.bfloat16).reshape(tok_rows, D)
    block_in_grad = (
        jnp.einsum("te,de->td", query_raw_grad, query_full, preferred_element_type=jnp.float32)
        + jnp.einsum("te,de->td", key_raw_grad, key_full, preferred_element_type=jnp.float32)
        + jnp.einsum("te,de->td", value_raw_grad, value_full, preferred_element_type=jnp.float32)
    )
    grad_query_w = jnp.einsum(
        "td,te->de", block_in, query_raw_grad, preferred_element_type=jnp.float32
    )
    grad_key_w = jnp.einsum("td,te->de", block_in, key_raw_grad, preferred_element_type=jnp.float32)
    grad_value_w = jnp.einsum(
        "td,te->de", block_in, value_raw_grad, preferred_element_type=jnp.float32
    )
    scale_one_tok = block_in_grad * normed_one
    inputs_grad = middle_grad + norm_back(
        block_in_grad * (1.0 + scale_one), normed_one, inverse_one
    )
    mod_grad_part = jnp.concatenate(
        [
            per_clip(select, block_in_grad),
            per_clip(select, scale_one_tok),
            per_clip(select, gate_one_tok),
            per_clip(select, ffn_in_grad),
            per_clip(select, scale_two_tok),
            per_clip(select, gate_two_tok),
        ],
        axis=1,
    )
    cap_key_home, cap_value_home, mod_grad = (
        lax.psum_scatter(
            cap_key_grad.reshape(CLIPS, CAP, D).astype(jnp.bfloat16),
            "sp",
            scatter_dimension=1,
            tiled=True,
        ).astype(jnp.float32),
        lax.psum_scatter(
            cap_value_grad.reshape(CLIPS, CAP, D).astype(jnp.bfloat16),
            "sp",
            scatter_dimension=1,
            tiled=True,
        ).astype(jnp.float32),
        lax.psum_scatter(
            mod_grad_part.astype(jnp.bfloat16), "sp", scatter_dimension=1, tiled=True
        ).astype(jnp.float32),
    )
    cap_key_low = cap_key_home.astype(jnp.bfloat16)
    cap_value_low = cap_value_home.astype(jnp.bfloat16)
    mod_low = mod_grad.astype(jnp.bfloat16)
    caption_grad = jnp.einsum(
        "cpd,ed->cpe", cap_key_low, text_key_full, preferred_element_type=jnp.float32
    ) + jnp.einsum(
        "cpd,ed->cpe", cap_value_low, text_value_full, preferred_element_type=jnp.float32
    )
    grad_text_key = jnp.einsum(
        "cpe,cpd->ed", caption_feats, cap_key_low, preferred_element_type=jnp.float32
    )
    grad_text_value = jnp.einsum(
        "cpe,cpd->ed", caption_feats, cap_value_low, preferred_element_type=jnp.float32
    )
    grad_ada = jnp.einsum("cu,cv->uv", cond_act, mod_low, preferred_element_type=jnp.float32)
    grad_bias = jnp.sum(mod_low.astype(jnp.float32), axis=0)
    cond_part = jnp.einsum("cv,uv->cu", mod_low, w_ada, preferred_element_type=jnp.float32)
    cond_sum, gate_sum = lax.psum((cond_part, gate_cross_part), "sp")
    sigmoid_cond = jax.nn.sigmoid(cond_row)
    cond_grad = cond_sum * sigmoid_cond * (1.0 + cond_row * (1.0 - sigmoid_cond))
    home = (
        lax.psum_scatter(
            grad_query_w.astype(jnp.bfloat16), "sp", scatter_dimension=0, tiled=True
        ).astype(jnp.float32),
        lax.psum_scatter(
            grad_key_w.astype(jnp.bfloat16), "sp", scatter_dimension=0, tiled=True
        ).astype(jnp.float32),
        lax.psum_scatter(
            grad_value_w.astype(jnp.bfloat16), "sp", scatter_dimension=0, tiled=True
        ).astype(jnp.float32),
        lax.psum_scatter(
            grad_out_w.astype(jnp.bfloat16), "sp", scatter_dimension=0, tiled=True
        ).astype(jnp.float32),
        lax.psum_scatter(
            grad_gate_w.astype(jnp.bfloat16), "sp", scatter_dimension=0, tiled=True
        ).astype(jnp.float32),
        lax.psum_scatter(
            grad_up_w.astype(jnp.bfloat16), "sp", scatter_dimension=0, tiled=True
        ).astype(jnp.float32),
        lax.psum_scatter(
            grad_down.astype(jnp.bfloat16), "sp", scatter_dimension=0, tiled=True
        ).astype(jnp.float32),
        lax.psum_scatter(
            grad_text_key.astype(jnp.bfloat16), "sp", scatter_dimension=0, tiled=True
        ).astype(jnp.float32),
        lax.psum_scatter(
            grad_text_value.astype(jnp.bfloat16), "sp", scatter_dimension=0, tiled=True
        ).astype(jnp.float32),
    )
    totals = (
        lax.psum(home[0].astype(jnp.bfloat16), "dp").astype(jnp.float32),
        lax.psum(home[1].astype(jnp.bfloat16), "dp").astype(jnp.float32),
        lax.psum(home[2].astype(jnp.bfloat16), "dp").astype(jnp.float32),
        lax.psum(home[3].astype(jnp.bfloat16), "dp").astype(jnp.float32),
        lax.psum(home[4].astype(jnp.bfloat16), "dp").astype(jnp.float32),
        lax.psum(home[5].astype(jnp.bfloat16), "dp").astype(jnp.float32),
        lax.psum(home[6].astype(jnp.bfloat16), "dp").astype(jnp.float32),
        lax.psum(home[7].astype(jnp.bfloat16), "dp").astype(jnp.float32),
        lax.psum(home[8].astype(jnp.bfloat16), "dp").astype(jnp.float32),
        lax.psum(grad_ada.astype(jnp.bfloat16), "dp").astype(jnp.float32),
        lax.psum(grad_bias.astype(jnp.bfloat16), "dp").astype(jnp.float32),
        lax.psum(gate_sum.astype(jnp.bfloat16), "dp").astype(jnp.float32),
    )
    (
        d_query,
        d_key,
        d_value,
        d_out,
        d_gate_w,
        d_up_w,
        d_down_w,
        d_text_key,
        d_text_value,
        d_ada,
        d_bias,
        d_gate_cross,
    ) = totals
    return (
        result[None],
        inputs_grad[None],
        caption_grad[None],
        cond_grad[None],
        d_ada,
        d_bias,
        d_query,
        d_key,
        d_value,
        d_out,
        d_gate_cross,
        d_text_key,
        d_text_value,
        d_gate_w,
        d_up_w,
        d_down_w,
    )


MIN_CLIP = 1024
N_DP = 4
OFFSETS = (0, 2, 1, 3)
VMEM_BYTES = 62 * 1024 * 1024
NT = (((1,), (1,)), ((), ()))
TN = (((0,), (0,)), ((), ()))
F32 = jnp.float32
BF16 = jnp.bfloat16


def dot(left, right, dims=(((1,), (0,)), ((), ()))):
    return lax.dot_general(left, right, dims, preferred_element_type=F32)


def ordered(tree):
    arrays, shape = jax.tree.flatten(tree)
    spec = pl.BlockSpec(memory_space=pl.ANY)
    out = pl.pallas_call(
        lambda *refs: None,
        in_specs=[spec] * len(arrays),
        out_specs=[spec] * len(arrays),
        out_shape=[jax.ShapeDtypeStruct(a.shape, a.dtype) for a in arrays],
        input_output_aliases={i: i for i in range(len(arrays))},
        compiler_params=pltpu.CompilerParams(vmem_limit_bytes=VMEM_BYTES),
        cost_estimate=pl.CostEstimate(flops=0, bytes_accessed=0, transcendentals=0),
    )(*arrays)
    return jax.tree.unflatten(shape, out)


class Ring:
    def __init__(self, size):
        self.size = size
        self.far = size // 2
        self.order = list(range(0, size, 2)) + list(range(size - 1, 0, -2))
        self.up = [(self.order[i], self.order[(i + 1) % size]) for i in range(size)]
        self.down = [(b, a) for a, b in self.up]
        shifts = [0]
        for step in range(1, self.far):
            shifts += [-step, step]
        shifts += [self.far]
        self.spots = {shift: i for i, shift in enumerate(shifts)}
        rows = [None] * size
        for spot, device in enumerate(self.order):
            devices = [self.order[(spot + shift) % size] for shift in shifts]
            rows[device] = [devices + [m ^ offset for offset in OFFSETS] for m in range(N_DP)]
        table = jnp.array(rows, jnp.int32).reshape(size * N_DP, -1)
        index = lax.axis_index("sp") * N_DP + lax.axis_index("dp")
        self.table = lax.dynamic_index_in_dim(table, index, 0, False)

    def send_up(self, values):
        return [lax.ppermute(v, "sp", self.up) for v in values]

    def send_down(self, values):
        return [lax.ppermute(v, "sp", self.down) for v in values]


class Gather:
    def __init__(self, ring, own):
        self.ring, self.own = ring, own
        self.step, self.live = 0, (own, own)
        self.blocks = [(0, own)]

    def send(self):
        ring = self.ring
        self.step += 1
        above, below = self.live
        if self.step == ring.far:
            above = [v[: v.shape[0] // 2] for v in above]
            below = [v[v.shape[0] // 2 :] for v in below]
        self.live = ring.send_up(above), ring.send_down(below)

    def keep(self):
        above, below = self.live
        if self.step == self.ring.far:
            self.halves = above, below
        else:
            self.blocks += [(-self.step, above), (self.step, below)]


def across(value, bit):
    return lax.ppermute(value, "dp", [(i, i ^ bit) for i in range(N_DP)])


def gather_packs(value):
    far = across(value, 2)
    return [value, far, across(value, 1), across(far, 1)]


def sum_packs_near(parts):
    own = parts[0].astype(F32) + across(parts[2].astype(BF16), 1).astype(F32)
    far = parts[1].astype(F32) + across(parts[3].astype(BF16), 1).astype(F32)
    return own, far.astype(BF16)


def gather_small(value, axis_name):
    size = lax.axis_size(axis_name)
    return lax.all_to_all(
        jnp.broadcast_to(value[None], (size,) + value.shape), axis_name, 0, 0, tiled=True
    )


def exchange(value):
    return lax.all_to_all(value, "sp", 0, 0, tiled=True)


def aligned(index, by):
    return index if isinstance(index, int) else pl.multiple_of(index, by)


def place(ring, write, blocks, shapes):
    first = ring.size
    listed = isinstance(blocks, list)
    arrays = blocks if listed else [blocks]

    def kernel(index_ref, *refs):
        for i in range(N_DP):
            if listed:
                write(refs[i], index_ref[first + i], refs[N_DP:])
            else:
                write(refs[0].at[i], i, refs[1:])

    vmem = pl.BlockSpec(memory_space=pltpu.VMEM)
    return pl.pallas_call(
        kernel,
        in_specs=[pl.BlockSpec(memory_space=pltpu.SMEM)] + [vmem] * len(arrays),
        out_specs=[vmem] * len(shapes),
        out_shape=shapes,
        compiler_params=pltpu.CompilerParams(vmem_limit_bytes=VMEM_BYTES),
        cost_estimate=pl.CostEstimate(
            flops=0,
            bytes_accessed=sum(s.size * s.dtype.itemsize for s in [*arrays, *shapes]),
            transcendentals=0,
        ),
    )(ring.table, *arrays)


def place_units(block_ref, index, out_refs):
    columns = block_ref.shape[1] - FOLD
    groups = columns // (2 * 128)
    for i, out_ref in enumerate(out_refs[:2]):
        for group in range(groups):
            start = unit_column(i, group)
            spot = pl.ds(aligned((group * N_DP + index) * 128, 128), 128)
            out_ref[:, spot] = block_ref[:, start : start + 128].astype(out_ref.dtype)
    for row, column, there_row, there_column, height, wide in folded():
        spot = pl.ds(aligned(index * 128 + row, 64), height)
        out_refs[2][spot, column : column + wide] = block_ref[
            there_row : there_row + height,
            columns + there_column : columns + there_column + wide,
        ].astype(out_refs[2].dtype)


def place_heads(block_ref, index, out_refs):
    groups, rows, width = block_ref.shape
    width = width // len(out_refs)
    spot = pl.ds(aligned(index * rows, rows), rows)
    for i, out_ref in enumerate(out_refs):
        for group in range(0, groups, 2):
            pair = [
                block_ref[group + k, :, i * width : (i + 1) * width].astype(F32) for k in range(2)
            ]
            columns = slice(group * width, (group + 2) * width)
            out_ref[spot, columns] = jnp.concatenate(pair, axis=1).astype(out_ref.dtype)


def join_projections(ring, blocks):
    size, part, columns = blocks[0].shape
    width = size * part * N_DP

    def kernel(index_ref, *refs):
        out_ref, turned_ref = refs[N_DP:]
        for i in range(N_DP):
            for device in range(size):
                start = (device * N_DP + index_ref[size + i]) * part
                out_ref[pl.ds(aligned(start, part), part), :] = refs[i][device]
        turned_ref[...] = jnp.transpose(out_ref[...])

    vmem = pl.BlockSpec(memory_space=pltpu.VMEM)
    return pl.pallas_call(
        kernel,
        in_specs=[pl.BlockSpec(memory_space=pltpu.SMEM)] + [vmem] * N_DP,
        out_specs=[vmem] * 2,
        out_shape=[
            jax.ShapeDtypeStruct((width, columns), BF16),
            jax.ShapeDtypeStruct((columns, width), BF16),
        ],
        compiler_params=pltpu.CompilerParams(vmem_limit_bytes=VMEM_BYTES),
        cost_estimate=pl.CostEstimate(
            flops=0, bytes_accessed=6 * width * columns, transcendentals=0
        ),
    )(ring.table, *blocks)


def caption_terms(w_key, w_value, captions):
    features, width = w_key.shape
    tokens = captions.shape[0]
    size = lax.axis_size("sp")
    columns = width // size

    def kernel(key_ref, value_ref, cap_ref, out_ref):
        for i, ref in enumerate((key_ref, value_ref)):
            total = jnp.transpose(dot(cap_ref[...], ref[...])).astype(BF16)
            for device in range(size):
                out_ref[device, :, i * tokens : (i + 1) * tokens] = total[
                    device * columns : (device + 1) * columns
                ]

    vmem = pl.BlockSpec(memory_space=pltpu.VMEM)
    return pl.pallas_call(
        kernel,
        in_specs=[vmem] * 3,
        out_specs=vmem,
        out_shape=jax.ShapeDtypeStruct((size, columns, 2 * tokens), BF16),
        compiler_params=pltpu.CompilerParams(vmem_limit_bytes=VMEM_BYTES),
        cost_estimate=pl.CostEstimate(
            flops=4 * tokens * features * width,
            bytes_accessed=4 * (features + tokens) * width,
            transcendentals=0,
        ),
    )(w_key, w_value, captions)


def text_grads(ring, captions, grads):
    width, columns = grads[0].shape
    tokens = columns // 2
    features = captions.shape[1]
    size = ring.size

    def kernel(index_ref, cap_ref, *refs):
        caps = [
            jnp.transpose(cap_ref[pl.ds(aligned(index_ref[size + i] * tokens, tokens), tokens), :])
            for i in range(N_DP)
        ]
        for which, out_ref in enumerate(refs[N_DP:]):
            total = None
            for i in range(N_DP):
                grad = refs[i][:, which * tokens : (which + 1) * tokens]
                term = dot(caps[i], jnp.transpose(grad))
                total = term if total is None else total + term
            out_ref[...] = total

    vmem = pl.BlockSpec(memory_space=pltpu.VMEM)
    return pl.pallas_call(
        kernel,
        in_specs=[pl.BlockSpec(memory_space=pltpu.SMEM)] + [vmem] * (1 + N_DP),
        out_specs=[vmem] * 2,
        out_shape=[jax.ShapeDtypeStruct((features, width), F32)] * 2,
        compiler_params=pltpu.CompilerParams(vmem_limit_bytes=VMEM_BYTES),
        cost_estimate=pl.CostEstimate(
            flops=4 * N_DP * tokens * features * width,
            bytes_accessed=8 * features * width + 4 * N_DP * tokens * width,
            transcendentals=0,
        ),
    )(ring.table, captions, *grads)


def out_terms(mixed, grad):
    width, rows = mixed.shape
    columns = width // N_DP

    def kernel(mixed_ref, grad_ref, out_ref):
        out_ref[0] = dot(mixed_ref[...], grad_ref[...]).astype(BF16)

    return pl.pallas_call(
        kernel,
        grid=(N_DP,),
        in_specs=[
            pl.BlockSpec((width, rows), lambda i: (0, 0)),
            pl.BlockSpec((rows, columns), lambda i: (0, i)),
        ],
        out_specs=pl.BlockSpec((1, width, columns), lambda i: (i, 0, 0)),
        out_shape=jax.ShapeDtypeStruct((N_DP, width, columns), BF16),
        compiler_params=pltpu.CompilerParams(vmem_limit_bytes=VMEM_BYTES),
        cost_estimate=pl.CostEstimate(
            flops=2 * width * width * rows, bytes_accessed=2 * width * width, transcendentals=0
        ),
    )(mixed, grad)


def finish_tokens(terms, received, middle_grad, tokens, scale):
    rows, width = tokens.shape
    half = rows // CLIPS
    last = terms.shape[0] // rows - 1

    def kernel(terms_ref, above_ref, below_ref, middle_ref, x_ref, scale_ref, out_ref, sums_ref):
        for clip in range(CLIPS):
            span = slice(clip * half, (clip + 1) * half)
            grad = (
                terms_ref[span].astype(F32) + above_ref[span].astype(F32) + below_ref[span].astype(F32)
            )
            x = x_ref[span].astype(F32)
            inverse = lax.rsqrt(jnp.mean(x * x, axis=-1, keepdims=True) + EPSILON)
            normed = x * inverse
            scaled = grad * (1.0 + scale_ref[clip : clip + 1, :])
            mean = jnp.mean(scaled * normed, axis=-1, keepdims=True)
            out_ref[span] = middle_ref[span] + inverse * (scaled - normed * mean)
            sums_ref[clip : clip + 1, :width] = jnp.sum(grad, axis=0, keepdims=True)
            sums_ref[clip : clip + 1, width:] = jnp.sum(grad * normed, axis=0, keepdims=True)

    fixed = pl.BlockSpec((rows, width), lambda i: (0, 0))
    return pl.pallas_call(
        kernel,
        grid=(1,),
        in_specs=[pl.BlockSpec((rows, width), lambda i: (last, 0))]
        + [fixed] * 4
        + [pl.BlockSpec((CLIPS, width), lambda i: (0, 0))],
        out_specs=[fixed, pl.BlockSpec((CLIPS, 2 * width), lambda i: (0, 0))],
        out_shape=[
            jax.ShapeDtypeStruct((rows, width), F32),
            jax.ShapeDtypeStruct((CLIPS, 2 * width), F32),
        ],
        compiler_params=pltpu.CompilerParams(vmem_limit_bytes=VMEM_BYTES),
        cost_estimate=pl.CostEstimate(
            flops=0, bytes_accessed=16 * rows * width, transcendentals=0
        ),
    )(terms, *received, middle_grad, tokens, scale)


def place_columns(block_ref, index, out_refs):
    width = block_ref.shape[1]
    out_refs[0][:, pl.ds(aligned(index * width, 128), width)] = block_ref[...].astype(
        out_refs[0].dtype
    )


UNITS = 512


HELD = 32


def pack_tokens(tokens, w_out):
    rows, width = tokens.shape
    half = rows // 2
    columns = width // N_DP
    k_rows = w_out.shape[0]
    part = k_rows // N_DP
    member = jnp.reshape(lax.axis_index("dp"), (1,)).astype(jnp.int32)

    def kernel(member_ref, tokens_ref, w_ref, out_ref):
        spot = pl.ds(aligned(member_ref[0] * columns, 128), columns)
        for clip in range(CLIPS):
            start = clip * (half + HELD)
            out_ref[start : start + half] = tokens_ref[clip * half : (clip + 1) * half]
            count = min(part - clip * HELD, HELD)
            for group in range(N_DP):
                top = group * part + clip * HELD
                out_ref[
                    start + half : start + half + count, group * columns : (group + 1) * columns
                ] = w_ref[top : top + count, spot]
            if count < HELD:
                out_ref[start + half + count : start + half + HELD] = jnp.zeros(
                    (HELD - count, width), BF16
                )

    vmem = pl.BlockSpec(memory_space=pltpu.VMEM)
    return pl.pallas_call(
        kernel,
        in_specs=[pl.BlockSpec(memory_space=pltpu.SMEM), vmem, vmem],
        out_specs=vmem,
        out_shape=jax.ShapeDtypeStruct((rows + CLIPS * HELD, width), BF16),
        compiler_params=pltpu.CompilerParams(vmem_limit_bytes=VMEM_BYTES),
        cost_estimate=pl.CostEstimate(
            flops=0, bytes_accessed=6 * rows * width, transcendentals=0
        ),
    )(member, tokens, w_out)


def unpack_w_out(ring, flow, half):
    width = flow.own[0].shape[1]
    columns = width // N_DP
    k_rows = width // ring.size
    part = k_rows // N_DP
    block = (half + HELD) // HELD
    groups = [[arrays[0]] for _, arrays in flow.blocks]
    groups += [[flow.halves[0][0], flow.halves[1][0]]]
    spots = [ring.spots[shift] for shift, _ in flow.blocks] + [ring.spots[ring.far]]
    operands, specs = [], []
    for group in groups:
        for clip in range(CLIPS):
            operands.append(group[clip] if len(group) > 1 else group[0])
            index = block - 1 if len(group) > 1 else (clip + 1) * block - 1
            specs.append(pl.BlockSpec((HELD, width), lambda i, index=index: (index, 0)))

    def kernel(index_ref, *refs):
        for i, spot in enumerate(spots):
            for clip in range(CLIPS):
                count = min(part - clip * HELD, HELD)
                for group in range(N_DP):
                    top = index_ref[spot] * k_rows + group * part + clip * HELD
                    refs[-1][pl.ds(aligned(top, 16), count), :] = refs[CLIPS * i + clip][
                        :count, group * columns : (group + 1) * columns
                    ]

    return pl.pallas_call(
        kernel,
        grid=(1,),
        in_specs=[pl.BlockSpec(memory_space=pltpu.SMEM)] + specs,
        out_specs=pl.BlockSpec((width, columns), lambda i: (0, 0)),
        out_shape=jax.ShapeDtypeStruct((width, columns), BF16),
        compiler_params=pltpu.CompilerParams(vmem_limit_bytes=VMEM_BYTES),
        cost_estimate=pl.CostEstimate(
            flops=0, bytes_accessed=4 * width * columns, transcendentals=0
        ),
    )(ring.table, *operands)


def unit_pieces(w_gate, w_up, w_down, after):
    rows, columns = w_gate.shape
    groups = columns // (N_DP * 128)
    member = jnp.reshape(lax.axis_index("dp"), (1,)).astype(jnp.int32)
    first = 2 * groups * 128
    width = first + FOLD

    def kernel(member_ref, gate_ref, up_ref, down_ref, after_ref, out_ref):
        for i, ref in enumerate((gate_ref, up_ref)):
            for group in range(groups):
                spot = aligned((group * N_DP + member_ref[0]) * 128, 128)
                start = unit_column(i, group)
                out_ref[:, start : start + 128] = ref[:, pl.ds(spot, 128)]
        spot = aligned(member_ref[0] * 128, 128)
        for row, column, there_row, there_column, height, wide in folded():
            out_ref[there_row : there_row + height, first + there_column : first + there_column + wide] = (
                down_ref[pl.ds(aligned(spot + row, 32), height), column : column + wide]
            )

    vmem = pl.BlockSpec(memory_space=pltpu.VMEM)
    return pl.pallas_call(
        kernel,
        in_specs=[pl.BlockSpec(memory_space=pltpu.SMEM), vmem, vmem, vmem, pl.BlockSpec(memory_space=pl.ANY)],
        out_specs=vmem,
        out_shape=jax.ShapeDtypeStruct((rows, width), w_gate.dtype),
        compiler_params=pltpu.CompilerParams(vmem_limit_bytes=VMEM_BYTES),
        cost_estimate=pl.CostEstimate(
            flops=0, bytes_accessed=8 * rows * columns, transcendentals=0
        ),
    )(member, w_gate, w_up, w_down, after)


FOLD = 1024


def folded(low=0, high=192):
    spots = []
    if low < 128:
        end = min(high, 128)
        spots.append((low, 0, 0, 0, end - low, FOLD))
    if high > 128:
        start = max(low, 128) - 128
        count = high - 128 - start
        for side in range(2):
            spots.append(
                (64 * side + start, FOLD, 128 + start - low, 512 * side, count, 512)
            )
    return spots


def unit_column(which, group):
    per_tile = UNITS // 128
    tile, rest = divmod(group, per_tile)
    return tile * 2 * UNITS + which * UNITS + rest * 128


def pack_first(w_query, w_key, w_value, captions, modulation, after):
    k_rows, width = w_query.shape
    size = width // k_rows
    part = k_rows // N_DP
    tokens, features = captions.shape
    columns = 3 * k_rows
    clips, own_mod = modulation.shape
    pieces = own_mod // columns
    mod_rows = 2 * clips * pieces
    member = jnp.reshape(lax.axis_index("dp"), (1,)).astype(jnp.int32)
    rows = part + tokens + 16

    def kernel(member_ref, q_ref, k_ref, v_ref, cap_ref, mod_ref, after_ref, out_ref):
        spot = pl.ds(aligned(member_ref[0] * part, part), part)
        mod = jnp.concatenate(
            [mod_ref[:, i * columns : (i + 1) * columns] for i in range(pieces)], axis=0
        )
        high = mod.astype(BF16).astype(F32)
        fill = jnp.zeros((16 - mod_rows, columns), F32)
        mod = jnp.concatenate([high, mod - high, fill], axis=0).astype(BF16)
        each = features // size
        fill = jnp.zeros((tokens, columns - each), BF16)
        for device in range(size):
            own = slice(device * k_rows, (device + 1) * k_rows)
            row = [ref[spot, own].astype(F32) for ref in (q_ref, k_ref, v_ref)]
            out_ref[device, :part] = jnp.concatenate(row, axis=1).astype(BF16)
            cap = cap_ref[:, device * each : (device + 1) * each]
            out_ref[device, part : part + tokens] = jnp.concatenate([cap, fill], axis=1)
            out_ref[device, part + tokens :] = mod

    vmem = pl.BlockSpec(memory_space=pltpu.VMEM)
    return pl.pallas_call(
        kernel,
        in_specs=[pl.BlockSpec(memory_space=pltpu.SMEM)] + [vmem] * 5 + [pl.BlockSpec(memory_space=pl.ANY)],
        out_specs=vmem,
        out_shape=jax.ShapeDtypeStruct((size, rows, columns), BF16),
        compiler_params=pltpu.CompilerParams(vmem_limit_bytes=VMEM_BYTES),
        cost_estimate=pl.CostEstimate(
            flops=0, bytes_accessed=8 * size * rows * columns, transcendentals=0
        ),
    )(member, w_query, w_key, w_value, captions, modulation, after)


def unpack_first(packed, part, tokens, features, clips, own_mod):
    size, _, columns = packed.shape
    pieces = own_mod // columns
    each = tokens // clips

    def kernel(in_ref, quarter_ref, cap_ref, mod_ref):
        for device in range(size):
            quarter_ref[device] = in_ref[device, :part]
            for clip in range(clips):
                start = part + clip * each
                cap_ref[clip, device * each : (device + 1) * each] = in_ref[
                    device, start : start + each, :features
                ]
            mod = in_ref[device, part + tokens :].astype(F32)
            count = clips * pieces
            mod = mod[:count] + mod[count : 2 * count]
            mod = [mod[i * clips : (i + 1) * clips] for i in range(pieces)]
            mod_ref[:, device * own_mod : (device + 1) * own_mod] = jnp.concatenate(mod, axis=1)

    vmem = pl.BlockSpec(memory_space=pltpu.VMEM)
    return pl.pallas_call(
        kernel,
        in_specs=[vmem],
        out_specs=[vmem] * 3,
        out_shape=[
            jax.ShapeDtypeStruct((size, part, columns), BF16),
            jax.ShapeDtypeStruct((clips, size * each, features), BF16),
            jax.ShapeDtypeStruct((clips, size * own_mod), F32),
        ],
        compiler_params=pltpu.CompilerParams(vmem_limit_bytes=VMEM_BYTES),
        cost_estimate=pl.CostEstimate(
            flops=0, bytes_accessed=4 * packed.size, transcendentals=0
        ),
    )(packed)


def feed_kernel(ids_ref, *refs, size, places):
    count = len(places)
    x_refs, grad_ref = refs[:N_DP], refs[N_DP]
    piece_refs = refs[N_DP + 1 : N_DP + 1 + count]
    hidden_ref, grads_ref, near_ref, far_ref = refs[N_DP + 1 + count : N_DP + 5 + count]
    down_out, x_out = refs[N_DP + 5 + count : N_DP + 7 + count]
    x_all, grad_all, w_all, down_all, total, sems, out_sems = refs[N_DP + 7 + count :]
    rows = x_refs[0].shape[0]
    columns = w_all.shape[1]
    tile = pl.program_id(0)
    last = pl.num_programs(0) - 1

    def spot(i):
        return pl.ds(aligned(ids_ref[size + i] * rows, rows), rows)

    def copies(first, end=None):
        pairs = []
        for i in range(N_DP):
            pairs.append((x_refs[i], x_all.at[spot(i)]))
        for i, (place_, start, height) in enumerate(places):
            top = aligned(ids_ref[place_] * 192 + start, 32)
            pairs.append((piece_refs[i].at[:, pl.ds(0, columns)], w_all.at[pl.ds(top, height)]))
        pairs.append((grad_ref, grad_all))
        for i, (place_, start, height) in enumerate(places):
            for row, column, there_row, there_column, high, wide in folded(start, start + height):
                top = aligned(ids_ref[place_] * 128 + row, 32)
                pairs.append(
                    (
                        piece_refs[i].at[
                            pl.ds(there_row, high), pl.ds(columns + there_column, wide)
                        ],
                        down_all.at[pl.ds(top, high), pl.ds(column, wide)],
                    )
                )
        numbered = list(enumerate(pairs))[first:end]
        return [pltpu.make_async_copy(a, b, sems.at[i]) for i, (a, b) in numbered]

    def keep(i):
        source, there = ((x_all, x_out), (down_all, down_out))[i]
        return pltpu.make_async_copy(source, there, out_sems.at[i])

    early = N_DP + count

    @pl.when(tile == 0)
    def _():
        for copy in copies(0):
            copy.start()
        for copy in copies(0, early):
            copy.wait()
        keep(0).start()

    weight = w_all[:, pl.ds(aligned(tile * 2 * UNITS, 2 * UNITS), 2 * UNITS)]
    both = dot(x_all[...], weight)
    gate, up = both[:, :UNITS], both[:, UNITS:]

    @pl.when(tile == 0)
    def _():
        for copy in copies(early):
            copy.wait()
        keep(1).start()

    down = down_all[pl.ds(aligned(tile * UNITS, UNITS), UNITS), :]
    hidden_grad = dot(grad_all[...], down, NT)
    sigmoid = jax.nn.sigmoid(gate)
    silu = gate * sigmoid
    hidden_ref[...] = (silu * up).astype(BF16)
    gate_grad = hidden_grad * up * sigmoid * (1.0 + gate * (1.0 - sigmoid))
    grads = jnp.concatenate([gate_grad.astype(BF16), (hidden_grad * silu).astype(BF16)], axis=1)
    grads_ref[...] = grads
    term = dot(grads, weight, NT)

    @pl.when(tile == 0)
    def _():
        total[...] = term

    @pl.when(tile > 0)
    def _():
        total[...] += term

    @pl.when(tile == last)
    def _():
        for i, out_ref in enumerate((near_ref, far_ref)):
            out_ref[:rows] = total[spot(i), :].astype(BF16)
            out_ref[rows:] = total[spot(2 + i), :].astype(BF16)
        keep(0).wait()
        keep(1).wait()


def feed(ring, xs, grads, pieces):
    rows, width = xs[0].shape
    units = (pieces[0][2].shape[1] - FOLD) // 2
    places = tuple((ring.spots[shift], start, piece.shape[0]) for shift, start, piece in pieces)
    copies = N_DP + 1 + len(pieces)
    copies += sum(len(folded(start, start + height)) for _, start, height in places)
    anywhere = pl.BlockSpec(memory_space=pl.ANY)
    return pl.pallas_call(
        functools.partial(feed_kernel, size=ring.size, places=places),
        grid_spec=pltpu.PrefetchScalarGridSpec(
            num_scalar_prefetch=1,
            grid=(units // UNITS,),
            in_specs=[anywhere] * (N_DP + 1 + len(pieces)),
            out_specs=[
                pl.BlockSpec((N_DP * rows, UNITS), lambda t, ids: (0, t)),
                pl.BlockSpec((N_DP * rows, 2 * UNITS), lambda t, ids: (0, t)),
                pl.BlockSpec((2 * rows, width), lambda t, ids: (0, 0)),
                pl.BlockSpec((2 * rows, width), lambda t, ids: (0, 0)),
                anywhere,
                anywhere,
            ],
            scratch_shapes=[
                pltpu.VMEM((N_DP * rows, width), BF16),
                pltpu.VMEM((N_DP * rows, width), BF16),
                pltpu.VMEM((width, 2 * units), BF16),
                pltpu.VMEM((units, width), BF16),
                pltpu.VMEM((N_DP * rows, width), F32),
                pltpu.SemaphoreType.DMA((copies,)),
                pltpu.SemaphoreType.DMA((2,)),
            ],
        ),
        out_shape=[
            jax.ShapeDtypeStruct((N_DP * rows, units), BF16),
            jax.ShapeDtypeStruct((N_DP * rows, 2 * units), BF16),
            jax.ShapeDtypeStruct((2 * rows, width), BF16),
            jax.ShapeDtypeStruct((2 * rows, width), BF16),
            jax.ShapeDtypeStruct((units, width), BF16),
            jax.ShapeDtypeStruct((N_DP * rows, width), BF16),
        ],
        compiler_params=pltpu.CompilerParams(vmem_limit_bytes=VMEM_BYTES),
        cost_estimate=pl.CostEstimate(
            flops=10 * N_DP * rows * width * units,
            bytes_accessed=24 * N_DP * rows * width,
            transcendentals=N_DP * rows * units,
        ),
    )(ring.table, *xs, grads, *[piece for _, _, piece in pieces])


def add_home(terms, received):
    rows, width = received[0].shape
    last = terms.shape[0] // rows - 1

    def kernel(own_ref, above_ref, below_ref, out_ref):
        total = own_ref[...].astype(F32) + above_ref[...].astype(F32) + below_ref[...].astype(F32)
        out_ref[...] = total.astype(BF16)

    fixed = pl.BlockSpec((rows, width), lambda i: (0, 0))
    return pl.pallas_call(
        kernel,
        grid=(1,),
        in_specs=[pl.BlockSpec((rows, width), lambda i: (last, 0)), fixed, fixed],
        out_specs=fixed,
        out_shape=jax.ShapeDtypeStruct((rows, width), BF16),
        compiler_params=pltpu.CompilerParams(vmem_limit_bytes=VMEM_BYTES),
        cost_estimate=pl.CostEstimate(
            flops=0, bytes_accessed=8 * rows * width, transcendentals=0
        ),
    )(terms, *received)


def unit_terms(table, first, count, xs, hidden, unit_grads, grads, apart):
    rows, width = xs.shape
    columns = unit_grads.shape[1]
    k_rows = width // lax.axis_size("sp")
    half = k_rows // 2

    def kernel(ids_ref, x_ref, hidden_ref, units_ref, grads_ref, *refs):
        out_refs, turned, whole = refs[:-2], refs[-2], refs[-1]
        device = ids_ref[first - pl.program_id(0)]
        turned[...] = jnp.transpose(x_ref[...])
        spot = pl.ds(aligned(lax.rem(device, 2) * k_rows, k_rows), k_rows)
        down = dot(hidden_ref[...], grads_ref[...], TN).astype(BF16)
        target = whole if apart else out_refs[0]
        target[:, :columns] = dot(turned[spot, :], units_ref[...]).astype(BF16)
        for row, column, there_row, there_column, height, wide in folded(0, k_rows):
            target[
                there_row : there_row + height,
                columns + there_column : columns + there_column + wide,
            ] = down[row : row + height, column : column + wide]
        if apart:
            out_refs[0][...] = whole[:half]
            out_refs[1][...] = whole[half:]

    outs, height = (2, half) if apart else (1, k_rows)
    return pl.pallas_call(
        kernel,
        grid_spec=pltpu.PrefetchScalarGridSpec(
            num_scalar_prefetch=1,
            grid=(count,),
            in_specs=[
                pl.BlockSpec((rows, 2 * k_rows), lambda i, ids: (0, ids[first - i] // 2)),
                pl.BlockSpec((rows, 128), lambda i, ids: (0, ids[first - i])),
                pl.BlockSpec((rows, columns), lambda i, ids: (0, 0)),
                pl.BlockSpec((rows, width), lambda i, ids: (0, 0)),
            ],
            out_specs=[pl.BlockSpec((height, columns + FOLD), lambda i, ids: (i, 0))] * outs,
            scratch_shapes=[
                pltpu.VMEM((2 * k_rows, rows), BF16),
                pltpu.VMEM((k_rows, columns + FOLD), BF16),
            ],
        ),
        out_shape=[jax.ShapeDtypeStruct((count * height, columns + FOLD), BF16)] * outs,
        compiler_params=pltpu.CompilerParams(vmem_limit_bytes=VMEM_BYTES),
        cost_estimate=pl.CostEstimate(
            flops=2 * count * rows * (k_rows * columns + 128 * width),
            bytes_accessed=4 * rows * columns + 2 * count * k_rows * (columns + FOLD),
            transcendentals=0,
        ),
    )(table, xs, hidden, unit_grads, grads)


def token_terms(table, first, count, grads, weight, apart):
    clips, columns, length = grads.shape
    width = weight.shape[1]
    half = length // lax.axis_size("sp")

    def kernel(ids_ref, grads_ref, w_ref, *out_refs):
        for clip in range(clips):
            value = dot(jnp.transpose(grads_ref[clip]), w_ref[...]).astype(BF16)
            if apart:
                out_refs[clip][...] = value
            else:
                out_refs[0][clip * half : (clip + 1) * half] = value

    outs, rows = (clips, half) if apart else (1, clips * half)
    return pl.pallas_call(
        kernel,
        grid_spec=pltpu.PrefetchScalarGridSpec(
            num_scalar_prefetch=1,
            grid=(count,),
            in_specs=[
                pl.BlockSpec((clips, columns, half), lambda i, ids: (0, 0, ids[first - i])),
                pl.BlockSpec((columns, width), lambda i, ids: (0, 0)),
            ],
            out_specs=[pl.BlockSpec((rows, width), lambda i, ids: (i, 0))] * outs,
        ),
        out_shape=[jax.ShapeDtypeStruct((count * rows, width), BF16)] * outs,
        compiler_params=pltpu.CompilerParams(vmem_limit_bytes=VMEM_BYTES),
        cost_estimate=pl.CostEstimate(
            flops=2 * clips * count * half * columns * width,
            bytes_accessed=2 * clips * count * half * (columns + width) + 2 * width * columns,
            transcendentals=0,
        ),
    )(table, grads, weight)


def add_received(index, terms, received):
    width = terms.shape[1]
    rows = terms.shape[0] // (2 * (lax.axis_size("sp") // 2 - 1) + 1)
    half = rows // 2

    def kernel(*refs):
        for side in range(2):
            own, arrived, out = refs[side], refs[2 + side], refs[4 + side]
            value = own[...].astype(F32)
            if arrived.shape[0] == rows:
                out[...] = (value + arrived[...].astype(F32)).astype(BF16)
            else:
                span = slice(side * half, (side + 1) * half)
                rest = slice((1 - side) * half, (2 - side) * half)
                out[span] = (value[span] + arrived[...].astype(F32)).astype(BF16)
                out[rest] = own[rest]

    def spec(height, block=0):
        return pl.BlockSpec((height, width), lambda i: (block, 0))

    return pl.pallas_call(
        kernel,
        grid=(1,),
        in_specs=[spec(rows, index[0]), spec(rows, index[1])]
        + [spec(a.shape[0]) for a in received],
        out_specs=[spec(rows)] * 2,
        out_shape=[jax.ShapeDtypeStruct((rows, width), BF16)] * 2,
        compiler_params=pltpu.CompilerParams(vmem_limit_bytes=VMEM_BYTES),
        cost_estimate=pl.CostEstimate(
            flops=0, bytes_accessed=12 * rows * width, transcendentals=0
        ),
    )(terms, terms, *received)


def head_weight_terms(ring, block_in, grads):
    clips, length, width = block_in.shape
    columns = grads.shape[1]
    size = ring.size
    k_rows = width // size
    part = k_rows // N_DP
    tile = 2 * k_rows

    def kernel(index_ref, in_ref, grads_ref, *refs):
        out_refs, turned = refs[:N_DP], refs[N_DP]
        total = dot(grads_ref[0], in_ref[0])
        for clip in range(1, clips):
            total = total + dot(grads_ref[clip], in_ref[clip])
        turned[...] = jnp.transpose(total)
        for i, out_ref in enumerate(out_refs):
            for shard in range(2):
                start = shard * k_rows + index_ref[size + i] * part
                out_ref[shard] = turned[pl.ds(aligned(start, part), part), :].astype(BF16)

    return pl.pallas_call(
        kernel,
        grid=(width // tile,),
        in_specs=[
            pl.BlockSpec(memory_space=pltpu.SMEM),
            pl.BlockSpec((clips, length, tile), lambda t: (0, 0, t)),
            pl.BlockSpec((clips, columns, length), lambda t: (0, 0, 0)),
        ],
        out_specs=[pl.BlockSpec((2, part, columns), lambda t: (t, 0, 0))] * N_DP,
        out_shape=[jax.ShapeDtypeStruct((size, part, columns), BF16)] * N_DP,
        scratch_shapes=[pltpu.VMEM((tile, columns), F32)],
        compiler_params=pltpu.CompilerParams(vmem_limit_bytes=VMEM_BYTES),
        cost_estimate=pl.CostEstimate(
            flops=2 * clips * length * width * columns,
            bytes_accessed=2 * clips * length * (width + columns) + 2 * width * columns,
            transcendentals=0,
        ),
    )(ring.table, block_in, grads)


def turn(values, cos, sin):
    half = HD // 2
    a, b = values[:half], values[half:]
    return jnp.concatenate([a * cos - b * sin, a * sin + b * cos], axis=0)


def turn_back(grads, cos, sin):
    half = HD // 2
    a, b = grads[:half], grads[half:]
    return jnp.concatenate([a * cos + b * sin, b * cos - a * sin], axis=0)


def head_inverse(values):
    return lax.rsqrt(jnp.mean(values * values, axis=0, keepdims=True) + EPSILON)


def project_kernel(place_ref, *refs, sizes):
    count = sum(sizes)
    blocks = refs[:count]
    shift_ref, scale_ref, w_ref, cos_ref, sin_ref = refs[count : count + 5]
    in_ref, out_ref, raw_ref = refs[-3:]
    half = in_ref.shape[1]
    heads = w_ref.shape[1] // (3 * HD)

    def run(x, clip):
        x = x.astype(F32)
        inverse = lax.rsqrt(jnp.mean(x * x, axis=-1, keepdims=True) + EPSILON)
        block = x * inverse * (1.0 + scale_ref[clip : clip + 1, :]) + shift_ref[clip : clip + 1, :]
        block = block.astype(BF16)
        in_ref[clip] = block
        raw = jnp.transpose(dot(block, w_ref[...]))
        raw_ref[clip] = raw[: 2 * heads * HD]
        cos, sin = cos_ref[clip], sin_ref[clip]
        for head in range(2 * heads):
            rows = raw[head * HD : (head + 1) * HD]
            rotated = turn(rows * head_inverse(rows), cos, sin)
            out_ref[clip, head * HD : (head + 1) * HD, :] = rotated.astype(BF16)
        out_ref[clip, 2 * heads * HD :, :] = raw[2 * heads * HD :].astype(BF16)

    first = 0
    for step, size in enumerate(sizes):
        group = blocks[first : first + size]
        first += size

        @pl.when(pl.program_id(0) == step)
        def _(group=group):
            for clip in range(CLIPS):
                if len(group) == 1:
                    start = clip * (half + HELD)
                    run(group[0][start : start + half, :], clip)
                else:
                    run(group[clip][:half], clip)


def project(table, first, groups, shift, scale, weight, cos, sin, before):
    sizes = tuple(len(g) for g in groups)
    blocks = [b for g in groups for b in g]
    width, columns = weight.shape
    length = cos.shape[2]
    half = groups[0][0].shape[0] * len(groups[0]) // CLIPS - HELD
    fixed = lambda a: pl.BlockSpec(a.shape, lambda i, ids: (0,) * a.ndim)
    out_shape = [
        jax.ShapeDtypeStruct((CLIPS, length, width), BF16),
        jax.ShapeDtypeStruct((CLIPS, columns, length), BF16),
        jax.ShapeDtypeStruct((CLIPS, 2 * columns // 3, length), F32),
    ]
    in_specs = [fixed(a) for a in (*blocks, shift, scale, weight)]
    in_specs += [pl.BlockSpec((CLIPS, HD // 2, half), lambda i, ids: (0, 0, ids[first + i]))] * 2
    operands = [*blocks, shift, scale, weight, cos, sin]
    aliases = {}
    if before is not None:
        aliases = {1 + len(operands) + i: i for i in range(3)}
        in_specs += [pl.BlockSpec(memory_space=pl.ANY)] * 3
        operands += before
    rows = CLIPS * half * len(groups)
    return pl.pallas_call(
        functools.partial(project_kernel, sizes=sizes),
        grid_spec=pltpu.PrefetchScalarGridSpec(
            num_scalar_prefetch=1,
            grid=(len(groups),),
            in_specs=in_specs,
            out_specs=[
                pl.BlockSpec((CLIPS, half, width), lambda i, ids: (0, ids[first + i], 0)),
                pl.BlockSpec((CLIPS, columns, half), lambda i, ids: (0, 0, ids[first + i])),
                pl.BlockSpec((CLIPS, 2 * columns // 3, half), lambda i, ids: (0, 0, ids[first + i])),
            ],
        ),
        out_shape=out_shape,
        input_output_aliases=aliases,
        compiler_params=pltpu.CompilerParams(vmem_limit_bytes=VMEM_BYTES),
        cost_estimate=pl.CostEstimate(
            flops=2 * rows * width * columns,
            bytes_accessed=4 * rows * width + 8 * rows * columns + 2 * width * columns,
            transcendentals=0,
        ),
    )(table, *operands)


def cross_probabilities(cap_key, query):
    scores = dot(cap_key, query, TN) * HD**-0.5
    grown = jnp.exp(scores - jnp.max(scores, axis=0, keepdims=True))
    return grown / jnp.sum(grown, axis=0, keepdims=True)


def attend_kernel(
    gate_ref, q_ref, k_ref, v_ref, ck_ref, cv_ref, mixed_ref, self_ref, cross_ref, log_ref, *, block
):
    length = q_ref.shape[2]
    half = mixed_ref.shape[2]
    gate = gate_ref[pl.program_id(1)]
    keys = jnp.transpose(k_ref[0])
    for start in range(0, length, block):
        query = q_ref[0, :, start : start + block]
        grown = jnp.exp(dot(keys, query) * HD**-0.5)
        total = jnp.sum(grown, axis=0, keepdims=True)
        self_out = dot(v_ref[0], grown.astype(BF16)) / total
        probs = cross_probabilities(ck_ref[...], query)
        cross_out = dot(cv_ref[...], probs.astype(BF16))
        self_ref[0, :, start : start + block] = self_out
        cross_ref[0, :, start : start + block] = cross_out
        log_ref[0, 0, :, start : start + block] = jnp.log(total)
        mixed = (self_out + gate * cross_out).astype(BF16)
        for piece in range(block // half):
            mixed_ref[start // half + piece] = mixed[:, piece * half : (piece + 1) * half]


def attend(gate, qkv, cap_key, cap_value, half):
    clips, columns, length = qkv.shape
    heads = columns // (3 * HD)
    head_spec = lambda first: pl.BlockSpec((1, HD, length), lambda c, h: (c, first * heads + h, 0))
    cap_spec = pl.BlockSpec((HD, CAP), lambda c, h: (h, c))
    own_spec = pl.BlockSpec((1, HD, length), lambda c, h: (c, h, 0))
    return pl.pallas_call(
        functools.partial(attend_kernel, block=length),
        grid=(clips, heads),
        in_specs=[
            pl.BlockSpec(memory_space=pltpu.SMEM),
            head_spec(0),
            head_spec(1),
            head_spec(2),
            cap_spec,
            cap_spec,
        ],
        out_specs=[
            pl.BlockSpec((length // half, HD, half), lambda c, h: (0, h, c)),
            own_spec,
            own_spec,
            pl.BlockSpec((1, 1, 1, length), lambda c, h: (c, h, 0, 0)),
        ],
        out_shape=[
            jax.ShapeDtypeStruct((length // half, heads * HD, clips * half), BF16),
            jax.ShapeDtypeStruct((clips, heads * HD, length), F32),
            jax.ShapeDtypeStruct((clips, heads * HD, length), F32),
            jax.ShapeDtypeStruct((clips, heads, 1, length), F32),
        ],
        compiler_params=pltpu.CompilerParams(vmem_limit_bytes=VMEM_BYTES),
        cost_estimate=pl.CostEstimate(
            flops=4 * clips * heads * length * length * HD * 4,
            bytes_accessed=clips * heads * length * HD * 20,
            transcendentals=clips * heads * length * length,
        ),
    )(gate, qkv, qkv, qkv, cap_key, cap_value)


def attend_back_kernel(
    gate_ref,
    q_ref,
    k_ref,
    v_ref,
    ck_ref,
    cv_ref,
    grad_ref,
    self_ref,
    cross_ref,
    log_ref,
    raw_q_ref,
    raw_k_ref,
    cos_ref,
    sin_ref,
    grads_ref,
    cap_ref,
    gate_grad_ref,
    key_acc,
    value_acc,
    *,
    block,
):
    length = q_ref.shape[2]
    half = grad_ref.shape[2]
    score_scale = HD**-0.5
    gate = gate_ref[pl.program_id(1)]
    keys, values = k_ref[0], v_ref[0]
    keys_turned, values_turned = jnp.transpose(keys), jnp.transpose(values)
    cap_key, cap_value = ck_ref[...], cv_ref[...]
    cap_key_grad = jnp.zeros((HD, CAP), F32)
    cap_value_grad = jnp.zeros((HD, CAP), F32)
    for start in range(0, length, block):
        span = slice(start, start + block)
        query = q_ref[0, :, span]
        grad = jnp.concatenate(
            [grad_ref[start // half + piece] for piece in range(block // half)], axis=1
        )
        wide = grad.astype(F32)
        delta = jnp.sum(wide * self_ref[0, :, span], axis=0, keepdims=True)
        gate_grad_ref[0, 0, :, span] = jnp.sum(
            wide * cross_ref[0, :, span], axis=0, keepdims=True
        )
        probs = jnp.exp(dot(keys_turned, query) * score_scale - log_ref[0, 0, :, span])
        score_grad = (probs * (dot(values_turned, grad) - delta)).astype(BF16)
        value_part = jnp.transpose(dot(probs.astype(BF16), jnp.transpose(grad)))
        key_part = jnp.transpose(dot(score_grad, jnp.transpose(query)))
        if start == 0:
            value_acc[...] = value_part
            key_acc[...] = key_part
        else:
            value_acc[...] += value_part
            key_acc[...] += key_part
        query_grad = dot(keys, score_grad)
        cross_grad = (gate * wide).astype(BF16)
        cross_probs = cross_probabilities(cap_key, query)
        cross_dp = dot(cap_value, cross_grad, TN)
        cross_score = cross_probs * (
            cross_dp - jnp.sum(cross_probs * cross_dp, axis=0, keepdims=True)
        )
        cross_score = cross_score.astype(BF16)
        cap_value_grad += dot(cross_grad, cross_probs.astype(BF16), NT)
        cap_key_grad += dot(query, cross_score, NT)
        query_grad = (query_grad + dot(cap_key, cross_score)) * score_scale
        raw = raw_q_ref[0, :, span]
        inverse = head_inverse(raw)
        normed = raw * inverse
        turned = turn_back(query_grad, cos_ref[0, :, span], sin_ref[0, :, span])
        mean = jnp.mean(turned * normed, axis=0, keepdims=True)
        grads_ref[0, 0, :, span] = (inverse * (turned - normed * mean)).astype(BF16)
    for start in range(0, length, block):
        span = slice(start, start + block)
        raw = raw_k_ref[0, :, span]
        inverse = head_inverse(raw)
        normed = raw * inverse
        turned = turn_back(
            key_acc[:, span] * score_scale, cos_ref[0, :, span], sin_ref[0, :, span]
        )
        mean = jnp.mean(turned * normed, axis=0, keepdims=True)
        grads_ref[0, 1, :, span] = (inverse * (turned - normed * mean)).astype(BF16)
        grads_ref[0, 2, :, span] = value_acc[:, span].astype(BF16)
    cap_ref[0] = (cap_key_grad * score_scale).astype(BF16)
    cap_ref[1] = cap_value_grad.astype(BF16)


def attend_back(gate, qkv, cap_key, cap_value, grad, self_out, cross_out, log_total, raw, cos, sin):
    clips, columns, length = qkv.shape
    heads = columns // (3 * HD)
    half = length // grad.shape[0]
    head_spec = lambda first: pl.BlockSpec((1, HD, length), lambda c, h: (c, first * heads + h, 0))
    cap_spec = pl.BlockSpec((HD, CAP), lambda c, h: (h, c))
    table_spec = pl.BlockSpec((1, HD // 2, length), lambda c, h: (c, 0, 0))
    row_spec = pl.BlockSpec((1, 1, 1, length), lambda c, h: (c, h, 0, 0))
    return pl.pallas_call(
        functools.partial(attend_back_kernel, block=length // 2),
        grid=(clips, heads),
        in_specs=[
            pl.BlockSpec(memory_space=pltpu.SMEM),
            head_spec(0),
            head_spec(1),
            head_spec(2),
            cap_spec,
            cap_spec,
            pl.BlockSpec((length // half, HD, half), lambda c, h: (0, h, c)),
            head_spec(0),
            head_spec(0),
            row_spec,
            head_spec(0),
            head_spec(1),
            table_spec,
            table_spec,
        ],
        out_specs=[
            pl.BlockSpec((1, 3, HD, length), lambda c, h: (c, 0, h, 0)),
            pl.BlockSpec((2, HD, CAP), lambda c, h: (0, h, c)),
            row_spec,
        ],
        out_shape=[
            jax.ShapeDtypeStruct((clips, 3, heads * HD, length), BF16),
            jax.ShapeDtypeStruct((2, heads * HD, clips * CAP), BF16),
            jax.ShapeDtypeStruct((clips, heads, 1, length), F32),
        ],
        scratch_shapes=[pltpu.VMEM((HD, length), F32), pltpu.VMEM((HD, length), F32)],
        compiler_params=pltpu.CompilerParams(vmem_limit_bytes=VMEM_BYTES),
        cost_estimate=pl.CostEstimate(
            flops=10 * clips * heads * length * length * HD * 4,
            bytes_accessed=clips * heads * length * HD * 32,
            transcendentals=clips * heads * length * length,
        ),
    )(
        gate,
        qkv,
        qkv,
        qkv,
        cap_key,
        cap_value,
        grad,
        self_out,
        cross_out,
        log_total,
        raw,
        raw,
        cos,
        sin,
    )


def clip_sums(values):
    return jnp.sum(values.reshape(CLIPS, -1, values.shape[-1]), axis=1)


def split_heads(
    tokens,
    cotangent,
    captions,
    conditioning,
    clip_lens,
    w_ada,
    b_ada,
    w_query,
    w_key,
    w_value,
    w_out,
    gate_cross,
    w_text_key,
    w_text_value,
    w_gate,
    w_up,
    w_down,
):
    shard = lax.axis_index("sp")
    member = lax.axis_index("dp")
    size = lax.axis_size("sp")
    ring = Ring(size)
    rows = tokens.shape[1]
    half = rows // 2
    own_cols = D // size
    heads = HEADS // size
    ff = w_gate.shape[1]
    ff_rows = ff // size
    ff_part = ff_rows // N_DP
    k_rows = D // size
    k_part = k_rows // N_DP
    text_rows = w_text_key.shape[0]

    inputs = tokens[0].astype(F32)
    out_grad = cotangent[0].astype(F32)
    hidden_units = ff // N_DP

    def by_row(values):
        return jnp.repeat(values, half, axis=0)

    far = size // 2
    out_cols_part = D // N_DP
    table = ring.table
    tanh_gate = jnp.tanh(gate_cross)
    own_gate = lax.dynamic_slice(tanh_gate, (shard * heads,), (heads,))

    token_rows = pack_tokens(tokens[0], w_out)
    token_flow = Gather(ring, [token_rows])
    token_flow.send()
    cond_row = conditioning[0]
    cond_act = jax.nn.silu(cond_row).astype(BF16)
    mod_part = dot(cond_act, w_ada) + b_ada[None, :]
    flat_caption = captions[0].reshape(-1, size * text_rows)
    packed = exchange(pack_first(w_query, w_key, w_value, flat_caption, mod_part, token_rows))
    token_flow.live, packed = ordered((token_flow.live, packed))
    token_flow.keep()

    token_flow.send()
    quarter, caption_cols, modulation = unpack_first(
        packed, k_part, flat_caption.shape[0], text_rows, CLIPS, mod_part.shape[1]
    )
    caption_cols = caption_cols.reshape(-1, text_rows)
    quarter_far = across(quarter, 2)
    cap_terms = caption_terms(w_text_key, w_text_value, caption_cols)
    caption_all = lax.all_gather(caption_cols, "dp", axis=0, tiled=True)
    token_flow.live, quarter, quarter_far, modulation, cap_terms = ordered(
        (token_flow.live, quarter, quarter_far, modulation, cap_terms)
    )
    token_flow.keep()

    token_flow.send()
    quarters = [quarter, quarter_far, across(quarter, 1), across(quarter_far, 1)]
    w_qkv, w_turned = join_projections(ring, quarters)
    cap_terms = lax.psum_scatter(cap_terms, "sp", scatter_dimension=0, tiled=True)
    shift_one, scale_one, gate_one, shift_two, scale_two, gate_two = jnp.split(modulation, 6, axis=1)
    branch_grad = (by_row(gate_two) * out_grad).astype(BF16)
    branch_grads = lax.all_gather(branch_grad, "dp", axis=0, tiled=True)
    lane = jnp.arange(size * half, dtype=jnp.int32)
    mirrored = (size - 1 - lane // half) * half + lane % half
    freq = 10000.0 ** (-(jnp.arange(HD // 2, dtype=F32) * 2.0 / HD))
    angle = jnp.stack([lane, mirrored]).astype(F32)[:, None, :] * freq[None, :, None]
    cos, sin = jnp.cos(angle), jnp.sin(angle)
    unit_piece = unit_pieces(w_gate, w_up, w_down, quarter)
    token_flow.live, w_qkv, unit_piece, caption_all = ordered(
        (token_flow.live, w_qkv, unit_piece, caption_all)
    )
    token_flow.keep()

    def project_some(first, groups, before):
        return project(table, first, groups, shift_one, scale_one, w_qkv, cos, sin, before)

    token_flow.send()
    weight_flow = Gather(ring, [unit_piece])
    weight_flow.send()
    blocks = [b for _, b in token_flow.blocks]
    projected = project_some(0, blocks[:5], None)
    token_flow.live, weight_flow.live, projected, cap_terms = ordered(
        (token_flow.live, weight_flow.live, projected, cap_terms)
    )
    token_flow.keep()
    weight_flow.keep()

    weight_flow.send()
    out_cols = unpack_w_out(ring, token_flow, half)
    out_full = lax.all_gather(out_cols, "dp", axis=1, tiled=True)
    halves = token_flow.halves
    block_in, qkv, raw = project_some(
        5, [*blocks[5:], [halves[0][0], halves[1][0]]], projected
    )
    cap_heads = jnp.sum(cap_terms.astype(F32), axis=0).astype(BF16)
    cap_key, cap_value = cap_heads[:, : CLIPS * CAP], cap_heads[:, CLIPS * CAP :]
    mixed_blocks, self_out, cross_out, log_total = attend(own_gate, qkv, cap_key, cap_value, half)
    weight_flow.live, mixed_blocks, branch_grads = ordered(
        (weight_flow.live, mixed_blocks, branch_grads)
    )
    weight_flow.keep()

    mixed = exchange(mixed_blocks)
    inverse_one = inverse_rms(inputs)
    normed_one = inputs * inverse_one
    mixed, out_full = ordered((mixed, out_full))

    weight_flow.send()
    mixed = mixed.reshape(D, rows)
    attn_out = dot(mixed, out_full, TN)
    middle = inputs + by_row(gate_one) * attn_out
    inverse_two = inverse_rms(middle)
    normed_two = middle * inverse_two
    ffn_in = (normed_two * (1.0 + by_row(scale_two)) + by_row(shift_two)).astype(BF16)
    ffn_far = across(ffn_in, 2)
    weight_flow.live, ffn_in = ordered((weight_flow.live, ffn_in))
    weight_flow.keep()

    weight_flow.send()
    weight_flow.keep()
    pieces = [(shift, 0, arrays[0]) for shift, arrays in weight_flow.blocks]
    pieces += [(far, 0, weight_flow.halves[0][0])]
    pieces += [(far, k_rows // 2, weight_flow.halves[1][0])]
    hidden, unit_grads, ffn_own, ffn_next, down, ffn_ins = feed(
        ring, [ffn_in, ffn_far, across(ffn_in, 1), across(ffn_far, 1)], branch_grads, pieces
    )
    near = across(jnp.concatenate([ffn_own[rows:], ffn_next[rows:]]), 1)
    ffn_far = (ffn_next[:rows].astype(F32) + near[rows:].astype(F32)).astype(BF16)
    ffn_own = ffn_own[:rows].astype(F32) + near[:rows].astype(F32)
    ffn_own, ffn_far, hidden, unit_grads = ordered((ffn_own, ffn_far, hidden, unit_grads))

    ffn_far = across(ffn_far, 2)
    last = ring.spots[far - 1]
    unit_args = (ffn_ins, hidden, unit_grads, branch_grads)
    unit_back = unit_terms(table, ring.spots[far], 1, *unit_args, True)

    def send(values):
        return ring.send_up(values[:1]) + ring.send_down(values[1:])

    unit_back = send(unit_back)
    (d_units,) = unit_terms(table, last, last + 1, *unit_args, False)

    def add_step(step, terms, received):
        return add_received((2 * step, 2 * step + 1), terms, received)

    ffn_far, d_units, unit_back, hidden = ordered(
        (ffn_far, d_units, add_step(0, d_units, unit_back), hidden)
    )

    unit_back = send(unit_back)
    ffn_in_grad = ffn_own + ffn_far.astype(F32)
    middle_grad = out_grad + norm_back(
        ffn_in_grad * (1.0 + by_row(scale_two)), normed_two, inverse_two
    )
    attn_grad = (by_row(gate_one) * middle_grad).astype(BF16)
    mixed_grad = dot(out_full, attn_grad, NT).astype(BF16).reshape(size, own_cols, rows)
    mixed_grad, mixed, attn_grad, hidden = ordered((mixed_grad, mixed, attn_grad, hidden))

    head_grad = exchange(mixed_grad)
    branch_terms = dot(hidden, down).astype(BF16)
    grad_out = out_terms(mixed, attn_grad)
    sums = [
        clip_sums(middle_grad * attn_out),
        clip_sums(ffn_in_grad),
        clip_sums(ffn_in_grad * normed_two),
    ]
    head_grad, grad_out, branch_terms, sums = ordered((head_grad, grad_out, branch_terms, sums))

    out_sum = lax.psum_scatter(grad_out, "dp", scatter_dimension=0, tiled=True)
    out_home = lax.psum_scatter(out_sum[0], "sp", scatter_dimension=0, tiled=True)
    grads, cap_grads, gate_rows = attend_back(
        own_gate, qkv, cap_key, cap_value, head_grad, self_out, cross_out, log_total, raw, cos, sin
    )
    grads = grads.reshape(CLIPS, 3 * own_cols, size * half)
    token_back = token_terms(table, ring.spots[far], 1, grads, w_turned, True)
    unit_back, grads, cap_grads, token_back, branch_terms = ordered(
        (unit_back, grads, cap_grads, token_back, branch_terms)
    )

    token_back = send(token_back)
    branch = lax.psum_scatter(branch_terms, "dp", scatter_dimension=0, tiled=True)
    unit_back = send(add_step(1, d_units, unit_back))
    (terms,) = token_terms(table, last, last + 1, grads, w_turned, False)
    qkv_terms = head_weight_terms(ring, block_in, grads)
    cap_all = jnp.transpose(cap_grads, (1, 0, 2)).reshape(own_cols, 2 * CLIPS * CAP)
    cap_all = gather_small(cap_all, "sp").reshape(D, 2 * CLIPS * CAP)
    token_back, unit_back, qkv_terms, cap_all = ordered(
        (add_step(0, terms, token_back), add_step(2, d_units, unit_back), qkv_terms, cap_all)
    )

    token_back = send(token_back)
    unit_back = send(unit_back)
    qkv_own, qkv_far = sum_packs_near(qkv_terms)
    qkv_far = across(qkv_far, 2)
    cap_far = across(cap_all, 2)
    caption_grad = dot(cap_all[:, : CLIPS * CAP], w_text_key, (((0,), (1,)), ((), ()))) + dot(
        cap_all[:, CLIPS * CAP :], w_text_value, (((0,), (1,)), ((), ()))
    )
    caption_grad = caption_grad.astype(BF16).reshape(CLIPS, size, -1, text_rows)
    caption_grad = jnp.transpose(caption_grad, (1, 0, 2, 3))
    caption_grad = exchange(caption_grad)
    token_back, unit_back, qkv_own, qkv_far, cap_all, cap_far, caption_grad = ordered(
        (
            add_step(1, terms, token_back),
            unit_back,
            qkv_own,
            qkv_far,
            cap_all,
            cap_far,
            caption_grad,
        )
    )

    token_back = send(token_back)
    unit_home = add_home(d_units, unit_back)
    unit_far = across(unit_home, 2)
    qkv_home = exchange((qkv_own + qkv_far.astype(F32)).astype(BF16))
    cap_blocks = [cap_all, cap_far, across(cap_all, 1), across(cap_far, 1)]
    token_back, unit_home, unit_far, cap_blocks, branch, out_home = ordered(
        (add_step(2, terms, token_back), unit_home, unit_far, cap_blocks, branch, out_home)
    )
    cap_all = cap_blocks[0]

    token_back = send(token_back)
    qkv_far = across(qkv_home, 2)
    d_text_key, d_text_value = text_grads(ring, caption_all, cap_blocks)
    shape = lambda *dims: jax.ShapeDtypeStruct(dims, F32)
    unit_blocks = [unit_home, unit_far, across(unit_home, 1), across(unit_far, 1)]
    d_gate_w, d_up_w, d_down = place(
        ring, place_units, unit_blocks, [shape(k_rows, ff), shape(k_rows, ff), shape(ff_rows, D)]
    )
    result = (middle + by_row(gate_two) * branch.astype(F32)).astype(BF16)
    sums = [*sums, clip_sums(out_grad * branch.astype(F32))]
    token_back, sums, qkv_home, qkv_far, out_home, result, d_down = ordered(
        (token_back, sums, qkv_home, qkv_far, out_home, result, d_down)
    )

    inputs_grad, own_sums = finish_tokens(terms, token_back, middle_grad, tokens[0], scale_one)

    mod_terms = jnp.concatenate([own_sums, *sums], axis=1)
    mod_terms = jnp.transpose(mod_terms.reshape(CLIPS, size, -1), (1, 0, 2))
    gate_own = jnp.sum(gate_rows, axis=(2, 3))
    gate_own = jnp.broadcast_to(gate_own[None], (size, CLIPS, heads))
    mod_terms = jnp.concatenate([mod_terms, gate_own], axis=2)
    mod_terms, qkv_home, qkv_far, out_home = ordered((mod_terms, qkv_home, qkv_far, out_home))

    arrived = exchange(mod_terms)
    qkv_blocks = [qkv_home, qkv_far, across(qkv_home, 1), across(qkv_far, 1)]
    out_blocks = gather_packs(out_home)

    own_mod = w_ada.shape[1]
    mod_low = jnp.sum(arrived[:, :, :own_mod], axis=0).astype(BF16)
    gate_all = jnp.transpose(arrived[:, :, own_mod:], (1, 0, 2)).reshape(CLIPS, HEADS)
    cond_part = dot(mod_low, w_ada, NT)
    cond_sum = jnp.sum(gather_small(cond_part, "sp"), axis=0)
    sigmoid_cond = jax.nn.sigmoid(cond_row)
    cond_grad = cond_sum * sigmoid_cond * (1.0 + cond_row * (1.0 - sigmoid_cond))
    both = jnp.concatenate([cond_act.astype(F32), mod_low.astype(F32), gate_all], axis=1)
    both_all = jnp.concatenate(gather_packs(both))
    cond_size = cond_act.shape[1]
    cond_all = both_all[:, :cond_size].astype(BF16)
    mod_all = both_all[:, cond_size : cond_size + own_mod].astype(BF16)
    d_ada = dot(cond_all, mod_all, TN)
    d_bias = jnp.sum(mod_all.astype(F32), axis=0)
    d_gate_cross = jnp.sum(both_all[:, cond_size + own_mod :], axis=0) * (
        1.0 - tanh_gate * tanh_gate
    )

    caption_grad = (
        jnp.transpose(caption_grad, (1, 2, 0, 3)).reshape(CLIPS, -1, size * text_rows).astype(F32)
    )

    (d_out,) = place(ring, place_columns, out_blocks, [shape(k_rows, D)])
    d_query, d_key, d_value = place(ring, place_heads, qkv_blocks, [shape(k_rows, D)] * 3)
    return (
        result[None],
        inputs_grad[None],
        caption_grad[None],
        cond_grad[None],
        d_ada,
        d_bias,
        d_query,
        d_key,
        d_value,
        d_out,
        d_gate_cross,
        d_text_key,
        d_text_value,
        d_gate_w,
        d_up_w,
        d_down,
    )


def layer(*arrays):
    tokens, clip_lens = arrays[0], arrays[4]
    size = lax.axis_size("sp")
    pack = tokens.shape[1] * size
    even = HEADS % size == 0 and size % 2 == 0 and size >= 4
    fixed = pack == clip_lens.shape[1] * MIN_CLIP and tokens.shape[1] % 256 == 0
    if even and fixed and lax.axis_size("dp") == N_DP:
        return split_heads(*arrays)
    return local(*arrays)


def solution(mesh):
    return jax.shard_map(
        layer,
        mesh=mesh,
        in_specs=(
            P("dp", "sp", None),
            P("dp", "sp", None),
            P("dp", None, "sp", None),
            P("dp", None, None),
            P("dp", None),
            P(None, "sp"),
            P("sp"),
            P("sp", None),
            P("sp", None),
            P("sp", None),
            P("sp", None),
            P(),
            P("sp", None),
            P("sp", None),
            P("sp", None),
            P("sp", None),
            P("sp", None),
        ),
        out_specs=(
            P("dp", "sp", None),
            P("dp", "sp", None),
            P("dp", None, "sp", None),
            P("dp", None, None),
            P(None, "sp"),
            P("sp"),
            P("sp", None),
            P("sp", None),
            P("sp", None),
            P("sp", None),
            P(),
            P("sp", None),
            P("sp", None),
            P("sp", None),
            P("sp", None),
            P("sp", None),
        ),
        check_vma=False,
    )
```
